128 devices in a mesh: chan: 32 (over y, x, core), tm: 4 (over z).
Axes of the slice: x: 4, y: 4, z: 4, core: 2. Of those that a mesh axis runs over, the one named last changes fastest.
Arguments:
- record: bfloat16 [4096, 16384], P('chan', 'tm')
- seg_starts: int32 [64], P('tm'), may hold values from 0 to 15872, as said below
- pair_blocks: int32 [93, 2], replicated, may hold values from 0 to 31, as said below
- pair_owner: int32 [93], replicated, may hold values from 0 to 127, as said below
Outputs:
- correlations: bfloat16 [128, 128, 64, 128], P('tm', 'chan')
The draws below stay inside these ranges and needn't reach their ends.
Inputs may be any that keep to these rules, and one draw needn't show every extreme that they name: `seg_starts`: each segment starts inside the time block of its own segment group: segment s starts between (s // 16) * 16 * 256 and that plus 16 * 256 - 1; every segment ends by 16384. `pair_blocks`: each row is a pair (first, second) with second - first equal to 0, 1 or 2; every such pair of the 32 blocks appears exactly once. `pair_owner`: slots are distinct. The owner (slot // 4) of a pair block (first, second) is first, or, where second - first = 2, first or first + 1. An owner holds at most 4 pair blocks, and some owner holds 4.
All inputs are finite; a program needn't handle non-finite values.
Results may differ from the reference program's by a relative error of at most 0.015.
Values may be sent and summed in bfloat16 or wider, within the bound.
A program may use at most 128 MiB of HBM per device.

```python
import math
import jax
import jax.numpy as jnp
from jax import lax

BLK = 128
SEG_LEN = 512
HOP = 256
F = 256
LOW_BIN = 1
NLAG = 64
SLOTS = 4
SEG_DEV = 16
SEGS = 64
TIME = 16384
NCH = 4096
N_CHAN = 32
N_TM = 4


def pair_table(key):
    key = jax.random.fold_in(key, 5)
    key_shift, key_rank, key_order = jax.random.split(key, 3)
    owners = jnp.arange(N_CHAN, dtype=jnp.int32)
    shifted = jax.random.randint(key_shift, (N_CHAN,), 0, 2).astype(jnp.int32)
    shifted = jnp.where(owners == 0, 1, jnp.where(owners == 1, 0, shifted))
    scores = jax.random.randint(key_rank, (N_CHAN, SLOTS), 0, 1 << 20) * SLOTS + jnp.arange(SLOTS, dtype=jnp.int32)[None, :]
    kind_col = jnp.arange(SLOTS, dtype=jnp.int32)[None, :]
    owner_row = owners[:, None]
    scores = jnp.where((owner_row == 0) & (kind_col == 0), -1, scores)
    scores = jnp.where((owner_row == N_CHAN - 1) & (kind_col == 0), (1 << 22) * SLOTS, scores)
    ranks = jnp.argsort(jnp.argsort(scores, axis=1), axis=1).astype(jnp.int32)
    lower = owners[:-2]
    first = jnp.concatenate([owners, owners[:-1], lower])
    second = jnp.concatenate([owners, owners[:-1] + 1, lower + 2])
    holder = jnp.concatenate([owners, owners[:-1], lower + shifted[:-2]])
    kinds = jnp.concatenate([jnp.zeros((N_CHAN,), jnp.int32), jnp.ones((N_CHAN - 1,), jnp.int32), jnp.where(shifted[:-2] == 1, 2, 3).astype(jnp.int32)])
    slot = holder * SLOTS + ranks[holder, kinds]
    order = jax.random.permutation(key_order, 3 * N_CHAN - 3)
    return (first[order], second[order], slot[order])


def draw_pair_blocks(key, part):
    first, second, slot = pair_table(key)
    return jnp.stack([first, second], axis=1).astype(jnp.int32)


def draw_pair_owner(key, part):
    first, second, slot = pair_table(key)
    return slot.astype(jnp.int32)


def draw_seg_starts(key, part):
    key = jax.random.fold_in(key, 23)
    jitter = jax.random.randint(key, (SEGS,), 0, HOP).astype(jnp.int32)
    starts = jnp.arange(SEGS, dtype=jnp.int32) * HOP + jitter
    starts = jnp.where(jnp.arange(SEGS, dtype=jnp.int32) == 0, 0, starts)
    return jnp.minimum(starts, TIME - SEG_LEN).astype(jnp.int32)


def draw_record(key, part):
    key = jax.random.fold_in(key, 11)
    key_base, key_chan, key_time = jax.random.split(key, 3)
    chan_scale = jnp.exp(jax.random.uniform(key_chan, (NCH, 1), minval=0.0, maxval=math.log(10.0)))
    time_scale = jnp.exp(jax.random.uniform(key_time, (1, TIME // HOP), minval=0.0, maxval=math.log(10.0)))
    time_scale = jnp.repeat(time_scale, HOP, axis=1)
    base = jax.random.normal(key_base, (NCH, TIME))
    return (base * chan_scale * time_scale).astype(jnp.bfloat16)


def setup_inputs(seed: int = 0) -> dict:
    key_list = jax.random.split(jax.random.key(seed), 5)
    return {
        "record": draw_record(jax.random.fold_in(key_list[4], 71), 0),
        "seg_starts": draw_seg_starts(jax.random.fold_in(key_list[4], 71), 0),
        "pair_blocks": draw_pair_blocks(jax.random.fold_in(key_list[4], 71), 0),
        "pair_owner": draw_pair_owner(jax.random.fold_in(key_list[4], 71), 0),
    }


LEVEL = 0.5
EPS = 1e-06

def transform_table():
    sample = jnp.arange(SEG_LEN, dtype=jnp.int32)
    bins = jnp.arange(F, dtype=jnp.int32) + LOW_BIN
    phase = (bins[:, None] * sample[None, :] % SEG_LEN).astype(jnp.float32) * (2.0 * math.pi / SEG_LEN)
    taper = 0.5 - 0.5 * jnp.cos(sample.astype(jnp.float32) * (2.0 * math.pi / SEG_LEN))
    table = jnp.concatenate([taper[None, :] * jnp.cos(phase), -taper[None, :] * jnp.sin(phase)], axis=0)
    return table.astype(jnp.bfloat16)

def lag_table():
    shifts = jnp.arange(NLAG, dtype=jnp.int32) - NLAG // 2
    bins = jnp.arange(F, dtype=jnp.int32) + LOW_BIN
    phase = (bins[:, None] * shifts[None, :] % SEG_LEN).astype(jnp.float32) * (2.0 * math.pi / SEG_LEN)
    return (jnp.cos(phase).astype(jnp.bfloat16), (-jnp.sin(phase)).astype(jnp.bfloat16))

def whiten(samples, starts, table):
    pieces = jax.vmap(lambda begin: lax.dynamic_slice_in_dim(samples, begin, SEG_LEN, 1))(starts)
    spectra = jnp.einsum('kn,sin->ksi', table.astype(jnp.float32), pieces.astype(jnp.float32), precision=lax.Precision.HIGHEST)
    spectra = spectra.reshape(2, F, spectra.shape[1], spectra.shape[2])
    amplitude = jnp.sqrt(spectra[0] * spectra[0] + spectra[1] * spectra[1])
    level = lax.optimization_barrier(jnp.mean(amplitude, axis=0)) + EPS
    return (spectra / (amplitude + LEVEL * level)[None]).astype(jnp.bfloat16)

def reference(record, seg_starts, pair_blocks, pair_owner):
    table = transform_table()
    cos_b, sin_b = lag_table()
    cos_tab = cos_b.astype(jnp.float32)
    sin_tab = sin_b.astype(jnp.float32)
    scale = 2.0 / math.sqrt(SEGS * F)
    blocks = record.reshape(N_CHAN, BLK, TIME)
    whitened = lax.map(lambda samples: whiten(samples, seg_starts, table), blocks)
    rows = jnp.arange(BLK, dtype=jnp.int32)
    self_pair = (rows[:, None] == rows[None, :]).astype(jnp.float32)
    high = lax.Precision.HIGHEST

    def one_slot(slot):
        match = (pair_owner == slot).astype(jnp.int32)
        live = jnp.sum(match).astype(jnp.float32)
        first = jnp.sum(match * pair_blocks[:, 0]).astype(jnp.int32)
        second = jnp.sum(match * pair_blocks[:, 1]).astype(jnp.int32)
        left = lax.dynamic_index_in_dim(whitened, first, 0, keepdims=False).astype(jnp.float32)
        right = lax.dynamic_index_in_dim(whitened, second, 0, keepdims=False).astype(jnp.float32)
        left = left.reshape(2, F, N_TM, SEG_DEV, BLK)
        right = right.reshape(2, F, N_TM, SEG_DEV, BLK)
        real = jnp.einsum('fgsi,fgsj->gfij', left[0], right[0], precision=high) + jnp.einsum('fgsi,fgsj->gfij', left[1], right[1], precision=high)
        imag = jnp.einsum('fgsi,fgsj->gfij', left[1], right[0], precision=high) - jnp.einsum('fgsi,fgsj->gfij', left[0], right[1], precision=high)
        real = real.astype(jnp.bfloat16).astype(jnp.float32)
        imag = imag.astype(jnp.bfloat16).astype(jnp.float32)
        lags = jnp.einsum('gfij,ft->itj', real, cos_tab, precision=high) + jnp.einsum('gfij,ft->itj', imag, sin_tab, precision=high)
        same = (first == second).astype(jnp.float32)
        keep = 1.0 - same * self_pair
        return lags * scale * keep[:, None, :] * live
    stacks = lax.map(one_slot, jnp.arange(N_CHAN * SLOTS, dtype=jnp.int32))
    return jnp.transpose(stacks, (1, 0, 2, 3)).astype(jnp.bfloat16)
```

```python
import functools
import math

import jax
import jax.numpy as jnp
import numpy as np
from jax import lax
from jax.experimental import pallas as pl
from jax.experimental.pallas import tpu as pltpu
from jax.sharding import PartitionSpec as P

MESH = pl.DeviceIdType.MESH

SEG_LEN = 512
F = 256
LOW_BIN = 1
NLAG = 64
SLOTS = 4
LEVEL = 0.5
EPS = 1e-06

BLK = 128
SEGS_DEV = 16
GROUPS = F // 8
DEPTH = SEGS_DEV * 2 * 8
TILE = 32
HALF = TILE // 2
KINDS = 3
OPP, UP, DOWN, OWN = range(4)


def transform_table():
    sample = np.arange(SEG_LEN)
    bins = np.arange(F) + LOW_BIN
    phase = (bins[:, None] * sample[None, :] % SEG_LEN) * (2.0 * math.pi / SEG_LEN)
    taper = 0.5 - 0.5 * np.cos(sample * (2.0 * math.pi / SEG_LEN))
    table = np.concatenate([taper[None, :] * np.cos(phase), -taper[None, :] * np.sin(phase)], axis=0)
    return jnp.asarray(table.astype(np.float32)).astype(jnp.bfloat16)


def lag_table():
    shifts = np.arange(NLAG) - NLAG // 2
    bins = np.arange(F) + LOW_BIN
    phase = (bins[:, None] * shifts[None, :] % SEG_LEN) * (2.0 * math.pi / SEG_LEN)
    table = np.stack([np.cos(phase), -np.sin(phase)], axis=1).reshape(2 * F, NLAG)
    return jnp.asarray(np.ascontiguousarray(table.T).astype(np.float32)).astype(jnp.bfloat16)


def nt_dot(a, b):
    return lax.dot_general(a, b, (((1,), (1,)), ((), ())), preferred_element_type=jnp.float32)


def stacks_kernel(
    n_chan,
    n_tm,
    scale,
    starts_ref,
    record_ref,
    table_ref,
    lag_ref,
    out_ref,
    own_ext,
    next_ext,
    turned,
    spectra,
    expanded,
    gram,
    part,
    relay_up,
    relay_down,
    from_down,
    from_up,
    shared,
    local_sem,
    near_send,
    near_recv,
    sum_send,
    sum_recv,
):
    c = lax.axis_index("chan")
    z = lax.axis_index("tm")
    block_len = record_ref.shape[1]
    up = lax.rem(z + 1, n_tm)
    down = lax.rem(z + n_tm - 1, n_tm)
    c_next = lax.rem(c + 1, n_chan)
    c_prev = lax.rem(c + n_chan - 1, n_chan)
    c_next2 = lax.rem(c + 2, n_chan)
    c_prev2 = lax.rem(c + n_chan - 2, n_chan)
    odd = lax.rem(c, 2)
    mate = c + 1 - 2 * odd

    tiles = block_len // 128

    def load_copy(tile):
        columns = pl.ds(pl.multiple_of(tile * 128, 128), 128)
        return pltpu.make_async_copy(record_ref.at[:, columns], own_ext.at[tile], local_sem.at[tile])

    def start_load(tile, carry):
        load_copy(tile).start()
        return carry

    def wait_load(tile, carry):
        load_copy(tile).wait()
        return carry

    lax.fori_loop(0, tiles, start_load, 0)

    barrier = pltpu.get_barrier_semaphore()
    for who in ((c, up), (c, down), (c_next2, z), (c_next2, up), (mate, z), (c_prev, z)):
        pl.semaphore_signal(barrier, inc=1, device_id=who, device_id_type=MESH)
    pl.semaphore_wait(barrier, 6)

    def near(index, src, dst, who):
        return pltpu.make_async_remote_copy(
            src_ref=src,
            dst_ref=dst,
            send_sem=near_send.at[index],
            recv_sem=near_recv.at[index],
            device_id=who,
            device_id_type=MESH,
        )

    main, halo = pl.ds(0, tiles), pl.ds(tiles, SEG_LEN // 128)
    head = own_ext.at[pl.ds(0, SEG_LEN // 128)]
    own_halo = near(0, head, own_ext.at[halo], (c, down))
    next_halo = near(1, head, next_ext.at[halo], (c_prev2, down))
    next_main = near(2, own_ext.at[main], next_ext.at[main], (c_prev2, z))
    lax.fori_loop(0, tiles, wait_load, 0)
    own_halo.start()
    next_halo.start()
    next_main.start()

    def to_mate():
        return near(3, spectra.at[2 - 2 * odd], spectra.at[1], (mate, z))

    def forward():
        return near(4, out_ref.at[2], shared, (c_next, z))

    def sum_copies(kind):
        low, high = pl.ds(0, HALF), pl.ds(HALF, HALF)
        routes = (
            (part.at[kind, OPP, low], relay_up.at[kind], up),
            (part.at[kind, OPP, high], relay_down.at[kind], down),
            (part.at[kind, UP, high], from_down.at[kind, high], up),
            (part.at[kind, UP, low], from_down.at[kind, low], up),
            (part.at[kind, DOWN, low], from_up.at[kind, low], down),
            (part.at[kind, DOWN, high], from_up.at[kind, high], down),
        )
        return [
            pltpu.make_async_remote_copy(
                src_ref=src,
                dst_ref=dst,
                send_sem=sum_send.at[kind, index],
                recv_sem=sum_recv.at[kind, index],
                device_id=(c, who),
                device_id_type=MESH,
            )
            for index, (src, dst, who) in enumerate(routes)
        ]

    ahead = lax.broadcasted_iota(jnp.int32, (256, 128), 0) - lax.broadcasted_iota(jnp.int32, (256, 128), 1)

    def cut(ext, seg):
        start = lax.rem(starts_ref[seg], block_len)
        first = lax.shift_right_logical(start, 7)
        shift = jnp.where(ahead == start - first * 128, 1.0, 0.0).astype(jnp.bfloat16)
        tiles = [ext[first + j] for j in range(SEG_LEN // 128 + 1)]
        rows = jnp.concatenate(
            [jnp.concatenate([tiles[j], tiles[j + 1]], axis=1) for j in range(SEG_LEN // 128)], axis=0
        )
        moved = jnp.dot(rows, shift, preferred_element_type=jnp.float32).astype(jnp.bfloat16)
        return jnp.concatenate([moved[BLK * j : BLK * (j + 1)] for j in range(SEG_LEN // 128)], axis=1)

    def whiten(ext, kind, turn_too):
        def step(pair, carry):
            pieces = jnp.concatenate([cut(ext, 2 * pair), cut(ext, 2 * pair + 1)], axis=0)
            both = nt_dot(table_ref[...], pieces)
            for h in range(2):
                real = both[:F, BLK * h : BLK * (h + 1)]
                imag = both[F:, BLK * h : BLK * (h + 1)]
                amplitude = jnp.sqrt(real * real + imag * imag)
                level = jnp.mean(amplitude, axis=0, keepdims=True) + EPS
                inverse = 1.0 / (amplitude + LEVEL * level)
                real = (real * inverse).reshape(GROUPS, 8, BLK)
                imag = (imag * inverse).reshape(GROUPS, 8, BLK)
                rows = pl.ds(pl.multiple_of((2 * pair + h) * 16, 16), 16)
                spectra[kind, :, rows, :] = jnp.concatenate([real, imag], axis=1).astype(jnp.bfloat16)
                if turn_too:
                    turned[:, rows, :] = jnp.concatenate([imag, -real], axis=1).astype(jnp.bfloat16)
            return carry

        lax.fori_loop(0, SEGS_DEV // 2, step, 0)

    def dest(tile):
        return lax.rem(z + jnp.where(tile == OPP, 2, jnp.where(tile == UP, 1, jnp.where(tile == DOWN, n_tm - 1, 0))), n_tm)

    ROWS = TILE * 8

    def expand(tile):
        row = lax.broadcasted_iota(jnp.int32, (ROWS, DEPTH), 0)
        col = lax.broadcasted_iota(jnp.int32, (ROWS, DEPTH), 1)
        wanted = (row % 2) * BLK + dest(tile) * TILE + row // 8
        pick = jnp.where(col == wanted, 1.0, 0.0).astype(jnp.bfloat16)
        mask = jnp.where(col % 4 == (row // 2) % 4, 1.0, 0.0)

        def step(group, carry):
            both = jnp.concatenate([spectra[0, group], turned[group]], axis=1)
            expanded[tile, group] = (nt_dot(pick, both) * mask).astype(jnp.bfloat16)
            return carry

        lax.fori_loop(0, GROUPS, step, 0)

    def tile_lags(kind, tile):
        row = lax.broadcasted_iota(jnp.int32, (DEPTH, BLK), 0)
        first = jnp.where(row % 8 < 4, 1.0, 0.0).astype(jnp.bfloat16)
        second = jnp.where(row % 8 < 4, 0.0, 1.0).astype(jnp.bfloat16)

        def gram_step(group, carry):
            right = spectra[kind, group]
            weights = jnp.concatenate([right * first, right * second], axis=1)
            cross = jnp.dot(expanded[tile, group], weights, preferred_element_type=jnp.float32)
            cross = jnp.concatenate(
                [cross[:, :BLK].reshape(TILE, 8, BLK), cross[:, BLK:].reshape(TILE, 8, BLK)], axis=1
            )
            rows = pl.ds(pl.multiple_of(group * 16, 16), 16)
            gram[:, rows, :] = cross.astype(jnp.bfloat16)
            return carry

        lax.fori_loop(0, GROUPS, gram_step, 0)

        def lag_step(pair, carry):
            two = jnp.concatenate([gram[2 * pair], gram[2 * pair + 1]], axis=1)
            lags = jnp.dot(lag_ref[...], two, preferred_element_type=jnp.float32) * scale
            part[kind, tile, 2 * pair] = lags[:, :BLK].astype(jnp.bfloat16)
            part[kind, tile, 2 * pair + 1] = lags[:, BLK:].astype(jnp.bfloat16)
            return carry

        lax.fori_loop(0, TILE // 2, lag_step, 0)

    def relay(kind):
        copies = sum_copies(kind)

        def add(tile, first_row, held):
            def step(i, carry):
                total = part[kind, tile, first_row + i].astype(jnp.float32) + held[kind, i].astype(jnp.float32)
                part[kind, tile, first_row + i] = total.astype(jnp.bfloat16)
                return carry

            lax.fori_loop(0, HALF, step, 0)

        copies[0].wait_recv()
        add(UP, 0, relay_up)
        copies[3].start()
        copies[1].wait_recv()
        add(DOWN, HALF, relay_down)
        copies[5].start()

    def finish(kind):
        copies = sum_copies(kind)
        for index in (2, 3, 4, 5):
            copies[index].wait_recv()
        column = lax.broadcasted_iota(jnp.int32, (NLAG, BLK), 1)

        def step(i, carry):
            total = part[kind, OWN, i].astype(jnp.float32) + (
                from_down[kind, i].astype(jnp.float32) + from_up[kind, i].astype(jnp.float32)
            )
            drop = jnp.where(kind == 0, z * TILE + i, -1)
            out_ref[kind, i] = jnp.where(column == drop, 0.0, total).astype(jnp.bfloat16)
            return carry

        lax.fori_loop(0, TILE, step, 0)

        @pl.when(kind == 2)
        def _():
            forward().start()

    own_halo.wait()
    whiten(own_ext, 0, True)

    @pl.when(odd == 1)
    def _():
        to_mate().start()

    def kind_of(step):
        return lax.rem(step * (1 + odd), KINDS)

    def kind_step(step, carry):
        kind = kind_of(step)

        @pl.when(step == 2 - odd)
        def _():
            next_main.wait()
            next_halo.wait()
            whiten(next_ext, 2, False)

            @pl.when(odd == 0)
            def _():
                to_mate().start()

        @pl.when(kind == 1)
        def _():
            to_mate().wait_recv()

        def tile_step(tile, carry):
            @pl.when(step == 0)
            def _():
                expand(tile)

            tile_lags(kind, tile)
            copies = sum_copies(kind)

            @pl.when(tile == OPP)
            def _():
                copies[0].start()
                copies[1].start()

            @pl.when(tile == UP)
            def _():
                copies[2].start()

            @pl.when(tile == DOWN)
            def _():
                copies[4].start()

            return carry

        lax.fori_loop(0, 4, tile_step, 0)
        relay(kind)

        @pl.when(step > 0)
        def _():
            finish(kind_of(step - 1))

        return carry

    lax.fori_loop(0, KINDS, kind_step, 0)
    finish(kind_of(2))

    to_mate().wait_send()
    forward().wait_send()
    forward().wait_recv()
    for kind in range(KINDS):
        for copy in sum_copies(kind):
            copy.wait_send()
    out_ref[3] = shared[...]


def place_kernel(kinds_ref, live_ref, block_ref, out_ref):
    q = pl.program_id(0)

    @pl.when(live_ref[q] > 0)
    def _():
        out_ref[...] = block_ref[0]

    @pl.when(live_ref[q] == 0)
    def _():
        out_ref[...] = jnp.zeros_like(out_ref)


def shards(n_chan, n_tm, record, seg_starts, pair_blocks, pair_owner):
    block_len = record.shape[1]
    scale = 2.0 / math.sqrt(SEGS_DEV * n_tm * F)
    bf16 = jnp.bfloat16
    stacks = pl.pallas_call(
        functools.partial(stacks_kernel, n_chan, n_tm, scale),
        out_shape=jax.ShapeDtypeStruct((4, TILE, NLAG, BLK), bf16),
        in_specs=[
            pl.BlockSpec(memory_space=pltpu.SMEM),
            pl.BlockSpec(memory_space=pl.ANY),
            pl.BlockSpec(memory_space=pltpu.VMEM),
            pl.BlockSpec(memory_space=pltpu.VMEM),
        ],
        out_specs=pl.BlockSpec(memory_space=pltpu.VMEM),
        scratch_shapes=[
            pltpu.VMEM(((block_len + SEG_LEN) // 128, BLK, 128), bf16),
            pltpu.VMEM(((block_len + SEG_LEN) // 128, BLK, 128), bf16),
            pltpu.VMEM((GROUPS, DEPTH, BLK), bf16),
            pltpu.VMEM((KINDS, GROUPS, DEPTH, BLK), bf16),
            pltpu.VMEM((4, GROUPS, TILE * 8, DEPTH), bf16),
            pltpu.VMEM((TILE, 2 * F, BLK), bf16),
            pltpu.VMEM((KINDS, 4, TILE, NLAG, BLK), bf16),
            pltpu.VMEM((KINDS, HALF, NLAG, BLK), bf16),
            pltpu.VMEM((KINDS, HALF, NLAG, BLK), bf16),
            pltpu.VMEM((KINDS, TILE, NLAG, BLK), bf16),
            pltpu.VMEM((KINDS, TILE, NLAG, BLK), bf16),
            pltpu.VMEM((TILE, NLAG, BLK), bf16),
            pltpu.SemaphoreType.DMA((block_len // 128,)),
            pltpu.SemaphoreType.DMA((5,)),
            pltpu.SemaphoreType.DMA((5,)),
            pltpu.SemaphoreType.DMA((KINDS, 6)),
            pltpu.SemaphoreType.DMA((KINDS, 6)),
        ],
        compiler_params=pltpu.CompilerParams(
            collective_id=0, has_side_effects=True, vmem_limit_bytes=60 * 1024 * 1024
        ),
        name="stacks",
    )(seg_starts, record, transform_table(), lag_table())

    chan = lax.axis_index("chan")
    wanted = chan * SLOTS + jnp.arange(SLOTS, dtype=jnp.int32)
    match = (pair_owner[None, :] == wanted[:, None]).astype(jnp.int32)
    apart = pair_blocks[:, 1] - pair_blocks[:, 0]
    kind = jnp.where((apart == 2) & (pair_blocks[:, 0] != chan), 3, apart)
    live = jnp.sum(match, axis=1)
    kinds = jnp.sum(match * kind[None, :], axis=1)
    return pl.pallas_call(
        place_kernel,
        out_shape=jax.ShapeDtypeStruct((TILE, SLOTS, NLAG, BLK), bf16),
        grid_spec=pltpu.PrefetchScalarGridSpec(
            num_scalar_prefetch=2,
            grid=(SLOTS,),
            in_specs=[pl.BlockSpec((1, TILE, NLAG, BLK), lambda q, kinds, live: (kinds[q], 0, 0, 0))],
            out_specs=pl.BlockSpec((TILE, None, NLAG, BLK), lambda q, kinds, live: (0, q, 0, 0)),
        ),
        name="place",
    )(kinds, live, stacks)


def solution(mesh):
    in_specs = (P("chan", "tm"), P("tm"), P(), P())
    out_specs = P("tm", "chan", None, None)
    body = functools.partial(shards, mesh.shape["chan"], mesh.shape["tm"])
    return jax.shard_map(body, mesh=mesh, in_specs=in_specs, out_specs=out_specs, check_vma=False)
```

```python
import functools
import math

import jax
import jax.numpy as jnp
import numpy as np
from jax import lax
from jax.experimental import pallas as pl
from jax.experimental.pallas import tpu as pltpu
from jax.sharding import PartitionSpec as P

MESH = pl.DeviceIdType.MESH

SEG_LEN = 512
F = 256
LOW_BIN = 1
NLAG = 64
SLOTS = 4
LEVEL = 0.5
EPS = 1e-06

BLK = 128
SEGS_DEV = 16
GROUPS = F // 8
DEPTH = SEGS_DEV * 2 * 8
TILE = 32
HALF = TILE // 2
KINDS = 3
OPP, UP, DOWN, OWN = range(4)


def transform_table():
    sample = np.arange(SEG_LEN)
    bins = np.arange(F) + LOW_BIN
    phase = (bins[:, None] * sample[None, :] % SEG_LEN) * (2.0 * math.pi / SEG_LEN)
    taper = 0.5 - 0.5 * np.cos(sample * (2.0 * math.pi / SEG_LEN))
    table = np.concatenate([taper[None, :] * np.cos(phase), -taper[None, :] * np.sin(phase)], axis=0)
    return jnp.asarray(table.astype(np.float32)).astype(jnp.bfloat16)


def lag_table():
    shifts = np.arange(NLAG) - NLAG // 2
    bins = np.arange(F) + LOW_BIN
    phase = (bins[:, None] * shifts[None, :] % SEG_LEN) * (2.0 * math.pi / SEG_LEN)
    table = np.stack([np.cos(phase), -np.sin(phase)], axis=1).reshape(2 * F, NLAG)
    return jnp.asarray(np.ascontiguousarray(table.T).astype(np.float32)).astype(jnp.bfloat16)


def nt_dot(a, b):
    return lax.dot_general(a, b, (((1,), (1,)), ((), ())), preferred_element_type=jnp.float32)


def stacks_kernel(
    n_chan,
    n_tm,
    scale,
    starts_ref,
    record_ref,
    table_ref,
    lag_ref,
    out_ref,
    own_ext,
    next_ext,
    turned,
    spectra,
    expanded,
    gram,
    part,
    relay_up,
    relay_down,
    from_down,
    from_up,
    shared,
    local_sem,
    near_send,
    near_recv,
    sum_send,
    sum_recv,
):
    c = lax.axis_index("chan")
    z = lax.axis_index("tm")
    block_len = record_ref.shape[1]
    up = lax.rem(z + 1, n_tm)
    down = lax.rem(z + n_tm - 1, n_tm)
    c_next = lax.rem(c + 1, n_chan)
    c_prev = lax.rem(c + n_chan - 1, n_chan)
    c_next2 = lax.rem(c + 2, n_chan)
    c_prev2 = lax.rem(c + n_chan - 2, n_chan)
    odd = lax.rem(c, 2)
    mate = c + 1 - 2 * odd

    tiles = block_len // 128

    def load_copy(tile):
        columns = pl.ds(pl.multiple_of(tile * 128, 128), 128)
        return pltpu.make_async_copy(record_ref.at[:, columns], own_ext.at[tile], local_sem.at[tile])

    def start_load(tile, carry):
        load_copy(tile).start()
        return carry

    def wait_load(tile, carry):
        load_copy(tile).wait()
        return carry

    lax.fori_loop(0, tiles, start_load, 0)

    barrier = pltpu.get_barrier_semaphore()
    for who in ((c, up), (c, down), (c_next2, z), (c_next2, up), (mate, z), (c_prev, z)):
        pl.semaphore_signal(barrier, inc=1, device_id=who, device_id_type=MESH)
    pl.semaphore_wait(barrier, 6)

    def near(index, src, dst, who):
        return pltpu.make_async_remote_copy(
            src_ref=src,
            dst_ref=dst,
            send_sem=near_send.at[index],
            recv_sem=near_recv.at[index],
            device_id=who,
            device_id_type=MESH,
        )

    main, halo = pl.ds(0, tiles), pl.ds(tiles, SEG_LEN // 128)
    head = own_ext.at[pl.ds(0, SEG_LEN // 128)]
    own_halo = near(0, head, own_ext.at[halo], (c, down))
    next_halo = near(1, head, next_ext.at[halo], (c_prev2, down))
    next_main = near(2, own_ext.at[main], next_ext.at[main], (c_prev2, z))
    lax.fori_loop(0, tiles, wait_load, 0)
    own_halo.start()
    next_halo.start()
    next_main.start()

    def to_mate():
        return near(3, spectra.at[2 - 2 * odd], spectra.at[1], (mate, z))

    def forward():
        return near(4, out_ref.at[2], shared, (c_next, z))

    def sum_copies(kind):
        low, high = pl.ds(0, HALF), pl.ds(HALF, HALF)
        routes = (
            (part.at[kind, OPP, low], relay_up.at[kind], up),
            (part.at[kind, OPP, high], relay_down.at[kind], down),
            (part.at[kind, UP, high], from_down.at[kind, high], up),
            (part.at[kind, UP, low], from_down.at[kind, low], up),
            (part.at[kind, DOWN, low], from_up.at[kind, low], down),
            (part.at[kind, DOWN, high], from_up.at[kind, high], down),
        )
        return [
            pltpu.make_async_remote_copy(
                src_ref=src,
                dst_ref=dst,
                send_sem=sum_send.at[kind, index],
                recv_sem=sum_recv.at[kind, index],
                device_id=(c, who),
                device_id_type=MESH,
            )
            for index, (src, dst, who) in enumerate(routes)
        ]

    lane = lax.broadcasted_iota(jnp.int32, (BLK, 128), 1)

    def cut(ext, seg):
        start = lax.rem(starts_ref[seg], block_len)
        first = lax.shift_right_logical(start, 7)
        rest = start - first * 128
        turn = jnp.bitwise_and(128 - rest, 127)
        cols = [
            pltpu.roll(ext[first + j].astype(jnp.float32), turn, 1) for j in range(SEG_LEN // 128 + 1)
        ]
        inside = lane < 128 - rest
        return jnp.concatenate(
            [jnp.where(inside, cols[j], cols[j + 1]) for j in range(SEG_LEN // 128)], axis=1
        ).astype(jnp.bfloat16)

    def whiten(ext, kind, turn_too):
        def step(pair, carry):
            pieces = jnp.concatenate([cut(ext, 2 * pair), cut(ext, 2 * pair + 1)], axis=0)
            both = nt_dot(table_ref[...], pieces)
            for h in range(2):
                real = both[:F, BLK * h : BLK * (h + 1)]
                imag = both[F:, BLK * h : BLK * (h + 1)]
                amplitude = jnp.sqrt(real * real + imag * imag)
                level = jnp.mean(amplitude, axis=0, keepdims=True) + EPS
                inverse = 1.0 / (amplitude + LEVEL * level)
                real = (real * inverse).reshape(GROUPS, 8, BLK)
                imag = (imag * inverse).reshape(GROUPS, 8, BLK)
                rows = pl.ds(pl.multiple_of((2 * pair + h) * 16, 16), 16)
                spectra[kind, :, rows, :] = jnp.concatenate([real, imag], axis=1).astype(jnp.bfloat16)
                if turn_too:
                    turned[:, rows, :] = jnp.concatenate([imag, -real], axis=1).astype(jnp.bfloat16)
            return carry

        lax.fori_loop(0, SEGS_DEV // 2, step, 0, unroll=4)

    def dest(tile):
        ahead = jnp.where(tile == OPP, 2, jnp.where(tile == UP, 1, jnp.where(tile == DOWN, n_tm - 1, 0)))
        return lax.rem(z + ahead, n_tm)

    def expand():
        row = lax.broadcasted_iota(jnp.int32, (8, DEPTH), 0)
        col = lax.broadcasted_iota(jnp.int32, (8, DEPTH), 1)
        mine = col % 4 == row // 2
        direct_mask = jnp.where(mine & (row % 2 == 0), 1.0, 0.0).reshape(1, 8, DEPTH)
        turned_mask = jnp.where(mine & (row % 2 == 1), 1.0, 0.0).reshape(1, 8, DEPTH)
        eye_row = lax.broadcasted_iota(jnp.int32, (BLK, BLK), 0)
        eye_col = lax.broadcasted_iota(jnp.int32, (BLK, BLK), 1)
        eye = jnp.where(eye_row == eye_col, 1.0, 0.0).astype(jnp.bfloat16)

        def step(group, carry):
            direct = nt_dot(eye, spectra[0, group])
            turn = nt_dot(eye, turned[group])
            for q in range(BLK // TILE):
                rows = slice(q * TILE, (q + 1) * TILE)
                both = (
                    direct[rows].reshape(TILE, 1, DEPTH) * direct_mask
                    + turn[rows].reshape(TILE, 1, DEPTH) * turned_mask
                )
                expanded[group, q * TILE * 8 : (q + 1) * TILE * 8] = both.reshape(TILE * 8, DEPTH).astype(jnp.bfloat16)
            return carry

        lax.fori_loop(0, GROUPS, step, 0, unroll=4)

    def tile_lags(kind, tile):
        row = lax.broadcasted_iota(jnp.int32, (DEPTH, BLK), 0)
        first = jnp.where(row % 8 < 4, 1.0, 0.0).astype(jnp.bfloat16)
        second = jnp.where(row % 8 < 4, 0.0, 1.0).astype(jnp.bfloat16)

        left_rows = pl.ds(pl.multiple_of(dest(tile) * TILE * 8, TILE * 8), TILE * 8)

        def gram_step(group, carry):
            right = spectra[kind, group]
            weights = jnp.concatenate([right * first, right * second], axis=1)
            cross = jnp.dot(expanded[group, left_rows], weights, preferred_element_type=jnp.float32)
            cross = jnp.concatenate(
                [cross[:, :BLK].reshape(TILE, 8, BLK), cross[:, BLK:].reshape(TILE, 8, BLK)], axis=1
            )
            rows = pl.ds(pl.multiple_of(group * 16, 16), 16)
            gram[:, rows, :] = cross.astype(jnp.bfloat16)
            return carry

        lax.fori_loop(0, GROUPS, gram_step, 0, unroll=16)

        def lag_step(pair, carry):
            two = jnp.concatenate([gram[2 * pair], gram[2 * pair + 1]], axis=1)
            lags = jnp.dot(lag_ref[...], two, preferred_element_type=jnp.float32) * scale
            part[kind, tile, 2 * pair] = lags[:, :BLK].astype(jnp.bfloat16)
            part[kind, tile, 2 * pair + 1] = lags[:, BLK:].astype(jnp.bfloat16)
            return carry

        lax.fori_loop(0, TILE // 2, lag_step, 0, unroll=16)

    def relay(kind):
        copies = sum_copies(kind)

        def add(tile, first_row, held):
            def step(i, carry):
                total = part[kind, tile, first_row + i].astype(jnp.float32) + held[kind, i].astype(jnp.float32)
                part[kind, tile, first_row + i] = total.astype(jnp.bfloat16)
                return carry

            lax.fori_loop(0, HALF, step, 0, unroll=4)

        copies[0].wait_recv()
        add(UP, 0, relay_up)
        copies[3].start()
        copies[1].wait_recv()
        add(DOWN, HALF, relay_down)
        copies[5].start()

    def finish(kind):
        copies = sum_copies(kind)
        for index in (2, 3, 4, 5):
            copies[index].wait_recv()
        column = lax.broadcasted_iota(jnp.int32, (NLAG, BLK), 1)

        def step(i, carry):
            total = part[kind, OWN, i].astype(jnp.float32) + (
                from_down[kind, i].astype(jnp.float32) + from_up[kind, i].astype(jnp.float32)
            )
            drop = jnp.where(kind == 0, z * TILE + i, -1)
            out_ref[kind, i] = jnp.where(column == drop, 0.0, total).astype(jnp.bfloat16)
            return carry

        lax.fori_loop(0, TILE, step, 0, unroll=4)

        @pl.when(kind == 2)
        def _():
            forward().start()

    own_halo.wait()
    whiten(own_ext, 0, True)

    @pl.when(odd == 1)
    def _():
        to_mate().start()

    expand()

    def kind_of(step):
        return lax.rem(step * (1 + odd), KINDS)

    def kind_step(step, carry):
        kind = kind_of(step)

        @pl.when(step == 2 - odd)
        def _():
            next_main.wait()
            next_halo.wait()
            whiten(next_ext, 2, False)

            @pl.when(odd == 0)
            def _():
                to_mate().start()

        @pl.when(kind == 1)
        def _():
            to_mate().wait_recv()

        def tile_step(tile, carry):
            tile_lags(kind, tile)
            copies = sum_copies(kind)

            @pl.when(tile == OPP)
            def _():
                copies[0].start()
                copies[1].start()

            @pl.when(tile == UP)
            def _():
                copies[2].start()

            @pl.when(tile == DOWN)
            def _():
                copies[4].start()

            return carry

        lax.fori_loop(0, 4, tile_step, 0)
        relay(kind)

        @pl.when(step > 0)
        def _():
            finish(kind_of(step - 1))

        return carry

    lax.fori_loop(0, KINDS, kind_step, 0)
    finish(kind_of(2))

    to_mate().wait_send()
    forward().wait_send()
    forward().wait_recv()
    for kind in range(KINDS):
        for copy in sum_copies(kind):
            copy.wait_send()
    out_ref[3] = shared[...]


def place_kernel(kinds_ref, live_ref, block_ref, out_ref):
    q = pl.program_id(0)

    @pl.when(live_ref[q] > 0)
    def _():
        out_ref[...] = block_ref[0]

    @pl.when(live_ref[q] == 0)
    def _():
        out_ref[...] = jnp.zeros_like(out_ref)


def shards(n_chan, n_tm, record, seg_starts, pair_blocks, pair_owner):
    block_len = record.shape[1]
    scale = 2.0 / math.sqrt(SEGS_DEV * n_tm * F)
    bf16 = jnp.bfloat16
    stacks = pl.pallas_call(
        functools.partial(stacks_kernel, n_chan, n_tm, scale),
        out_shape=jax.ShapeDtypeStruct((4, TILE, NLAG, BLK), bf16),
        in_specs=[
            pl.BlockSpec(memory_space=pltpu.SMEM),
            pl.BlockSpec(memory_space=pl.ANY),
            pl.BlockSpec(memory_space=pltpu.VMEM),
            pl.BlockSpec(memory_space=pltpu.VMEM),
        ],
        out_specs=pl.BlockSpec(memory_space=pltpu.VMEM),
        scratch_shapes=[
            pltpu.VMEM(((block_len + SEG_LEN) // 128, BLK, 128), bf16),
            pltpu.VMEM(((block_len + SEG_LEN) // 128, BLK, 128), bf16),
            pltpu.VMEM((GROUPS, DEPTH, BLK), bf16),
            pltpu.VMEM((KINDS, GROUPS, DEPTH, BLK), bf16),
            pltpu.VMEM((GROUPS, BLK * 8, DEPTH), bf16),
            pltpu.VMEM((TILE, 2 * F, BLK), bf16),
            pltpu.VMEM((KINDS, 4, TILE, NLAG, BLK), bf16),
            pltpu.VMEM((KINDS, HALF, NLAG, BLK), bf16),
            pltpu.VMEM((KINDS, HALF, NLAG, BLK), bf16),
            pltpu.VMEM((KINDS, TILE, NLAG, BLK), bf16),
            pltpu.VMEM((KINDS, TILE, NLAG, BLK), bf16),
            pltpu.VMEM((TILE, NLAG, BLK), bf16),
            pltpu.SemaphoreType.DMA((block_len // 128,)),
            pltpu.SemaphoreType.DMA((5,)),
            pltpu.SemaphoreType.DMA((5,)),
            pltpu.SemaphoreType.DMA((KINDS, 6)),
            pltpu.SemaphoreType.DMA((KINDS, 6)),
        ],
        compiler_params=pltpu.CompilerParams(
            collective_id=0, has_side_effects=True, vmem_limit_bytes=60 * 1024 * 1024
        ),
        name="stacks",
    )(seg_starts, record, transform_table(), lag_table())

    chan = lax.axis_index("chan")
    wanted = chan * SLOTS + jnp.arange(SLOTS, dtype=jnp.int32)
    match = (pair_owner[None, :] == wanted[:, None]).astype(jnp.int32)
    apart = pair_blocks[:, 1] - pair_blocks[:, 0]
    kind = jnp.where((apart == 2) & (pair_blocks[:, 0] != chan), 3, apart)
    live = jnp.sum(match, axis=1)
    kinds = jnp.sum(match * kind[None, :], axis=1)
    return pl.pallas_call(
        place_kernel,
        out_shape=jax.ShapeDtypeStruct((TILE, SLOTS, NLAG, BLK), bf16),
        grid_spec=pltpu.PrefetchScalarGridSpec(
            num_scalar_prefetch=2,
            grid=(SLOTS,),
            in_specs=[pl.BlockSpec((1, TILE, NLAG, BLK), lambda q, kinds, live: (kinds[q], 0, 0, 0))],
            out_specs=pl.BlockSpec((TILE, None, NLAG, BLK), lambda q, kinds, live: (0, q, 0, 0)),
        ),
        name="place",
    )(kinds, live, stacks)


def solution(mesh):
    in_specs = (P("chan", "tm"), P("tm"), P(), P())
    out_specs = P("tm", "chan", None, None)
    body = functools.partial(shards, mesh.shape["chan"], mesh.shape["tm"])
    return jax.shard_map(body, mesh=mesh, in_specs=in_specs, out_specs=out_specs, check_vma=False)
```

```python
import functools
import math

import jax
import jax.numpy as jnp
import numpy as np
from jax import lax
from jax.experimental import pallas as pl
from jax.experimental.pallas import tpu as pltpu
from jax.sharding import PartitionSpec as P

MESH = pl.DeviceIdType.MESH

SEG_LEN = 512
F = 256
LOW_BIN = 1
NLAG = 64
SLOTS = 4
LEVEL = 0.5
EPS = 1e-06

BLK = 128
SEGS_DEV = 16
GROUPS = F // 8
DEPTH = SEGS_DEV * 2 * 8
TILE = 32
HALF = TILE // 2
KINDS = 3
OPP, UP, DOWN, OWN = range(4)


def transform_table():
    sample = np.arange(SEG_LEN)
    bins = np.arange(F) + LOW_BIN
    phase = (bins[:, None] * sample[None, :] % SEG_LEN) * (2.0 * math.pi / SEG_LEN)
    taper = 0.5 - 0.5 * np.cos(sample * (2.0 * math.pi / SEG_LEN))
    table = np.concatenate([taper[None, :] * np.cos(phase), -taper[None, :] * np.sin(phase)], axis=0)
    return jnp.asarray(table.astype(np.float32)).astype(jnp.bfloat16)


def lag_table():
    shifts = np.arange(NLAG) - NLAG // 2
    bins = np.arange(F) + LOW_BIN
    phase = (bins[:, None] * shifts[None, :] % SEG_LEN) * (2.0 * math.pi / SEG_LEN)
    table = np.stack([np.cos(phase), -np.sin(phase)], axis=1).reshape(2 * F, NLAG)
    return jnp.asarray(np.ascontiguousarray(table.T).astype(np.float32)).astype(jnp.bfloat16)


def nt_dot(a, b):
    return lax.dot_general(a, b, (((1,), (1,)), ((), ())), preferred_element_type=jnp.float32)


def stacks_kernel(
    n_chan,
    n_tm,
    scale,
    starts_ref,
    blocks_ref,
    owner_ref,
    record_ref,
    table_hbm,
    lag_ref,
    out_ref,
    kinds_ref,
    table_ref,
    own_ext,
    next_ext,
    turned,
    sides,
    spectra,
    expanded,
    gram,
    part,
    relay_up,
    relay_down,
    from_down,
    from_up,
    done,
    local_sem,
    table_sem,
    done_sem,
    near_send,
    near_recv,
    sum_send,
    sum_recv,
):
    c = lax.axis_index("chan")
    z = lax.axis_index("tm")
    block_len = record_ref.shape[1]
    up = lax.rem(z + 1, n_tm)
    down = lax.rem(z + n_tm - 1, n_tm)
    c_next = lax.rem(c + 1, n_chan)
    c_prev = lax.rem(c + n_chan - 1, n_chan)
    c_next2 = lax.rem(c + 2, n_chan)
    c_prev2 = lax.rem(c + n_chan - 2, n_chan)
    odd = lax.rem(c, 2)
    mate = c + 1 - 2 * odd

    tiles = block_len // 128

    def load_copy(tile):
        columns = pl.ds(pl.multiple_of(tile * 128, 128), 128)
        return pltpu.make_async_copy(record_ref.at[:, columns], own_ext.at[tile], local_sem.at[tile])

    def start_load(tile, carry):
        load_copy(tile).start()
        return carry

    def wait_load(tile, carry):
        load_copy(tile).wait()
        return carry

    lax.fori_loop(0, tiles, start_load, 0)
    table_copy = pltpu.make_async_copy(table_hbm, table_ref, table_sem)
    table_copy.start()

    barrier = pltpu.get_barrier_semaphore()
    for who in ((c, up), (c, down), (c_next2, z), (c_next2, up), (mate, z), (c_prev, z)):
        pl.semaphore_signal(barrier, inc=1, device_id=who, device_id_type=MESH)
    pl.semaphore_wait(barrier, 6)

    def near(index, src, dst, who):
        return pltpu.make_async_remote_copy(
            src_ref=src,
            dst_ref=dst,
            send_sem=near_send.at[index],
            recv_sem=near_recv.at[index],
            device_id=who,
            device_id_type=MESH,
        )

    main, halo = pl.ds(0, tiles), pl.ds(tiles, SEG_LEN // 128)
    head = own_ext.at[pl.ds(0, SEG_LEN // 128)]
    own_halo = near(0, head, own_ext.at[halo], (c, down))
    next_halo = near(1, head, next_ext.at[halo], (c_prev2, down))
    next_main = near(2, own_ext.at[main], next_ext.at[main], (c_prev2, z))
    lax.fori_loop(0, tiles, wait_load, 0)
    own_halo.start()
    next_halo.start()
    next_main.start()

    def to_mate():
        return near(3, spectra.at[2 - 2 * odd], spectra.at[1], (mate, z))

    def forward():
        return near(4, done.at[2], out_ref.at[3], (c_next, z))

    def store(kind):
        return pltpu.make_async_copy(done.at[kind], out_ref.at[kind], done_sem.at[kind])

    def sum_copies(kind):
        low, high = pl.ds(0, HALF), pl.ds(HALF, HALF)
        routes = (
            (part.at[kind, OPP, low], relay_up.at[kind], up),
            (part.at[kind, OPP, high], relay_down.at[kind], down),
            (part.at[kind, UP, high], from_down.at[kind, high], up),
            (part.at[kind, UP, low], from_down.at[kind, low], up),
            (part.at[kind, DOWN, low], from_up.at[kind, low], down),
            (part.at[kind, DOWN, high], from_up.at[kind, high], down),
        )
        return [
            pltpu.make_async_remote_copy(
                src_ref=src,
                dst_ref=dst,
                send_sem=sum_send.at[kind, index],
                recv_sem=sum_recv.at[kind, index],
                device_id=(c, who),
                device_id_type=MESH,
            )
            for index, (src, dst, who) in enumerate(routes)
        ]

    lane = lax.broadcasted_iota(jnp.int32, (BLK, 128), 1)

    def cut(ext, seg):
        start = lax.rem(starts_ref[seg], block_len)
        first = lax.shift_right_logical(start, 7)
        rest = start - first * 128
        turn = jnp.bitwise_and(128 - rest, 127)
        cols = [
            pltpu.roll(ext[first + j].astype(jnp.float32), turn, 1) for j in range(SEG_LEN // 128 + 1)
        ]
        inside = lane < 128 - rest
        return jnp.concatenate(
            [jnp.where(inside, cols[j], cols[j + 1]) for j in range(SEG_LEN // 128)], axis=1
        ).astype(jnp.bfloat16)

    def whiten(ext, kind, turn_too):
        def step(pair, carry):
            pieces = jnp.concatenate([cut(ext, 2 * pair), cut(ext, 2 * pair + 1)], axis=0)
            both = nt_dot(table_ref[...], pieces)
            for h in range(2):
                real = both[:F, BLK * h : BLK * (h + 1)]
                imag = both[F:, BLK * h : BLK * (h + 1)]
                amplitude = jnp.sqrt(real * real + imag * imag)
                level = jnp.mean(amplitude, axis=0, keepdims=True) + EPS
                inverse = 1.0 / (amplitude + LEVEL * level)
                real = (real * inverse).reshape(GROUPS, 8, BLK)
                imag = (imag * inverse).reshape(GROUPS, 8, BLK)
                rows = pl.ds(pl.multiple_of((2 * pair + h) * 16, 16), 16)
                spectra[kind, :, rows, :] = jnp.concatenate([real, imag], axis=1).astype(jnp.bfloat16)
                if turn_too:
                    turned[:, rows, :] = jnp.concatenate([imag, -real], axis=1).astype(jnp.bfloat16)
            return carry

        lax.fori_loop(0, SEGS_DEV // 2, step, 0, unroll=4)

    def dest(tile):
        ahead = jnp.where(tile == OPP, 2, jnp.where(tile == UP, 1, jnp.where(tile == DOWN, n_tm - 1, 0)))
        return lax.rem(z + ahead, n_tm)

    def transpose():
        eye_row = lax.broadcasted_iota(jnp.int32, (BLK, BLK), 0)
        eye_col = lax.broadcasted_iota(jnp.int32, (BLK, BLK), 1)
        eye = jnp.where(eye_row == eye_col, 1.0, 0.0).astype(jnp.bfloat16)

        def step(group, carry):
            sides[group] = nt_dot(eye, jnp.concatenate([spectra[0, group], turned[group]], axis=0))
            return carry

        lax.fori_loop(0, GROUPS, step, 0, unroll=8)

    def tile_lags(step, kind, tile):
        row = lax.broadcasted_iota(jnp.int32, (DEPTH, BLK), 0)
        low_bins = jnp.where(row % 8 < 4, 1.0, 0.0).astype(jnp.bfloat16)
        high_bins = jnp.where(row % 8 < 4, 0.0, 1.0).astype(jnp.bfloat16)
        first = dest(tile) * TILE
        left_rows = pl.ds(pl.multiple_of(first * 8, TILE * 8), TILE * 8)

        def cross(group, left):
            right = spectra[kind, group]
            weights = jnp.concatenate([right * low_bins, right * high_bins], axis=1)
            both = jnp.dot(left, weights, preferred_element_type=jnp.float32)
            both = jnp.concatenate(
                [both[:, :BLK].reshape(TILE, 8, BLK), both[:, BLK:].reshape(TILE, 8, BLK)], axis=1
            )
            rows = pl.ds(pl.multiple_of(group * 16, 16), 16)
            gram[:, rows, :] = both.astype(jnp.bfloat16)

        @pl.when(step == 0)
        def _():
            row = lax.broadcasted_iota(jnp.int32, (8, DEPTH), 0)
            col = lax.broadcasted_iota(jnp.int32, (8, DEPTH), 1)
            mine = col % 4 == row // 2
            direct_mask = jnp.where(mine & (row % 2 == 0), 1.0, 0.0)
            turned_mask = jnp.where(mine & (row % 2 == 1), 1.0, 0.0)

            def expand_step(group, carry):
                parts = []
                for i in range(TILE):
                    line = sides[group, pl.ds(first + i, 1), :]
                    parts.append(line[:, :DEPTH] * direct_mask + line[:, DEPTH:] * turned_mask)
                left = jnp.concatenate(parts, axis=0).astype(jnp.bfloat16)
                expanded[group, left_rows] = left
                cross(group, left)
                return carry

            lax.fori_loop(0, GROUPS, expand_step, 0, unroll=4)

        @pl.when(step > 0)
        def _():
            def gram_step(group, carry):
                cross(group, expanded[group, left_rows])
                return carry

            lax.fori_loop(0, GROUPS, gram_step, 0, unroll=32)

        def lag_step(pair, carry):
            two = jnp.concatenate([gram[2 * pair], gram[2 * pair + 1]], axis=1)
            lags = jnp.dot(lag_ref[...], two, preferred_element_type=jnp.float32) * scale
            part[kind, tile, 2 * pair] = lags[:, :BLK].astype(jnp.bfloat16)
            part[kind, tile, 2 * pair + 1] = lags[:, BLK:].astype(jnp.bfloat16)
            return carry

        lax.fori_loop(0, TILE // 2, lag_step, 0, unroll=16)

    def relay(kind):
        copies = sum_copies(kind)

        def add(tile, first_row, held):
            def step(i, carry):
                total = part[kind, tile, first_row + i].astype(jnp.float32) + held[kind, i].astype(jnp.float32)
                part[kind, tile, first_row + i] = total.astype(jnp.bfloat16)
                return carry

            lax.fori_loop(0, HALF, step, 0, unroll=4)

        copies[0].wait_recv()
        add(UP, 0, relay_up)
        copies[3].start()
        copies[1].wait_recv()
        add(DOWN, HALF, relay_down)
        copies[5].start()

    def finish(kind):
        copies = sum_copies(kind)
        for index in (2, 3, 4, 5):
            copies[index].wait_recv()
        column = lax.broadcasted_iota(jnp.int32, (NLAG, BLK), 1)

        def step(i, carry):
            total = part[kind, OWN, i].astype(jnp.float32) + (
                from_down[kind, i].astype(jnp.float32) + from_up[kind, i].astype(jnp.float32)
            )
            drop = jnp.where(kind == 0, z * TILE + i, -1)
            done[kind, i] = jnp.where(column == drop, 0.0, total).astype(jnp.bfloat16)
            return carry

        lax.fori_loop(0, TILE, step, 0, unroll=4)

        store(kind).start()

        @pl.when(kind == 2)
        def _():
            forward().start()

    def match(p, slots):
        apart = blocks_ref[p, 1] - blocks_ref[p, 0]
        kind = jnp.where(blocks_ref[p, 0] == c, apart, 3)
        owned = owner_ref[p] - c * SLOTS
        return tuple(held + jnp.where(owned == q, kind + 1, 0) for q, held in enumerate(slots))

    for q, held in enumerate(lax.fori_loop(0, owner_ref.shape[0], match, (0,) * SLOTS)):
        kinds_ref[q] = held

    table_copy.wait()
    own_halo.wait()
    whiten(own_ext, 0, True)

    @pl.when(odd == 1)
    def _():
        to_mate().start()

    transpose()

    def kind_of(step):
        return lax.rem(step * (1 + odd), KINDS)

    def kind_step(step, carry):
        kind = kind_of(step)

        @pl.when(step == 2 - odd)
        def _():
            next_main.wait()
            next_halo.wait()
            whiten(next_ext, 2, False)

            @pl.when(odd == 0)
            def _():
                to_mate().start()

        @pl.when(kind == 1)
        def _():
            to_mate().wait_recv()

        def tile_step(tile, carry):
            tile_lags(step, kind, tile)
            copies = sum_copies(kind)

            @pl.when(tile == OPP)
            def _():
                copies[0].start()
                copies[1].start()

            @pl.when(tile == UP)
            def _():
                copies[2].start()

            @pl.when(tile == DOWN)
            def _():
                copies[4].start()

            return carry

        lax.fori_loop(0, 4, tile_step, 0)
        relay(kind)

        @pl.when(step > 0)
        def _():
            finish(kind_of(step - 1))

        return carry

    lax.fori_loop(0, KINDS, kind_step, 0)
    finish(kind_of(2))

    to_mate().wait_send()
    forward().wait_send()
    forward().wait_recv()
    for kind in range(KINDS):
        for copy in sum_copies(kind):
            copy.wait_send()
    for kind in range(KINDS):
        store(kind).wait()


def place_kernel(kinds_ref, stacks_ref, out_ref, zeros, sem):
    zeros[...] = jnp.zeros_like(zeros)

    def copy(q, src):
        return pltpu.make_async_copy(src, out_ref.at[:, q], sem.at[q])

    for q in range(SLOTS):
        held = kinds_ref[q]

        @pl.when(held > 0)
        def _():
            copy(q, stacks_ref.at[held - 1]).start()

        @pl.when(held == 0)
        def _():
            copy(q, zeros).start()

    for q in range(SLOTS):
        copy(q, zeros).wait()


def shards(n_chan, n_tm, record, seg_starts, pair_blocks, pair_owner):
    block_len = record.shape[1]
    scale = 2.0 / math.sqrt(SEGS_DEV * n_tm * F)
    bf16 = jnp.bfloat16
    hbm = pl.BlockSpec(memory_space=pl.ANY)
    smem = pl.BlockSpec(memory_space=pltpu.SMEM)
    stacks, kinds = pl.pallas_call(
        functools.partial(stacks_kernel, n_chan, n_tm, scale),
        out_shape=(
            jax.ShapeDtypeStruct((4, TILE, NLAG, BLK), bf16),
            jax.ShapeDtypeStruct((SLOTS,), jnp.int32),
        ),
        in_specs=[smem, smem, smem, hbm, hbm, pl.BlockSpec(memory_space=pltpu.VMEM)],
        out_specs=(hbm, smem),
        scratch_shapes=[
            pltpu.VMEM((2 * F, SEG_LEN), bf16),
            pltpu.VMEM(((block_len + SEG_LEN) // 128, BLK, 128), bf16),
            pltpu.VMEM(((block_len + SEG_LEN) // 128, BLK, 128), bf16),
            pltpu.VMEM((GROUPS, DEPTH, BLK), bf16),
            pltpu.VMEM((GROUPS, BLK, 2 * DEPTH), jnp.float32),
            pltpu.VMEM((KINDS, GROUPS, DEPTH, BLK), bf16),
            pltpu.VMEM((GROUPS, BLK * 8, DEPTH), bf16),
            pltpu.VMEM((TILE, 2 * F, BLK), bf16),
            pltpu.VMEM((KINDS, 4, TILE, NLAG, BLK), bf16),
            pltpu.VMEM((KINDS, HALF, NLAG, BLK), bf16),
            pltpu.VMEM((KINDS, HALF, NLAG, BLK), bf16),
            pltpu.VMEM((KINDS, TILE, NLAG, BLK), bf16),
            pltpu.VMEM((KINDS, TILE, NLAG, BLK), bf16),
            pltpu.VMEM((KINDS, TILE, NLAG, BLK), bf16),
            pltpu.SemaphoreType.DMA((block_len // 128,)),
            pltpu.SemaphoreType.DMA,
            pltpu.SemaphoreType.DMA((KINDS,)),
            pltpu.SemaphoreType.DMA((5,)),
            pltpu.SemaphoreType.DMA((5,)),
            pltpu.SemaphoreType.DMA((KINDS, 6)),
            pltpu.SemaphoreType.DMA((KINDS, 6)),
        ],
        compiler_params=pltpu.CompilerParams(
            collective_id=0, has_side_effects=True, vmem_limit_bytes=60 * 1024 * 1024
        ),
        name="stacks",
    )(seg_starts, pair_blocks, pair_owner, record, transform_table(), lag_table())
    return pl.pallas_call(
        place_kernel,
        out_shape=jax.ShapeDtypeStruct((TILE, SLOTS, NLAG, BLK), bf16),
        in_specs=[smem, hbm],
        out_specs=hbm,
        scratch_shapes=[pltpu.VMEM((TILE, NLAG, BLK), bf16), pltpu.SemaphoreType.DMA((SLOTS,))],
        name="place",
    )(kinds, stacks)


def solution(mesh):
    in_specs = (P("chan", "tm"), P("tm"), P(), P())
    out_specs = P("tm", "chan", None, None)
    body = functools.partial(shards, mesh.shape["chan"], mesh.shape["tm"])
    return jax.shard_map(body, mesh=mesh, in_specs=in_specs, out_specs=out_specs, check_vma=False)
```

```python
import functools
import math

import jax
import jax.numpy as jnp
import numpy as np
from jax import lax
from jax.experimental import pallas as pl
from jax.experimental.pallas import tpu as pltpu
from jax.sharding import PartitionSpec as P

MESH = pl.DeviceIdType.MESH

SEG_LEN = 512
F = 256
LOW_BIN = 1
NLAG = 64
SLOTS = 4
LEVEL = 0.5
EPS = 1e-06

BLK = 128
SEGS_DEV = 16
GROUPS = F // 8
DEPTH = SEGS_DEV * 2 * 8
TILE = 32
HALF = TILE // 2
KINDS = 3
OPP, UP, DOWN, OWN = range(4)


def transform_table():
    sample = np.arange(SEG_LEN)
    bins = np.arange(F) + LOW_BIN
    phase = (bins[:, None] * sample[None, :] % SEG_LEN) * (2.0 * math.pi / SEG_LEN)
    taper = 0.5 - 0.5 * np.cos(sample * (2.0 * math.pi / SEG_LEN))
    table = np.concatenate([taper[None, :] * np.cos(phase), -taper[None, :] * np.sin(phase)], axis=0)
    return jnp.asarray(table.astype(np.float32)).astype(jnp.bfloat16)


def lag_table():
    shifts = np.arange(NLAG) - NLAG // 2
    bins = np.arange(F) + LOW_BIN
    phase = (bins[:, None] * shifts[None, :] % SEG_LEN) * (2.0 * math.pi / SEG_LEN)
    table = np.stack([np.cos(phase), -np.sin(phase)], axis=1).reshape(2 * F, NLAG)
    return jnp.asarray(np.ascontiguousarray(table.T).astype(np.float32)).astype(jnp.bfloat16)


def nt_dot(a, b):
    return lax.dot_general(a, b, (((1,), (1,)), ((), ())), preferred_element_type=jnp.float32)


def stacks_kernel(
    n_chan,
    n_tm,
    scale,
    starts_ref,
    blocks_ref,
    owner_ref,
    record_ref,
    table_hbm,
    lag_ref,
    out_ref,
    kinds_ref,
    table_ref,
    own_ext,
    next_ext,
    turned,
    sides,
    spectra,
    expanded,
    gram,
    part,
    relay_up,
    relay_down,
    from_down,
    from_up,
    done,
    local_sem,
    table_sem,
    done_sem,
    near_send,
    near_recv,
    sum_send,
    sum_recv,
):
    c = lax.axis_index("chan")
    z = lax.axis_index("tm")
    block_len = record_ref.shape[1]
    up = lax.rem(z + 1, n_tm)
    down = lax.rem(z + n_tm - 1, n_tm)
    c_next = lax.rem(c + 1, n_chan)
    c_prev = lax.rem(c + n_chan - 1, n_chan)
    c_next2 = lax.rem(c + 2, n_chan)
    c_prev2 = lax.rem(c + n_chan - 2, n_chan)
    odd = lax.rem(c, 2)
    mate = c + 1 - 2 * odd

    tiles = block_len // 128

    def load_copy(tile):
        columns = pl.ds(pl.multiple_of(tile * 128, 128), 128)
        return pltpu.make_async_copy(record_ref.at[:, columns], own_ext.at[tile], local_sem.at[tile])

    def start_load(tile, carry):
        load_copy(tile).start()
        return carry

    def wait_load(tile, carry):
        load_copy(tile).wait()
        return carry

    lax.fori_loop(0, tiles, start_load, 0)
    table_copy = pltpu.make_async_copy(table_hbm, table_ref, table_sem)
    table_copy.start()

    barrier = pltpu.get_barrier_semaphore()
    for who in ((c, up), (c, down), (c_next2, z), (c_next2, up), (mate, z), (c_prev, z)):
        pl.semaphore_signal(barrier, inc=1, device_id=who, device_id_type=MESH)
    pl.semaphore_wait(barrier, 6)

    def near(index, src, dst, who):
        return pltpu.make_async_remote_copy(
            src_ref=src,
            dst_ref=dst,
            send_sem=near_send.at[index],
            recv_sem=near_recv.at[index],
            device_id=who,
            device_id_type=MESH,
        )

    main, halo = pl.ds(0, tiles), pl.ds(tiles, SEG_LEN // 128)
    head = own_ext.at[pl.ds(0, SEG_LEN // 128)]
    own_halo = near(0, head, own_ext.at[halo], (c, down))
    next_halo = near(1, head, next_ext.at[halo], (c_prev2, down))
    next_main = near(2, own_ext.at[main], next_ext.at[main], (c_prev2, z))
    lax.fori_loop(0, tiles, wait_load, 0)
    own_halo.start()
    next_halo.start()
    next_main.start()

    def to_mate():
        return near(3, spectra.at[2 - 2 * odd], spectra.at[1], (mate, z))

    def forward():
        return near(4, done.at[2], out_ref.at[3], (c_next, z))

    def store(kind):
        return pltpu.make_async_copy(done.at[kind], out_ref.at[kind], done_sem.at[kind])

    def sum_copies(kind):
        low, high = pl.ds(0, HALF), pl.ds(HALF, HALF)
        routes = (
            (part.at[kind, OPP, low], relay_up.at[kind], up),
            (part.at[kind, OPP, high], relay_down.at[kind], down),
            (part.at[kind, UP, high], from_down.at[kind, high], up),
            (part.at[kind, UP, low], from_down.at[kind, low], up),
            (part.at[kind, DOWN, low], from_up.at[kind, low], down),
            (part.at[kind, DOWN, high], from_up.at[kind, high], down),
        )
        return [
            pltpu.make_async_remote_copy(
                src_ref=src,
                dst_ref=dst,
                send_sem=sum_send.at[kind, index],
                recv_sem=sum_recv.at[kind, index],
                device_id=(c, who),
                device_id_type=MESH,
            )
            for index, (src, dst, who) in enumerate(routes)
        ]

    lane = lax.broadcasted_iota(jnp.int32, (BLK, 128), 1)

    def cut(ext, seg):
        start = lax.rem(starts_ref[seg], block_len)
        first = lax.shift_right_logical(start, 7)
        rest = start - first * 128
        turn = jnp.bitwise_and(128 - rest, 127)
        cols = [
            pltpu.roll(ext[first + j].astype(jnp.float32), turn, 1) for j in range(SEG_LEN // 128 + 1)
        ]
        inside = lane < 128 - rest
        return jnp.concatenate(
            [jnp.where(inside, cols[j], cols[j + 1]) for j in range(SEG_LEN // 128)], axis=1
        ).astype(jnp.bfloat16)

    def whiten(ext, kind, turn_too):
        def step(pair, carry):
            pieces = jnp.concatenate([cut(ext, 2 * pair), cut(ext, 2 * pair + 1)], axis=0)
            both = nt_dot(table_ref[...], pieces)
            for h in range(2):
                real = both[:F, BLK * h : BLK * (h + 1)]
                imag = both[F:, BLK * h : BLK * (h + 1)]
                amplitude = jnp.sqrt(real * real + imag * imag)
                level = jnp.mean(amplitude, axis=0, keepdims=True) + EPS
                inverse = 1.0 / (amplitude + LEVEL * level)
                real = (real * inverse).reshape(GROUPS, 8, BLK)
                imag = (imag * inverse).reshape(GROUPS, 8, BLK)
                rows = pl.ds(pl.multiple_of((2 * pair + h) * 16, 16), 16)
                spectra[kind, :, rows, :] = jnp.concatenate([real, imag], axis=1).astype(jnp.bfloat16)
                if turn_too:
                    turned[:, rows, :] = jnp.concatenate([imag, -real], axis=1).astype(jnp.bfloat16)
            return carry

        lax.fori_loop(0, SEGS_DEV // 2, step, 0, unroll=4)

    def dest(tile):
        ahead = jnp.where(tile == OPP, 2, jnp.where(tile == UP, 1, jnp.where(tile == DOWN, n_tm - 1, 0)))
        return lax.rem(z + ahead, n_tm)

    def transpose():
        eye_row = lax.broadcasted_iota(jnp.int32, (BLK, BLK), 0)
        eye_col = lax.broadcasted_iota(jnp.int32, (BLK, BLK), 1)
        eye = jnp.where(eye_row == eye_col, 1.0, 0.0).astype(jnp.bfloat16)

        def step(group, carry):
            sides[group] = nt_dot(eye, jnp.concatenate([spectra[0, group], turned[group]], axis=0))
            return carry

        lax.fori_loop(0, GROUPS, step, 0, unroll=8)

    def tile_lags(step, kind, tile):
        row = lax.broadcasted_iota(jnp.int32, (DEPTH, BLK), 0)
        low_bins = jnp.where(row % 8 < 4, 1.0, 0.0).astype(jnp.bfloat16)
        high_bins = jnp.where(row % 8 < 4, 0.0, 1.0).astype(jnp.bfloat16)
        first = dest(tile) * TILE
        left_rows = pl.ds(pl.multiple_of(first * 8, TILE * 8), TILE * 8)

        def cross(group, left):
            right = spectra[kind, group]
            weights = jnp.concatenate([right * low_bins, right * high_bins], axis=1)
            both = jnp.dot(left, weights, preferred_element_type=jnp.float32)
            both = jnp.concatenate(
                [both[:, :BLK].reshape(TILE, 8, BLK), both[:, BLK:].reshape(TILE, 8, BLK)], axis=1
            )
            rows = pl.ds(pl.multiple_of(group * 16, 16), 16)
            gram[:, rows, :] = both.astype(jnp.bfloat16)

        @pl.when(step == 0)
        def _():
            row = lax.broadcasted_iota(jnp.int32, (8, DEPTH), 0)
            col = lax.broadcasted_iota(jnp.int32, (8, DEPTH), 1)
            mine = col % 4 == row // 2
            direct_mask = jnp.where(mine & (row % 2 == 0), 1.0, 0.0)
            turned_mask = jnp.where(mine & (row % 2 == 1), 1.0, 0.0)

            def expand_step(group, carry):
                parts = []
                for i in range(TILE):
                    line = sides[group, pl.ds(first + i, 1), :]
                    parts.append(line[:, :DEPTH] * direct_mask + line[:, DEPTH:] * turned_mask)
                left = jnp.concatenate(parts, axis=0).astype(jnp.bfloat16)
                expanded[group, left_rows] = left
                cross(group, left)
                return carry

            lax.fori_loop(0, GROUPS, expand_step, 0, unroll=4)

        @pl.when(step > 0)
        def _():
            def gram_step(group, carry):
                cross(group, expanded[group, left_rows])
                return carry

            lax.fori_loop(0, GROUPS, gram_step, 0, unroll=32)

        def lag_step(pair, carry):
            two = jnp.concatenate([gram[2 * pair], gram[2 * pair + 1]], axis=1)
            lags = jnp.dot(lag_ref[...], two, preferred_element_type=jnp.float32) * scale
            part[kind, tile, 2 * pair] = lags[:, :BLK].astype(jnp.bfloat16)
            part[kind, tile, 2 * pair + 1] = lags[:, BLK:].astype(jnp.bfloat16)
            return carry

        lax.fori_loop(0, TILE // 2, lag_step, 0, unroll=16)

    def relay(kind):
        copies = sum_copies(kind)

        def add(tile, first_row, held):
            def step(i, carry):
                total = part[kind, tile, first_row + i].astype(jnp.float32) + held[kind, i].astype(jnp.float32)
                part[kind, tile, first_row + i] = total.astype(jnp.bfloat16)
                return carry

            lax.fori_loop(0, HALF, step, 0, unroll=4)

        copies[0].wait_recv()
        add(UP, 0, relay_up)
        copies[3].start()
        copies[1].wait_recv()
        add(DOWN, HALF, relay_down)
        copies[5].start()

    def finish(kind):
        copies = sum_copies(kind)
        for index in (2, 3, 4, 5):
            copies[index].wait_recv()
        column = lax.broadcasted_iota(jnp.int32, (NLAG, BLK), 1)

        def step(i, carry):
            total = part[kind, OWN, i].astype(jnp.float32) + (
                from_down[kind, i].astype(jnp.float32) + from_up[kind, i].astype(jnp.float32)
            )
            drop = jnp.where(kind == 0, z * TILE + i, -1)
            done[kind, i] = jnp.where(column == drop, 0.0, total).astype(jnp.bfloat16)
            return carry

        lax.fori_loop(0, TILE, step, 0, unroll=4)

        store(kind).start()

        @pl.when(kind == 2)
        def _():
            forward().start()

    def match(p, slots):
        apart = blocks_ref[1, p] - blocks_ref[0, p]
        kind = jnp.where(blocks_ref[0, p] == c, apart, 3)
        owned = owner_ref[p] - c * SLOTS
        return tuple(held + jnp.where(owned == q, kind + 1, 0) for q, held in enumerate(slots))

    for q, held in enumerate(lax.fori_loop(0, owner_ref.shape[0], match, (0,) * SLOTS)):
        kinds_ref[q] = held

    table_copy.wait()
    own_halo.wait()
    whiten(own_ext, 0, True)

    @pl.when(odd == 1)
    def _():
        to_mate().start()

    transpose()

    def kind_of(step):
        return lax.rem(step * (1 + odd), KINDS)

    def kind_step(step, carry):
        kind = kind_of(step)

        @pl.when(step == 2 - odd)
        def _():
            next_main.wait()
            next_halo.wait()
            whiten(next_ext, 2, False)

            @pl.when(odd == 0)
            def _():
                to_mate().start()

        @pl.when(kind == 1)
        def _():
            to_mate().wait_recv()

        def tile_step(tile, carry):
            tile_lags(step, kind, tile)
            copies = sum_copies(kind)

            @pl.when(tile == OPP)
            def _():
                copies[0].start()
                copies[1].start()

            @pl.when(tile == UP)
            def _():
                copies[2].start()

            @pl.when(tile == DOWN)
            def _():
                copies[4].start()

            return carry

        lax.fori_loop(0, 4, tile_step, 0)
        relay(kind)

        @pl.when(step > 0)
        def _():
            finish(kind_of(step - 1))

        return carry

    lax.fori_loop(0, KINDS, kind_step, 0)
    finish(kind_of(2))

    to_mate().wait_send()
    forward().wait_send()
    forward().wait_recv()
    for kind in range(KINDS):
        for copy in sum_copies(kind):
            copy.wait_send()
    for kind in range(KINDS):
        store(kind).wait()


def place_kernel(kinds_ref, stacks_ref, out_ref, held, in_sem, out_sem):
    def fetch(q):
        return pltpu.make_async_copy(stacks_ref.at[kinds_ref[q] - 1], held.at[q], in_sem.at[q])

    def put(q):
        return pltpu.make_async_copy(held.at[q], out_ref.at[:, q], out_sem.at[q])

    for q in range(SLOTS):

        @pl.when(kinds_ref[q] > 0)
        def _():
            fetch(q).start()

        @pl.when(kinds_ref[q] == 0)
        def _():
            held[q] = jnp.zeros_like(held[q])

    for q in range(SLOTS):

        @pl.when(kinds_ref[q] > 0)
        def _():
            fetch(q).wait()

        put(q).start()

    for q in range(SLOTS):
        put(q).wait()


def shards(n_chan, n_tm, record, seg_starts, pair_blocks, pair_owner):
    block_len = record.shape[1]
    scale = 2.0 / math.sqrt(SEGS_DEV * n_tm * F)
    bf16 = jnp.bfloat16
    hbm = pl.BlockSpec(memory_space=pl.ANY)
    smem = pl.BlockSpec(memory_space=pltpu.SMEM)
    stacks, kinds = pl.pallas_call(
        functools.partial(stacks_kernel, n_chan, n_tm, scale),
        out_shape=(
            jax.ShapeDtypeStruct((4, TILE, NLAG, BLK), bf16),
            jax.ShapeDtypeStruct((SLOTS,), jnp.int32),
        ),
        in_specs=[smem, smem, smem, hbm, hbm, pl.BlockSpec(memory_space=pltpu.VMEM)],
        out_specs=(hbm, smem),
        scratch_shapes=[
            pltpu.VMEM((2 * F, SEG_LEN), bf16),
            pltpu.VMEM(((block_len + SEG_LEN) // 128, BLK, 128), bf16),
            pltpu.VMEM(((block_len + SEG_LEN) // 128, BLK, 128), bf16),
            pltpu.VMEM((GROUPS, DEPTH, BLK), bf16),
            pltpu.VMEM((GROUPS, BLK, 2 * DEPTH), jnp.float32),
            pltpu.VMEM((KINDS, GROUPS, DEPTH, BLK), bf16),
            pltpu.VMEM((GROUPS, BLK * 8, DEPTH), bf16),
            pltpu.VMEM((TILE, 2 * F, BLK), bf16),
            pltpu.VMEM((KINDS, 4, TILE, NLAG, BLK), bf16),
            pltpu.VMEM((KINDS, HALF, NLAG, BLK), bf16),
            pltpu.VMEM((KINDS, HALF, NLAG, BLK), bf16),
            pltpu.VMEM((KINDS, TILE, NLAG, BLK), bf16),
            pltpu.VMEM((KINDS, TILE, NLAG, BLK), bf16),
            pltpu.VMEM((KINDS, TILE, NLAG, BLK), bf16),
            pltpu.SemaphoreType.DMA((block_len // 128,)),
            pltpu.SemaphoreType.DMA,
            pltpu.SemaphoreType.DMA((KINDS,)),
            pltpu.SemaphoreType.DMA((5,)),
            pltpu.SemaphoreType.DMA((5,)),
            pltpu.SemaphoreType.DMA((KINDS, 6)),
            pltpu.SemaphoreType.DMA((KINDS, 6)),
        ],
        compiler_params=pltpu.CompilerParams(
            collective_id=0, has_side_effects=True, vmem_limit_bytes=60 * 1024 * 1024
        ),
        name="stacks",
    )(seg_starts, pair_blocks.T, pair_owner, record, transform_table(), lag_table())
    return pl.pallas_call(
        place_kernel,
        out_shape=jax.ShapeDtypeStruct((TILE, SLOTS, NLAG, BLK), bf16),
        in_specs=[smem, hbm],
        out_specs=hbm,
        scratch_shapes=[
            pltpu.VMEM((SLOTS, TILE, NLAG, BLK), bf16),
            pltpu.SemaphoreType.DMA((SLOTS,)),
            pltpu.SemaphoreType.DMA((SLOTS,)),
        ],
        name="place",
    )(kinds, stacks)


def solution(mesh):
    in_specs = (P("chan", "tm"), P("tm"), P(), P())
    out_specs = P("tm", "chan", None, None)
    body = functools.partial(shards, mesh.shape["chan"], mesh.shape["tm"])
    return jax.shard_map(body, mesh=mesh, in_specs=in_specs, out_specs=out_specs, check_vma=False)
```

```python
import functools
import math

import jax
import jax.numpy as jnp
import numpy as np
from jax import lax
from jax.experimental import pallas as pl
from jax.experimental.pallas import tpu as pltpu
from jax.sharding import PartitionSpec as P

MESH = pl.DeviceIdType.MESH

SEG_LEN = 512
F = 256
LOW_BIN = 1
NLAG = 64
SLOTS = 4
LEVEL = 0.5
EPS = 1e-06

BLK = 128
SEGS_DEV = 16
GROUPS = F // 8
DEPTH = SEGS_DEV * 2 * 8
TILE = 32
HALF = TILE // 2
KINDS = 3
OPP, UP, DOWN, OWN = range(4)


def transform_table():
    sample = np.arange(SEG_LEN)
    bins = np.arange(F) + LOW_BIN
    phase = (bins[:, None] * sample[None, :] % SEG_LEN) * (2.0 * math.pi / SEG_LEN)
    taper = 0.5 - 0.5 * np.cos(sample * (2.0 * math.pi / SEG_LEN))
    table = np.concatenate([taper[None, :] * np.cos(phase), -taper[None, :] * np.sin(phase)], axis=0)
    return jnp.asarray(table.astype(np.float32)).astype(jnp.bfloat16)


def lag_table():
    shifts = np.arange(NLAG) - NLAG // 2
    bins = np.arange(F) + LOW_BIN
    phase = (bins[:, None] * shifts[None, :] % SEG_LEN) * (2.0 * math.pi / SEG_LEN)
    table = np.stack([np.cos(phase), -np.sin(phase)], axis=1).reshape(2 * F, NLAG)
    return jnp.asarray(np.ascontiguousarray(table.T).astype(np.float32)).astype(jnp.bfloat16)


def nt_dot(a, b):
    return lax.dot_general(a, b, (((1,), (1,)), ((), ())), preferred_element_type=jnp.float32)


def stacks_kernel(
    n_chan,
    n_tm,
    scale,
    starts_ref,
    blocks_ref,
    owner_ref,
    record_ref,
    table_hbm,
    lag_ref,
    out_ref,
    kinds_ref,
    table_ref,
    own_ext,
    next_ext,
    turned,
    sides,
    spectra,
    expanded,
    gram,
    part,
    relay_up,
    relay_down,
    from_down,
    from_up,
    shared,
    local_sem,
    table_sem,
    near_send,
    near_recv,
    sum_send,
    sum_recv,
):
    c = lax.axis_index("chan")
    z = lax.axis_index("tm")
    block_len = record_ref.shape[1]
    up = lax.rem(z + 1, n_tm)
    down = lax.rem(z + n_tm - 1, n_tm)
    c_next = lax.rem(c + 1, n_chan)
    c_prev = lax.rem(c + n_chan - 1, n_chan)
    c_next2 = lax.rem(c + 2, n_chan)
    c_prev2 = lax.rem(c + n_chan - 2, n_chan)
    odd = lax.rem(c, 2)
    mate = c + 1 - 2 * odd

    tiles = block_len // 128

    def load_copy(tile):
        columns = pl.ds(pl.multiple_of(tile * 128, 128), 128)
        return pltpu.make_async_copy(record_ref.at[:, columns], own_ext.at[tile], local_sem.at[tile])

    def start_load(tile, carry):
        load_copy(tile).start()
        return carry

    def wait_load(tile, carry):
        load_copy(tile).wait()
        return carry

    lax.fori_loop(0, tiles, start_load, 0)
    table_copy = pltpu.make_async_copy(table_hbm, table_ref, table_sem)
    table_copy.start()

    barrier = pltpu.get_barrier_semaphore()
    for who in ((c, up), (c, down), (c_next2, z), (mate, z), (c_prev, z)):
        pl.semaphore_signal(barrier, inc=1, device_id=who, device_id_type=MESH)
    pl.semaphore_wait(barrier, 5)

    def near(index, src, dst, who):
        return pltpu.make_async_remote_copy(
            src_ref=src,
            dst_ref=dst,
            send_sem=near_send.at[index],
            recv_sem=near_recv.at[index],
            device_id=who,
            device_id_type=MESH,
        )

    main, halo = pl.ds(0, tiles), pl.ds(tiles, SEG_LEN // 128)
    head = own_ext.at[pl.ds(0, SEG_LEN // 128)]
    own_halo = near(0, head, own_ext.at[halo], (c, down))
    next_halo = near(1, own_ext.at[halo], next_ext.at[halo], (c_prev2, z))
    next_main = near(2, own_ext.at[main], next_ext.at[main], (c_prev2, z))
    lax.fori_loop(0, tiles, wait_load, 0)
    own_halo.start()
    next_main.start()

    def to_mate():
        return near(3, spectra.at[2 - 2 * odd], spectra.at[1], (mate, z))

    def forward():
        return near(4, out_ref.at[2], shared, (c_next, z))

    def sum_copies(kind):
        low, high = pl.ds(0, HALF), pl.ds(HALF, HALF)
        routes = (
            (part.at[kind, OPP, low], relay_up.at[kind], up),
            (part.at[kind, OPP, high], relay_down.at[kind], down),
            (part.at[kind, UP, high], from_down.at[kind, high], up),
            (part.at[kind, UP, low], from_down.at[kind, low], up),
            (part.at[kind, DOWN, low], from_up.at[kind, low], down),
            (part.at[kind, DOWN, high], from_up.at[kind, high], down),
        )
        return [
            pltpu.make_async_remote_copy(
                src_ref=src,
                dst_ref=dst,
                send_sem=sum_send.at[kind, index],
                recv_sem=sum_recv.at[kind, index],
                device_id=(c, who),
                device_id_type=MESH,
            )
            for index, (src, dst, who) in enumerate(routes)
        ]

    lane = lax.broadcasted_iota(jnp.int32, (BLK, 128), 1)

    def cut(ext, seg):
        start = lax.rem(starts_ref[seg], block_len)
        first = lax.shift_right_logical(start, 7)
        rest = start - first * 128
        turn = jnp.bitwise_and(128 - rest, 127)
        cols = [
            pltpu.roll(ext[first + j].astype(jnp.float32), turn, 1) for j in range(SEG_LEN // 128 + 1)
        ]
        inside = lane < 128 - rest
        return jnp.concatenate(
            [jnp.where(inside, cols[j], cols[j + 1]) for j in range(SEG_LEN // 128)], axis=1
        ).astype(jnp.bfloat16)

    def whiten(ext, kind, turn_too):
        def step(pair, carry):
            pieces = jnp.concatenate([cut(ext, 2 * pair), cut(ext, 2 * pair + 1)], axis=0)
            both = nt_dot(table_ref[...], pieces)
            for h in range(2):
                real = both[:F, BLK * h : BLK * (h + 1)]
                imag = both[F:, BLK * h : BLK * (h + 1)]
                amplitude = jnp.sqrt(real * real + imag * imag)
                level = jnp.mean(amplitude, axis=0, keepdims=True) + EPS
                inverse = 1.0 / (amplitude + LEVEL * level)
                real = (real * inverse).reshape(GROUPS, 8, BLK)
                imag = (imag * inverse).reshape(GROUPS, 8, BLK)
                rows = pl.ds(pl.multiple_of((2 * pair + h) * 16, 16), 16)
                spectra[kind, :, rows, :] = jnp.concatenate([real, imag], axis=1).astype(jnp.bfloat16)
                if turn_too:
                    turned[:, rows, :] = jnp.concatenate([imag, -real], axis=1).astype(jnp.bfloat16)
            return carry

        lax.fori_loop(0, SEGS_DEV // 2, step, 0, unroll=4)

    def dest(tile):
        ahead = jnp.where(tile == OPP, 2, jnp.where(tile == UP, 1, jnp.where(tile == DOWN, n_tm - 1, 0)))
        return lax.rem(z + ahead, n_tm)

    def transpose():
        eye_row = lax.broadcasted_iota(jnp.int32, (BLK, BLK), 0)
        eye_col = lax.broadcasted_iota(jnp.int32, (BLK, BLK), 1)
        eye = jnp.where(eye_row == eye_col, 1.0, 0.0).astype(jnp.bfloat16)

        def step(group, carry):
            sides[group] = nt_dot(eye, jnp.concatenate([spectra[0, group], turned[group]], axis=0))
            return carry

        lax.fori_loop(0, GROUPS, step, 0, unroll=8)

    def tile_lags(step, kind, tile):
        row = lax.broadcasted_iota(jnp.int32, (DEPTH, BLK), 0)
        low_bins = jnp.where(row % 8 < 4, 1.0, 0.0).astype(jnp.bfloat16)
        high_bins = jnp.where(row % 8 < 4, 0.0, 1.0).astype(jnp.bfloat16)
        first = dest(tile) * TILE
        left_rows = pl.ds(pl.multiple_of(first * 8, TILE * 8), TILE * 8)

        def cross(group, left):
            right = spectra[kind, group]
            weights = jnp.concatenate([right * low_bins, right * high_bins], axis=1)
            both = jnp.dot(left, weights, preferred_element_type=jnp.float32)
            both = jnp.concatenate(
                [both[:, :BLK].reshape(TILE, 8, BLK), both[:, BLK:].reshape(TILE, 8, BLK)], axis=1
            )
            rows = pl.ds(pl.multiple_of(group * 16, 16), 16)
            gram[:, rows, :] = both.astype(jnp.bfloat16)

        @pl.when(step == 0)
        def _():
            direct_row = lax.broadcasted_iota(jnp.int32, (8, DEPTH), 0) % 2 == 0
            row = lax.broadcasted_iota(jnp.int32, (16, DEPTH), 0)
            col = lax.broadcasted_iota(jnp.int32, (16, DEPTH), 1)
            mine = jnp.where(col % 4 == (row // 2) % 4, 1.0, 0.0).astype(jnp.bfloat16)

            def expand_step(group, carry):
                parts = []
                for i in range(0, TILE, 2):
                    two = []
                    for line in (sides[group, pl.ds(first + i, 1), :], sides[group, pl.ds(first + i + 1, 1), :]):
                        two.append(jnp.where(direct_row, line[:, :DEPTH], line[:, DEPTH:]))
                    parts.append(jnp.concatenate(two, axis=0).astype(jnp.bfloat16) * mine)
                left = jnp.concatenate(parts, axis=0)
                expanded[group, left_rows] = left
                cross(group, left)
                return carry

            lax.fori_loop(0, GROUPS, expand_step, 0, unroll=4)

        @pl.when(step > 0)
        def _():
            def gram_step(group, carry):
                cross(group, expanded[group, left_rows])
                return carry

            lax.fori_loop(0, GROUPS, gram_step, 0, unroll=32)

        def lag_step(pair, carry):
            two = jnp.concatenate([gram[2 * pair], gram[2 * pair + 1]], axis=1)
            lags = jnp.dot(lag_ref[...], two, preferred_element_type=jnp.float32) * scale
            part[kind, tile, 2 * pair] = lags[:, :BLK].astype(jnp.bfloat16)
            part[kind, tile, 2 * pair + 1] = lags[:, BLK:].astype(jnp.bfloat16)
            return carry

        copies = sum_copies(kind)

        def half(h, carry):
            lax.fori_loop(0, HALF // 2, lambda i, carry: lag_step(h * (HALF // 2) + i, carry), 0, unroll=8)
            for index, (of_tile, of_half) in ((0, (OPP, 0)), (1, (OPP, 1)), (2, (UP, 1)), (4, (DOWN, 0))):

                @pl.when((tile == of_tile) & (h == of_half))
                def _():
                    copies[index].start()

            return carry

        lax.fori_loop(0, 2, half, 0)

    def relay(kind):
        copies = sum_copies(kind)

        def add(tile, first_row, held):
            def step(i, carry):
                total = part[kind, tile, first_row + i].astype(jnp.float32) + held[kind, i].astype(jnp.float32)
                part[kind, tile, first_row + i] = total.astype(jnp.bfloat16)
                return carry

            lax.fori_loop(0, HALF, step, 0, unroll=4)

        copies[0].wait_recv()
        add(UP, 0, relay_up)
        copies[3].start()
        copies[1].wait_recv()
        add(DOWN, HALF, relay_down)
        copies[5].start()

    def finish(kind):
        copies = sum_copies(kind)
        for index in (2, 3, 4, 5):
            copies[index].wait_recv()
        column = lax.broadcasted_iota(jnp.int32, (NLAG, BLK), 1)

        def step(i, carry):
            total = part[kind, OWN, i].astype(jnp.float32) + (
                from_down[kind, i].astype(jnp.float32) + from_up[kind, i].astype(jnp.float32)
            )
            drop = jnp.where(kind == 0, z * TILE + i, -1)
            out_ref[kind, i] = jnp.where(column == drop, 0.0, total).astype(jnp.bfloat16)
            return carry

        lax.fori_loop(0, TILE, step, 0, unroll=4)

        @pl.when(kind == 2)
        def _():
            forward().start()

    def match(p, slots):
        apart = blocks_ref[1, p] - blocks_ref[0, p]
        kind = jnp.where(blocks_ref[0, p] == c, apart, 3)
        owned = owner_ref[p] - c * SLOTS
        return tuple(held + jnp.where(owned == q, kind + 1, 0) for q, held in enumerate(slots))

    for q, held in enumerate(lax.fori_loop(0, owner_ref.shape[0], match, (0,) * SLOTS)):
        kinds_ref[q] = held

    table_copy.wait()
    own_halo.wait()
    next_halo.start()
    whiten(own_ext, 0, True)

    @pl.when(odd == 1)
    def _():
        to_mate().start()

    transpose()

    def kind_of(step):
        return lax.rem(step * (1 + odd), KINDS)

    def kind_step(step, carry):
        kind = kind_of(step)

        @pl.when(step == 2 - odd)
        def _():
            next_main.wait()
            next_halo.wait()
            whiten(next_ext, 2, False)

            @pl.when(odd == 0)
            def _():
                to_mate().start()

        @pl.when(kind == 1)
        def _():
            to_mate().wait_recv()

        def tile_step(tile, carry):
            tile_lags(step, kind, tile)
            return carry

        lax.fori_loop(0, 4, tile_step, 0)
        relay(kind)

        @pl.when(step > 0)
        def _():
            finish(kind_of(step - 1))

        return carry

    lax.fori_loop(0, KINDS, kind_step, 0)
    finish(kind_of(2))

    to_mate().wait_send()
    forward().wait_send()
    forward().wait_recv()
    for kind in range(KINDS):
        for copy in sum_copies(kind):
            copy.wait_send()
    out_ref[3] = shared[...]


def place_kernel(kinds_ref, stacks_ref, out_ref, zeros, sem):
    zeros[...] = jnp.zeros_like(zeros)

    def put(q, src):
        return pltpu.make_async_copy(src, out_ref.at[:, q], sem.at[q])

    for q in range(SLOTS):
        held = kinds_ref[q]

        @pl.when(held > 0)
        def _():
            put(q, stacks_ref.at[held - 1]).start()

        @pl.when(held == 0)
        def _():
            put(q, zeros).start()

    for q in range(SLOTS):
        put(q, zeros).wait()


def shards(n_chan, n_tm, record, seg_starts, pair_blocks, pair_owner):
    block_len = record.shape[1]
    scale = 2.0 / math.sqrt(SEGS_DEV * n_tm * F)
    bf16 = jnp.bfloat16
    hbm = pl.BlockSpec(memory_space=pl.ANY)
    smem = pl.BlockSpec(memory_space=pltpu.SMEM)
    vmem = pl.BlockSpec(memory_space=pltpu.VMEM)
    stacks, kinds = pl.pallas_call(
        functools.partial(stacks_kernel, n_chan, n_tm, scale),
        out_shape=(
            pltpu.VMEM((4, TILE, NLAG, BLK), bf16),
            jax.ShapeDtypeStruct((SLOTS,), jnp.int32),
        ),
        in_specs=[smem, smem, smem, hbm, hbm, vmem],
        out_specs=(vmem, smem),
        scratch_shapes=[
            pltpu.VMEM((2 * F, SEG_LEN), bf16),
            pltpu.VMEM(((block_len + SEG_LEN) // 128, BLK, 128), bf16),
            pltpu.VMEM(((block_len + SEG_LEN) // 128, BLK, 128), bf16),
            pltpu.VMEM((GROUPS, DEPTH, BLK), bf16),
            pltpu.VMEM((GROUPS, BLK, 2 * DEPTH), jnp.float32),
            pltpu.VMEM((KINDS, GROUPS, DEPTH, BLK), bf16),
            pltpu.VMEM((GROUPS, BLK * 8, DEPTH), bf16),
            pltpu.VMEM((TILE, 2 * F, BLK), bf16),
            pltpu.VMEM((KINDS, 4, TILE, NLAG, BLK), bf16),
            pltpu.VMEM((KINDS, HALF, NLAG, BLK), bf16),
            pltpu.VMEM((KINDS, HALF, NLAG, BLK), bf16),
            pltpu.VMEM((KINDS, TILE, NLAG, BLK), bf16),
            pltpu.VMEM((KINDS, TILE, NLAG, BLK), bf16),
            pltpu.VMEM((TILE, NLAG, BLK), bf16),
            pltpu.SemaphoreType.DMA((block_len // 128,)),
            pltpu.SemaphoreType.DMA,
            pltpu.SemaphoreType.DMA((5,)),
            pltpu.SemaphoreType.DMA((5,)),
            pltpu.SemaphoreType.DMA((KINDS, 6)),
            pltpu.SemaphoreType.DMA((KINDS, 6)),
        ],
        compiler_params=pltpu.CompilerParams(
            collective_id=0, has_side_effects=True, vmem_limit_bytes=60 * 1024 * 1024
        ),
        name="stacks",
    )(seg_starts, pair_blocks.T, pair_owner, record, transform_table(), lag_table())
    return pl.pallas_call(
        place_kernel,
        out_shape=jax.ShapeDtypeStruct((TILE, SLOTS, NLAG, BLK), bf16),
        in_specs=[smem, vmem],
        out_specs=hbm,
        scratch_shapes=[pltpu.VMEM((TILE, NLAG, BLK), bf16), pltpu.SemaphoreType.DMA((SLOTS,))],
        name="place",
    )(kinds, stacks)


def solution(mesh):
    in_specs = (P("chan", "tm"), P("tm"), P(), P())
    out_specs = P("tm", "chan", None, None)
    body = functools.partial(shards, mesh.shape["chan"], mesh.shape["tm"])
    return jax.shard_map(body, mesh=mesh, in_specs=in_specs, out_specs=out_specs, check_vma=False)
```

```python
import functools
import math

import jax
import jax.numpy as jnp
import numpy as np
from jax import lax
from jax.experimental import pallas as pl
from jax.experimental.pallas import tpu as pltpu
from jax.sharding import PartitionSpec as P

MESH = pl.DeviceIdType.MESH

SEG_LEN = 512
F = 256
LOW_BIN = 1
NLAG = 64
SLOTS = 4
LEVEL = 0.5
EPS = 1e-06

BLK = 128
SEGS_DEV = 16
GROUPS = F // 8
DEPTH = SEGS_DEV * 2 * 8
TILE = 32
HALF = TILE // 2
KINDS = 3
OPP, UP, DOWN, OWN = range(4)


def transform_table():
    sample = np.arange(SEG_LEN)
    bins = np.arange(F) + LOW_BIN
    phase = (bins[:, None] * sample[None, :] % SEG_LEN) * (2.0 * math.pi / SEG_LEN)
    taper = 0.5 - 0.5 * np.cos(sample * (2.0 * math.pi / SEG_LEN))
    table = np.concatenate([taper[None, :] * np.cos(phase), -taper[None, :] * np.sin(phase)], axis=0)
    return jnp.asarray(table.astype(np.float32)).astype(jnp.bfloat16)


def lag_table():
    shifts = np.arange(NLAG) - NLAG // 2
    bins = np.arange(F) + LOW_BIN
    phase = (bins[:, None] * shifts[None, :] % SEG_LEN) * (2.0 * math.pi / SEG_LEN)
    table = np.stack([np.cos(phase), -np.sin(phase)], axis=1).reshape(2 * F, NLAG)
    return jnp.asarray(np.ascontiguousarray(table.T).astype(np.float32)).astype(jnp.bfloat16)


def nt_dot(a, b):
    return lax.dot_general(a, b, (((1,), (1,)), ((), ())), preferred_element_type=jnp.float32)


def stacks_kernel(
    n_chan,
    n_tm,
    scale,
    starts_ref,
    blocks_ref,
    owner_ref,
    record_ref,
    table_hbm,
    lag_ref,
    out_ref,
    kinds_ref,
    table_ref,
    own_ext,
    next_ext,
    turned,
    sides,
    spectra,
    expanded,
    gram,
    part,
    relay_up,
    relay_down,
    from_down,
    from_up,
    shared,
    local_sem,
    table_sem,
    near_send,
    near_recv,
    sum_send,
    sum_recv,
):
    c = lax.axis_index("chan")
    z = lax.axis_index("tm")
    block_len = record_ref.shape[1]
    up = lax.rem(z + 1, n_tm)
    down = lax.rem(z + n_tm - 1, n_tm)
    c_next = lax.rem(c + 1, n_chan)
    c_prev = lax.rem(c + n_chan - 1, n_chan)
    c_next2 = lax.rem(c + 2, n_chan)
    c_prev2 = lax.rem(c + n_chan - 2, n_chan)
    odd = lax.rem(c, 2)
    mate = c + 1 - 2 * odd

    tiles = block_len // 128

    def load_copy(tile):
        columns = pl.ds(pl.multiple_of(tile * 128, 128), 128)
        return pltpu.make_async_copy(record_ref.at[:, columns], own_ext.at[tile], local_sem.at[tile])

    def start_load(tile, carry):
        load_copy(tile).start()
        return carry

    def wait_load(tile, carry):
        load_copy(tile).wait()
        return carry

    lax.fori_loop(0, tiles, start_load, 0)
    table_copy = pltpu.make_async_copy(table_hbm, table_ref, table_sem)
    table_copy.start()

    barrier = pltpu.get_barrier_semaphore()
    for who in ((c, up), (c, down), (c_next2, z), (mate, z), (c_prev, z)):
        pl.semaphore_signal(barrier, inc=1, device_id=who, device_id_type=MESH)
    pl.semaphore_wait(barrier, 5)

    def near(index, src, dst, who):
        return pltpu.make_async_remote_copy(
            src_ref=src,
            dst_ref=dst,
            send_sem=near_send.at[index],
            recv_sem=near_recv.at[index],
            device_id=who,
            device_id_type=MESH,
        )

    main, halo = pl.ds(0, tiles), pl.ds(tiles, SEG_LEN // 128)
    head = own_ext.at[pl.ds(0, SEG_LEN // 128)]
    own_halo = near(0, head, own_ext.at[halo], (c, down))
    next_halo = near(1, own_ext.at[halo], next_ext.at[halo], (c_prev2, z))
    next_main = near(2, own_ext.at[main], next_ext.at[main], (c_prev2, z))
    lax.fori_loop(0, tiles, wait_load, 0)
    own_halo.start()
    next_main.start()

    def to_mate():
        return near(3, spectra.at[2 - 2 * odd], spectra.at[1], (mate, z))

    def forward():
        return near(4, out_ref.at[2], shared, (c_next, z))

    def sum_copies(kind):
        low, high = pl.ds(0, HALF), pl.ds(HALF, HALF)
        routes = (
            (part.at[kind, OPP, low], relay_up.at[kind], up),
            (part.at[kind, OPP, high], relay_down.at[kind], down),
            (part.at[kind, UP, high], from_down.at[kind, high], up),
            (part.at[kind, UP, low], from_down.at[kind, low], up),
            (part.at[kind, DOWN, low], from_up.at[kind, low], down),
            (part.at[kind, DOWN, high], from_up.at[kind, high], down),
        )
        return [
            pltpu.make_async_remote_copy(
                src_ref=src,
                dst_ref=dst,
                send_sem=sum_send.at[kind, index],
                recv_sem=sum_recv.at[kind, index],
                device_id=(c, who),
                device_id_type=MESH,
            )
            for index, (src, dst, who) in enumerate(routes)
        ]

    lane = lax.broadcasted_iota(jnp.int32, (BLK, 128), 1)

    def cut(ext, seg):
        start = lax.rem(starts_ref[seg], block_len)
        first = lax.shift_right_logical(start, 7)
        rest = start - first * 128
        turn = jnp.bitwise_and(128 - rest, 127)
        cols = [
            pltpu.roll(ext[first + j].astype(jnp.float32), turn, 1) for j in range(SEG_LEN // 128 + 1)
        ]
        inside = lane < 128 - rest
        return jnp.concatenate(
            [jnp.where(inside, cols[j], cols[j + 1]) for j in range(SEG_LEN // 128)], axis=1
        ).astype(jnp.bfloat16)

    def whiten(ext, kind, turn_too):
        def step(pair, carry):
            pieces = jnp.concatenate([cut(ext, 2 * pair), cut(ext, 2 * pair + 1)], axis=0)
            both = nt_dot(table_ref[...], pieces)
            for h in range(2):
                real = both[:F, BLK * h : BLK * (h + 1)]
                imag = both[F:, BLK * h : BLK * (h + 1)]
                amplitude = jnp.sqrt(real * real + imag * imag)
                level = jnp.mean(amplitude, axis=0, keepdims=True) + EPS
                inverse = 1.0 / (amplitude + LEVEL * level)
                real = (real * inverse).reshape(GROUPS, 8, BLK)
                imag = (imag * inverse).reshape(GROUPS, 8, BLK)
                rows = pl.ds(pl.multiple_of((2 * pair + h) * 16, 16), 16)
                spectra[kind, :, rows, :] = jnp.concatenate([real, imag], axis=1).astype(jnp.bfloat16)
                if turn_too:
                    turned[:, rows, :] = jnp.concatenate([imag, -real], axis=1).astype(jnp.bfloat16)
            return carry

        lax.fori_loop(0, SEGS_DEV // 2, step, 0, unroll=4)

    def dest(tile):
        ahead = jnp.where(tile == OPP, 2, jnp.where(tile == UP, 1, jnp.where(tile == DOWN, n_tm - 1, 0)))
        return lax.rem(z + ahead, n_tm)

    def transpose():
        eye_row = lax.broadcasted_iota(jnp.int32, (BLK, BLK), 0)
        eye_col = lax.broadcasted_iota(jnp.int32, (BLK, BLK), 1)
        eye = jnp.where(eye_row == eye_col, 1.0, 0.0).astype(jnp.bfloat16)

        def step(group, carry):
            sides[group] = nt_dot(eye, jnp.concatenate([spectra[0, group], turned[group]], axis=0))
            return carry

        lax.fori_loop(0, GROUPS, step, 0, unroll=8)

    def tile_lags(step, kind, tile):
        row = lax.broadcasted_iota(jnp.int32, (DEPTH, BLK), 0)
        low_bins = jnp.where(row % 8 < 4, 1.0, 0.0).astype(jnp.bfloat16)
        high_bins = jnp.where(row % 8 < 4, 0.0, 1.0).astype(jnp.bfloat16)
        first = dest(tile) * TILE
        left_rows = pl.ds(pl.multiple_of(first * 8, TILE * 8), TILE * 8)

        def cross(group, left):
            right = spectra[kind, group]
            weights = jnp.concatenate([right * low_bins, right * high_bins], axis=1)
            both = jnp.dot(left, weights, preferred_element_type=jnp.float32)
            both = jnp.concatenate(
                [both[:, :BLK].reshape(TILE, 8, BLK), both[:, BLK:].reshape(TILE, 8, BLK)], axis=1
            )
            rows = pl.ds(pl.multiple_of(group * 16, 16), 16)
            gram[:, rows, :] = both.astype(jnp.bfloat16)

        @pl.when(step == 0)
        def _():
            direct_row = lax.broadcasted_iota(jnp.int32, (8, DEPTH), 0) % 2 == 0
            row = lax.broadcasted_iota(jnp.int32, (16, DEPTH), 0)
            col = lax.broadcasted_iota(jnp.int32, (16, DEPTH), 1)
            mine = jnp.where(col % 4 == (row // 2) % 4, 1.0, 0.0).astype(jnp.bfloat16)

            def expand_step(group, carry):
                parts = []
                for i in range(0, TILE, 2):
                    two = []
                    for line in (sides[group, pl.ds(first + i, 1), :], sides[group, pl.ds(first + i + 1, 1), :]):
                        two.append(jnp.where(direct_row, line[:, :DEPTH], line[:, DEPTH:]))
                    parts.append(jnp.concatenate(two, axis=0).astype(jnp.bfloat16) * mine)
                left = jnp.concatenate(parts, axis=0)
                expanded[group, left_rows] = left
                cross(group, left)
                return carry

            lax.fori_loop(0, GROUPS, expand_step, 0, unroll=4)

        @pl.when(step > 0)
        def _():
            def gram_step(group, carry):
                cross(group, expanded[group, left_rows])
                return carry

            lax.fori_loop(0, GROUPS, gram_step, 0, unroll=32)

        def lag_step(pair, carry):
            two = jnp.concatenate([gram[2 * pair], gram[2 * pair + 1]], axis=1)
            lags = jnp.dot(lag_ref[...], two, preferred_element_type=jnp.float32) * scale
            part[kind, tile, 2 * pair] = lags[:, :BLK].astype(jnp.bfloat16)
            part[kind, tile, 2 * pair + 1] = lags[:, BLK:].astype(jnp.bfloat16)
            return carry

        copies = sum_copies(kind)

        def half(h, carry):
            lax.fori_loop(0, HALF // 2, lambda i, carry: lag_step(h * (HALF // 2) + i, carry), 0, unroll=8)
            for index, (of_tile, of_half) in ((0, (OPP, 0)), (1, (OPP, 1)), (2, (UP, 1)), (4, (DOWN, 0))):

                @pl.when((tile == of_tile) & (h == of_half))
                def _():
                    copies[index].start()

            return carry

        lax.fori_loop(0, 2, half, 0)

    def relay(kind):
        copies = sum_copies(kind)

        def add(tile, first_row, held):
            def step(i, carry):
                total = part[kind, tile, first_row + i].astype(jnp.float32) + held[kind, i].astype(jnp.float32)
                part[kind, tile, first_row + i] = total.astype(jnp.bfloat16)
                return carry

            lax.fori_loop(0, HALF, step, 0, unroll=4)

        copies[0].wait_recv()
        add(UP, 0, relay_up)
        copies[3].start()
        copies[1].wait_recv()
        add(DOWN, HALF, relay_down)
        copies[5].start()

    def finish(kind):
        copies = sum_copies(kind)
        for index in (2, 3, 4, 5):
            copies[index].wait_recv()
        column = lax.broadcasted_iota(jnp.int32, (NLAG, BLK), 1)

        def step(i, carry):
            total = part[kind, OWN, i].astype(jnp.float32) + (
                from_down[kind, i].astype(jnp.float32) + from_up[kind, i].astype(jnp.float32)
            )
            drop = jnp.where(kind == 0, z * TILE + i, -1)
            out_ref[kind, i] = jnp.where(column == drop, 0.0, total).astype(jnp.bfloat16)
            return carry

        lax.fori_loop(0, TILE, step, 0, unroll=4)

        @pl.when(kind == 2)
        def _():
            forward().start()

    def match(p, slots):
        apart = blocks_ref[1, p] - blocks_ref[0, p]
        kind = jnp.where(blocks_ref[0, p] == c, apart, 3)
        owned = owner_ref[p] - c * SLOTS
        return tuple(held + jnp.where(owned == q, kind + 1, 0) for q, held in enumerate(slots))

    for q, held in enumerate(lax.fori_loop(0, owner_ref.shape[0], match, (0,) * SLOTS)):
        kinds_ref[q] = jnp.minimum(held, KINDS + 1)

    table_copy.wait()
    own_halo.wait()
    next_halo.start()
    whiten(own_ext, 0, True)

    @pl.when(odd == 1)
    def _():
        to_mate().start()

    transpose()

    def kind_of(step):
        return lax.rem(step * (1 + odd), KINDS)

    def kind_step(step, carry):
        kind = kind_of(step)

        @pl.when(step == 2 - odd)
        def _():
            next_main.wait()
            next_halo.wait()
            whiten(next_ext, 2, False)

            @pl.when(odd == 0)
            def _():
                to_mate().start()

        @pl.when(kind == 1)
        def _():
            to_mate().wait_recv()

        def tile_step(tile, carry):
            tile_lags(step, kind, tile)
            return carry

        lax.fori_loop(0, 4, tile_step, 0)
        relay(kind)

        @pl.when(step > 0)
        def _():
            finish(kind_of(step - 1))

        return carry

    lax.fori_loop(0, KINDS, kind_step, 0)
    finish(kind_of(2))

    to_mate().wait_send()
    forward().wait_send()
    forward().wait_recv()
    for kind in range(KINDS):
        for copy in sum_copies(kind):
            copy.wait_send()
    out_ref[3] = shared[...]


def place_kernel(kinds_ref, stacks_ref, out_ref, zeros, sem):
    zeros[...] = jnp.zeros_like(zeros)

    def put(q, src):
        return pltpu.make_async_copy(src, out_ref.at[:, q], sem.at[q])

    for q in range(SLOTS):
        held = kinds_ref[q]

        @pl.when(held > 0)
        def _():
            put(q, stacks_ref.at[held - 1]).start()

        @pl.when(held == 0)
        def _():
            put(q, zeros).start()

    for q in range(SLOTS):
        put(q, zeros).wait()


def shards(n_chan, n_tm, record, seg_starts, pair_blocks, pair_owner):
    block_len = record.shape[1]
    scale = 2.0 / math.sqrt(SEGS_DEV * n_tm * F)
    bf16 = jnp.bfloat16
    hbm = pl.BlockSpec(memory_space=pl.ANY)
    smem = pl.BlockSpec(memory_space=pltpu.SMEM)
    vmem = pl.BlockSpec(memory_space=pltpu.VMEM)
    stacks, kinds = pl.pallas_call(
        functools.partial(stacks_kernel, n_chan, n_tm, scale),
        out_shape=(
            pltpu.VMEM((4, TILE, NLAG, BLK), bf16),
            pltpu.SMEM((SLOTS,), jnp.int32),
        ),
        in_specs=[smem, smem, smem, hbm, hbm, vmem],
        out_specs=(vmem, smem),
        scratch_shapes=[
            pltpu.VMEM((2 * F, SEG_LEN), bf16),
            pltpu.VMEM(((block_len + SEG_LEN) // 128, BLK, 128), bf16),
            pltpu.VMEM(((block_len + SEG_LEN) // 128, BLK, 128), bf16),
            pltpu.VMEM((GROUPS, DEPTH, BLK), bf16),
            pltpu.VMEM((GROUPS, BLK, 2 * DEPTH), jnp.float32),
            pltpu.VMEM((KINDS, GROUPS, DEPTH, BLK), bf16),
            pltpu.VMEM((GROUPS, BLK * 8, DEPTH), bf16),
            pltpu.VMEM((TILE, 2 * F, BLK), bf16),
            pltpu.VMEM((KINDS, 4, TILE, NLAG, BLK), bf16),
            pltpu.VMEM((KINDS, HALF, NLAG, BLK), bf16),
            pltpu.VMEM((KINDS, HALF, NLAG, BLK), bf16),
            pltpu.VMEM((KINDS, TILE, NLAG, BLK), bf16),
            pltpu.VMEM((KINDS, TILE, NLAG, BLK), bf16),
            pltpu.VMEM((TILE, NLAG, BLK), bf16),
            pltpu.SemaphoreType.DMA((block_len // 128,)),
            pltpu.SemaphoreType.DMA,
            pltpu.SemaphoreType.DMA((5,)),
            pltpu.SemaphoreType.DMA((5,)),
            pltpu.SemaphoreType.DMA((KINDS, 6)),
            pltpu.SemaphoreType.DMA((KINDS, 6)),
        ],
        compiler_params=pltpu.CompilerParams(
            collective_id=0, has_side_effects=True, vmem_limit_bytes=60 * 1024 * 1024
        ),
        name="stacks",
    )(seg_starts, pair_blocks.T, pair_owner, record, transform_table(), lag_table())
    return pl.pallas_call(
        place_kernel,
        out_shape=jax.ShapeDtypeStruct((TILE, SLOTS, NLAG, BLK), bf16),
        in_specs=[smem, vmem],
        out_specs=hbm,
        scratch_shapes=[pltpu.VMEM((TILE, NLAG, BLK), bf16), pltpu.SemaphoreType.DMA((SLOTS,))],
        compiler_params=pltpu.CompilerParams(vmem_limit_bytes=4 * 1024 * 1024),
        name="place",
    )(kinds, pltpu.with_memory_space_constraint(stacks, pltpu.VMEM))


def solution(mesh):
    in_specs = (P("chan", "tm"), P("tm"), P(), P())
    out_specs = P("tm", "chan", None, None)
    body = functools.partial(shards, mesh.shape["chan"], mesh.shape["tm"])
    return jax.shard_map(body, mesh=mesh, in_specs=in_specs, out_specs=out_specs, check_vma=False)
```

```python
import functools
import math

import jax
import jax.numpy as jnp
import numpy as np
from jax import lax
from jax.experimental import pallas as pl
from jax.experimental.pallas import tpu as pltpu
from jax.sharding import PartitionSpec as P

MESH = pl.DeviceIdType.MESH

SEG_LEN = 512
F = 256
LOW_BIN = 1
NLAG = 64
SLOTS = 4
LEVEL = 0.5
EPS = 1e-06

BLK = 128
SEGS_DEV = 16
GROUPS = F // 8
DEPTH = SEGS_DEV * 2 * 8
TILE = 32
HALF = TILE // 2
KINDS = 3
OPP, UP, DOWN, OWN = range(4)
MIRROR = NLAG // 2


def transform_table():
    sample = np.arange(SEG_LEN)
    bins = np.arange(F) + LOW_BIN
    phase = (bins[:, None] * sample[None, :] % SEG_LEN) * (2.0 * math.pi / SEG_LEN)
    taper = 0.5 - 0.5 * np.cos(sample * (2.0 * math.pi / SEG_LEN))
    table = np.concatenate([taper[None, :] * np.cos(phase), -taper[None, :] * np.sin(phase)], axis=0)
    return jnp.asarray(table.astype(np.float32)).astype(jnp.bfloat16)


def lag_table(shifts):
    bins = np.arange(F) + LOW_BIN
    phase = (bins[:, None] * shifts[None, :] % SEG_LEN) * (2.0 * math.pi / SEG_LEN)
    table = np.stack([np.cos(phase), -np.sin(phase)], axis=1).reshape(2 * F, len(shifts))
    return jnp.asarray(np.ascontiguousarray(table.T).astype(np.float32)).astype(jnp.bfloat16)


def nt_dot(a, b):
    return lax.dot_general(a, b, (((1,), (1,)), ((), ())), preferred_element_type=jnp.float32)


def stacks_kernel(
    n_chan,
    n_tm,
    scale,
    starts_ref,
    blocks_ref,
    owner_ref,
    record_ref,
    table_hbm,
    lag_ref,
    self_lag_ref,
    out_ref,
    kinds_ref,
    table_ref,
    own_ext,
    next_ext,
    turned,
    sides,
    spectra,
    expanded,
    gram,
    part,
    relay_up,
    relay_down,
    from_down,
    from_up,
    self_part,
    self_relay_up,
    self_relay_down,
    self_from_down,
    self_from_up,
    zero_lag,
    folded,
    unfolded,
    mirror_out,
    mirror_in,
    shared,
    local_sem,
    table_sem,
    near_send,
    near_recv,
    sum_send,
    sum_recv,
    mirror_send,
    mirror_recv,
):
    c = lax.axis_index("chan")
    z = lax.axis_index("tm")
    block_len = record_ref.shape[1]
    up = lax.rem(z + 1, n_tm)
    down = lax.rem(z + n_tm - 1, n_tm)
    opposite = lax.rem(z + 2, n_tm)
    c_next = lax.rem(c + 1, n_chan)
    c_prev = lax.rem(c + n_chan - 1, n_chan)
    c_next2 = lax.rem(c + 2, n_chan)
    c_prev2 = lax.rem(c + n_chan - 2, n_chan)
    odd = lax.rem(c, 2)
    mate = c + 1 - 2 * odd

    tiles = block_len // 128

    def load_copy(tile):
        columns = pl.ds(pl.multiple_of(tile * 128, 128), 128)
        return pltpu.make_async_copy(record_ref.at[:, columns], own_ext.at[tile], local_sem.at[tile])

    def start_load(tile, carry):
        load_copy(tile).start()
        return carry

    def wait_load(tile, carry):
        load_copy(tile).wait()
        return carry

    lax.fori_loop(0, tiles, start_load, 0)
    table_copy = pltpu.make_async_copy(table_hbm, table_ref, table_sem)
    table_copy.start()

    barrier = pltpu.get_barrier_semaphore()
    for who in ((c, up), (c, down), (c, opposite), (c_next2, z), (mate, z), (c_prev, z)):
        pl.semaphore_signal(barrier, inc=1, device_id=who, device_id_type=MESH)
    pl.semaphore_wait(barrier, 6)

    def near(index, src, dst, who):
        return pltpu.make_async_remote_copy(
            src_ref=src,
            dst_ref=dst,
            send_sem=near_send.at[index],
            recv_sem=near_recv.at[index],
            device_id=who,
            device_id_type=MESH,
        )

    main, halo = pl.ds(0, tiles), pl.ds(tiles, SEG_LEN // 128)
    head = own_ext.at[pl.ds(0, SEG_LEN // 128)]
    own_halo = near(0, head, own_ext.at[halo], (c, down))
    next_halo = near(1, own_ext.at[halo], next_ext.at[halo], (c_prev2, z))
    next_main = near(2, own_ext.at[main], next_ext.at[main], (c_prev2, z))
    lax.fori_loop(0, tiles, wait_load, 0)
    own_halo.start()
    next_main.start()

    def to_mate():
        return near(3, spectra.at[2 - 2 * odd], spectra.at[1], (mate, z))

    def forward():
        return near(4, out_ref.at[2], shared, (c_next, z))

    def ring_copies(kind, piece, up_slot, down_slot, below, above):
        routes = (
            (piece(OPP, 0), up_slot, up),
            (piece(OPP, 1), down_slot, down),
            (piece(UP, 1), below(1), up),
            (piece(UP, 0), below(0), up),
            (piece(DOWN, 0), above(0), down),
            (piece(DOWN, 1), above(1), down),
        )
        return [
            pltpu.make_async_remote_copy(
                src_ref=src,
                dst_ref=dst,
                send_sem=sum_send.at[kind, index],
                recv_sem=sum_recv.at[kind, index],
                device_id=(c, who),
                device_id_type=MESH,
            )
            for index, (src, dst, who) in enumerate(routes)
        ]

    def sum_copies(kind):
        def rows(half):
            return pl.ds(half * HALF, HALF)

        k = kind - 1
        return ring_copies(
            kind,
            lambda tile, half: part.at[k, tile, rows(half)],
            relay_up.at[k],
            relay_down.at[k],
            lambda half: from_down.at[k, rows(half)],
            lambda half: from_up.at[k, rows(half)],
        )

    def self_copies():
        return ring_copies(
            0,
            lambda tile, half: self_part.at[tile, half],
            self_relay_up,
            self_relay_down,
            lambda half: self_from_down.at[half],
            lambda half: self_from_up.at[half],
        )

    def mirror_copies():
        return [
            pltpu.make_async_remote_copy(
                src_ref=mirror_out.at[who],
                dst_ref=mirror_in.at[index],
                send_sem=mirror_send.at[index],
                recv_sem=mirror_recv.at[index],
                device_id=(c, who),
                device_id_type=MESH,
            )
            for index, who in enumerate((opposite, up, down))
        ]

    lane = lax.broadcasted_iota(jnp.int32, (BLK, 128), 1)

    def cut(ext, seg):
        start = lax.rem(starts_ref[seg], block_len)
        first = lax.shift_right_logical(start, 7)
        rest = start - first * 128
        turn = jnp.bitwise_and(128 - rest, 127)
        cols = [
            pltpu.roll(ext[first + j].astype(jnp.float32), turn, 1) for j in range(SEG_LEN // 128 + 1)
        ]
        inside = lane < 128 - rest
        return jnp.concatenate(
            [jnp.where(inside, cols[j], cols[j + 1]) for j in range(SEG_LEN // 128)], axis=1
        ).astype(jnp.bfloat16)

    def whiten(ext, kind, turn_too):
        def step(pair, carry):
            pieces = jnp.concatenate([cut(ext, 2 * pair), cut(ext, 2 * pair + 1)], axis=0)
            both = nt_dot(table_ref[...], pieces)
            for h in range(2):
                real = both[:F, BLK * h : BLK * (h + 1)]
                imag = both[F:, BLK * h : BLK * (h + 1)]
                amplitude = jnp.sqrt(real * real + imag * imag)
                level = jnp.mean(amplitude, axis=0, keepdims=True) + EPS
                inverse = 1.0 / (amplitude + LEVEL * level)
                real = (real * inverse).reshape(GROUPS, 8, BLK)
                imag = (imag * inverse).reshape(GROUPS, 8, BLK)
                rows = pl.ds(pl.multiple_of((2 * pair + h) * 16, 16), 16)
                spectra[kind, :, rows, :] = jnp.concatenate([real, imag], axis=1).astype(jnp.bfloat16)
                if turn_too:
                    turned[:, rows, :] = jnp.concatenate([imag, -real], axis=1).astype(jnp.bfloat16)
            return carry

        lax.fori_loop(0, SEGS_DEV // 2, step, 0, unroll=4)

    def dest(tile):
        ahead = jnp.where(tile == OPP, 2, jnp.where(tile == UP, 1, jnp.where(tile == DOWN, n_tm - 1, 0)))
        return lax.rem(z + ahead, n_tm)

    def transpose():
        eye_row = lax.broadcasted_iota(jnp.int32, (BLK, BLK), 0)
        eye_col = lax.broadcasted_iota(jnp.int32, (BLK, BLK), 1)
        eye = jnp.where(eye_row == eye_col, 1.0, 0.0).astype(jnp.bfloat16)

        def step(group, carry):
            sides[group] = nt_dot(eye, jnp.concatenate([spectra[0, group], turned[group]], axis=0))
            return carry

        lax.fori_loop(0, GROUPS, step, 0, unroll=8)

    def cross(kind, group, left):
        row = lax.broadcasted_iota(jnp.int32, (DEPTH, BLK), 0)
        low_bins = jnp.where(row % 8 < 4, 1.0, 0.0).astype(jnp.bfloat16)
        high_bins = jnp.where(row % 8 < 4, 0.0, 1.0).astype(jnp.bfloat16)
        right = spectra[kind, group]
        weights = jnp.concatenate([right * low_bins, right * high_bins], axis=1)
        both = jnp.dot(left, weights, preferred_element_type=jnp.float32)
        both = jnp.concatenate(
            [both[:, :BLK].reshape(TILE, 8, BLK), both[:, BLK:].reshape(TILE, 8, BLK)], axis=1
        )
        rows = pl.ds(pl.multiple_of(group * 16, 16), 16)
        gram[:, rows, :] = both.astype(jnp.bfloat16)

    def left_rows(tile):
        return pl.ds(pl.multiple_of(dest(tile) * TILE * 8, TILE * 8), TILE * 8)

    def pair_lags(table, pair):
        two = jnp.concatenate([gram[2 * pair], gram[2 * pair + 1]], axis=1)
        lags = jnp.dot(table, two, preferred_element_type=jnp.float32) * scale
        return lags[:, :BLK], lags[:, BLK:]

    def start_ready(copies, tile, h):
        for index, (of_tile, of_half) in ((0, (OPP, 0)), (1, (OPP, 1)), (2, (UP, 1)), (4, (DOWN, 0))):

            @pl.when((tile == of_tile) & (h == of_half))
            def _():
                copies[index].start()

    def self_tile(tile):
        direct_row = lax.broadcasted_iota(jnp.int32, (8, DEPTH), 0) % 2 == 0
        row = lax.broadcasted_iota(jnp.int32, (16, DEPTH), 0)
        col = lax.broadcasted_iota(jnp.int32, (16, DEPTH), 1)
        mine = jnp.where(col % 4 == (row // 2) % 4, 1.0, 0.0).astype(jnp.bfloat16)
        first = dest(tile) * TILE

        def expand_step(group, carry):
            parts = []
            for i in range(0, TILE, 2):
                two = []
                for line in (sides[group, pl.ds(first + i, 1), :], sides[group, pl.ds(first + i + 1, 1), :]):
                    two.append(jnp.where(direct_row, line[:, :DEPTH], line[:, DEPTH:]))
                parts.append(jnp.concatenate(two, axis=0).astype(jnp.bfloat16) * mine)
            left = jnp.concatenate(parts, axis=0)
            expanded[group, left_rows(tile)] = left
            cross(0, group, left)
            return carry

        lax.fori_loop(0, GROUPS, expand_step, 0, unroll=4)
        copies = self_copies()

        def half(h, carry):
            def lag_step(i, carry):
                for k, lags in enumerate(pair_lags(self_lag_ref[...], h * (HALF // 2) + i)):
                    self_part[tile, h, 2 * i + k] = lags[:MIRROR].astype(jnp.bfloat16)
                    zero_lag[pl.ds(2 * i + k, 1), :] = lags[MIRROR : MIRROR + 1]
                return carry

            lax.fori_loop(0, HALF // 2, lag_step, 0, unroll=8)
            self_part[tile, h, HALF] = zero_lag[...].astype(jnp.bfloat16)
            start_ready(copies, tile, h)
            return carry

        lax.fori_loop(0, 2, half, 0)

    def kind_tile(kind, tile):
        def gram_step(group, carry):
            cross(kind, group, expanded[group, left_rows(tile)])
            return carry

        lax.fori_loop(0, GROUPS, gram_step, 0, unroll=32)
        copies = sum_copies(kind)

        def half(h, carry):
            def lag_step(i, carry):
                pair = h * (HALF // 2) + i
                for k, lags in enumerate(pair_lags(lag_ref[...], pair)):
                    part[kind - 1, tile, 2 * pair + k] = lags.astype(jnp.bfloat16)
                return carry

            lax.fori_loop(0, HALF // 2, lag_step, 0, unroll=8)
            start_ready(copies, tile, h)
            return carry

        lax.fori_loop(0, 2, half, 0)

    def add(count, total, rows, held, held_rows):
        def step(i, carry):
            here = rows(i)
            total[here] = (total[here].astype(jnp.float32) + held[held_rows(i)].astype(jnp.float32)).astype(jnp.bfloat16)
            return carry

        lax.fori_loop(0, count, step, 0, unroll=4 if count % 4 == 0 else 1)

    def relay(kind):
        copies = sum_copies(kind)
        k = kind - 1
        copies[0].wait_recv()
        add(HALF, part, lambda i: (k, UP, i), relay_up, lambda i: (k, i))
        copies[3].start()
        copies[1].wait_recv()
        add(HALF, part, lambda i: (k, DOWN, HALF + i), relay_down, lambda i: (k, i))
        copies[5].start()

    def self_relay():
        copies = self_copies()
        copies[0].wait_recv()
        add(HALF + 1, self_part, lambda i: (UP, 0, i), self_relay_up, lambda i: i)
        copies[3].start()
        copies[1].wait_recv()
        add(HALF + 1, self_part, lambda i: (DOWN, 1, i), self_relay_down, lambda i: i)
        copies[5].start()

    def three(own, below, above):
        return own.astype(jnp.float32) + (below.astype(jnp.float32) + above.astype(jnp.float32))

    def finish(kind):
        copies = sum_copies(kind)
        for index in (2, 3, 4, 5):
            copies[index].wait_recv()
        k = kind - 1

        def step(i, carry):
            out_ref[kind, i] = three(part[k, OWN, i], from_down[k, i], from_up[k, i]).astype(jnp.bfloat16)
            return carry

        lax.fori_loop(0, TILE, step, 0, unroll=4)

        @pl.when(kind == 2)
        def _():
            forward().start()

    def self_finish():
        copies = self_copies()
        for index in (2, 3, 4, 5):
            copies[index].wait_recv()
        column = lax.broadcasted_iota(jnp.int32, (MIRROR, BLK), 1)
        row = lax.broadcasted_iota(jnp.int32, (MIRROR, BLK), 0)

        def half(h, carry):
            zero_lag[...] = three(self_part[OWN, h, HALF], self_from_down[h, HALF], self_from_up[h, HALF])

            def step(i, carry):
                total = three(self_part[OWN, h, i], self_from_down[h, i], self_from_up[h, i])
                mine = h * HALF + i
                total = jnp.where(column == z * TILE + mine, 0.0, total)
                folded[pl.ds(pl.multiple_of(mine * MIRROR, MIRROR), MIRROR), :] = total
                zero = jnp.where(column == z * TILE + mine, 0.0, zero_lag[pl.ds(i, 1), :])
                later = jnp.where(row == 0, zero, pltpu.roll(total, 1, 0))
                out_ref[0, mine, MIRROR:] = later.astype(jnp.bfloat16)
                return carry

            lax.fori_loop(0, HALF, step, 0, unroll=2)
            return carry

        lax.fori_loop(0, 2, half, 0)
        eye_row = lax.broadcasted_iota(jnp.int32, (BLK, BLK), 0)
        eye_col = lax.broadcasted_iota(jnp.int32, (BLK, BLK), 1)
        eye = jnp.where(eye_row == eye_col, 1.0, 0.0).astype(jnp.bfloat16)
        for quad in range(MIRROR // 4):
            lines = [folded[pl.ds(4 * quad + k, TILE, stride=MIRROR), :] for k in range(4)]
            turned_over = nt_dot(eye, jnp.concatenate(lines, axis=0).astype(jnp.bfloat16))
            mirror_out[:, quad] = turned_over.reshape(n_tm, TILE, BLK).astype(jnp.bfloat16)
        for copy in mirror_copies():
            copy.start()
        mirror_in[OWN] = mirror_out[z]

    def self_unfold():
        for copy in mirror_copies():
            copy.wait_recv()
        place = lax.broadcasted_iota(jnp.int32, (TILE, BLK), 1) // TILE
        sources = [opposite, down, up, z]
        for quad in range(MIRROR // 4):
            held = [mirror_in[slot, quad].astype(jnp.float32) for slot in range(n_tm)]
            for k in range(4):
                line = jnp.zeros((TILE, BLK), jnp.float32)
                for slot, source in enumerate(sources):
                    moved = pltpu.roll(held[slot], lax.rem(source + 4 - k, 4) * TILE, 1)
                    line = jnp.where(place == source, moved, line)
                unfolded[pl.ds(MIRROR - 1 - 4 * quad - k, TILE, stride=MIRROR), :] = line

        def step(i, carry):
            lines = unfolded[pl.ds(pl.multiple_of(i * MIRROR, MIRROR), MIRROR), :]
            out_ref[0, i, :MIRROR] = lines.astype(jnp.bfloat16)
            return carry

        lax.fori_loop(0, TILE, step, 0, unroll=4)

    def match(p, slots):
        apart = blocks_ref[1, p] - blocks_ref[0, p]
        kind = jnp.where(blocks_ref[0, p] == c, apart, 3)
        owned = owner_ref[p] - c * SLOTS
        return tuple(held + jnp.where(owned == q, kind + 1, 0) for q, held in enumerate(slots))

    for q, held in enumerate(lax.fori_loop(0, owner_ref.shape[0], match, (0,) * SLOTS)):
        kinds_ref[q] = jnp.minimum(held, KINDS + 1)

    table_copy.wait()
    own_halo.wait()
    next_halo.start()
    whiten(own_ext, 0, True)

    @pl.when(odd == 1)
    def _():
        to_mate().start()

    transpose()

    def kind_of(step):
        return lax.rem(step * (1 + odd), KINDS)

    def self_step(tile, carry):
        self_tile(tile)
        return carry

    zero_lag[...] = jnp.zeros_like(zero_lag)
    lax.fori_loop(0, 4, self_step, 0)
    self_relay()

    def kind_step(step, carry):
        kind = kind_of(step)

        @pl.when(step == 2 - odd)
        def _():
            next_main.wait()
            next_halo.wait()
            whiten(next_ext, 2, False)

            @pl.when(odd == 0)
            def _():
                to_mate().start()

        @pl.when(kind == 1)
        def _():
            to_mate().wait_recv()

        def tile_step(tile, carry):
            kind_tile(kind, tile)
            return carry

        lax.fori_loop(0, 4, tile_step, 0)
        relay(kind)

        @pl.when(step == 1)
        def _():
            self_finish()

        @pl.when(step == 2)
        def _():
            finish(kind_of(1))
            self_unfold()

        return carry

    lax.fori_loop(1, KINDS, kind_step, 0)
    finish(kind_of(2))

    to_mate().wait_send()
    forward().wait_send()
    forward().wait_recv()
    for copy in self_copies() + sum_copies(1) + sum_copies(2) + mirror_copies():
        copy.wait_send()
    out_ref[3] = shared[...]


def place_kernel(kinds_ref, stacks_ref, out_ref, zeros, sem):
    zeros[...] = jnp.zeros_like(zeros)

    def put(q, src):
        return pltpu.make_async_copy(src, out_ref.at[:, q], sem.at[q])

    for q in range(SLOTS):
        held = kinds_ref[q]

        @pl.when(held > 0)
        def _():
            put(q, stacks_ref.at[held - 1]).start()

        @pl.when(held == 0)
        def _():
            put(q, zeros).start()

    for q in range(SLOTS):
        put(q, zeros).wait()


def shards(n_chan, n_tm, record, seg_starts, pair_blocks, pair_owner):
    block_len = record.shape[1]
    scale = 2.0 / math.sqrt(SEGS_DEV * n_tm * F)
    bf16 = jnp.bfloat16
    shifts = np.arange(NLAG) - NLAG // 2
    self_lags = lag_table(np.concatenate([np.arange(1, MIRROR + 1), np.zeros(16, np.int64)]))
    hbm = pl.BlockSpec(memory_space=pl.ANY)
    smem = pl.BlockSpec(memory_space=pltpu.SMEM)
    vmem = pl.BlockSpec(memory_space=pltpu.VMEM)
    stacks, kinds = pl.pallas_call(
        functools.partial(stacks_kernel, n_chan, n_tm, scale),
        out_shape=(
            pltpu.VMEM((4, TILE, NLAG, BLK), bf16),
            pltpu.SMEM((SLOTS,), jnp.int32),
        ),
        in_specs=[smem, smem, smem, hbm, hbm, vmem, vmem],
        out_specs=(vmem, smem),
        scratch_shapes=[
            pltpu.VMEM((2 * F, SEG_LEN), bf16),
            pltpu.VMEM(((block_len + SEG_LEN) // 128, BLK, 128), bf16),
            pltpu.VMEM(((block_len + SEG_LEN) // 128, BLK, 128), bf16),
            pltpu.VMEM((GROUPS, DEPTH, BLK), bf16),
            pltpu.VMEM((GROUPS, BLK, 2 * DEPTH), jnp.float32),
            pltpu.VMEM((KINDS, GROUPS, DEPTH, BLK), bf16),
            pltpu.VMEM((GROUPS, BLK * 8, DEPTH), bf16),
            pltpu.VMEM((TILE, 2 * F, BLK), bf16),
            pltpu.VMEM((KINDS - 1, 4, TILE, NLAG, BLK), bf16),
            pltpu.VMEM((KINDS - 1, HALF, NLAG, BLK), bf16),
            pltpu.VMEM((KINDS - 1, HALF, NLAG, BLK), bf16),
            pltpu.VMEM((KINDS - 1, TILE, NLAG, BLK), bf16),
            pltpu.VMEM((KINDS - 1, TILE, NLAG, BLK), bf16),
            pltpu.VMEM((4, 2, HALF + 1, MIRROR, BLK), bf16),
            pltpu.VMEM((HALF + 1, MIRROR, BLK), bf16),
            pltpu.VMEM((HALF + 1, MIRROR, BLK), bf16),
            pltpu.VMEM((2, HALF + 1, MIRROR, BLK), bf16),
            pltpu.VMEM((2, HALF + 1, MIRROR, BLK), bf16),
            pltpu.VMEM((MIRROR, BLK), jnp.float32),
            pltpu.VMEM((TILE * MIRROR, BLK), jnp.float32),
            pltpu.VMEM((TILE * MIRROR, BLK), jnp.float32),
            pltpu.VMEM((n_tm, MIRROR // 4, TILE, BLK), bf16),
            pltpu.VMEM((n_tm, MIRROR // 4, TILE, BLK), bf16),
            pltpu.VMEM((TILE, NLAG, BLK), bf16),
            pltpu.SemaphoreType.DMA((block_len // 128,)),
            pltpu.SemaphoreType.DMA,
            pltpu.SemaphoreType.DMA((5,)),
            pltpu.SemaphoreType.DMA((5,)),
            pltpu.SemaphoreType.DMA((KINDS, 6)),
            pltpu.SemaphoreType.DMA((KINDS, 6)),
            pltpu.SemaphoreType.DMA((3,)),
            pltpu.SemaphoreType.DMA((3,)),
        ],
        compiler_params=pltpu.CompilerParams(
            collective_id=0, has_side_effects=True, vmem_limit_bytes=60 * 1024 * 1024
        ),
        name="stacks",
    )(seg_starts, pair_blocks.T, pair_owner, record, transform_table(), lag_table(shifts), self_lags)
    return pl.pallas_call(
        place_kernel,
        out_shape=jax.ShapeDtypeStruct((TILE, SLOTS, NLAG, BLK), bf16),
        in_specs=[smem, vmem],
        out_specs=hbm,
        scratch_shapes=[pltpu.VMEM((TILE, NLAG, BLK), bf16), pltpu.SemaphoreType.DMA((SLOTS,))],
        compiler_params=pltpu.CompilerParams(vmem_limit_bytes=4 * 1024 * 1024),
        name="place",
    )(kinds, pltpu.with_memory_space_constraint(stacks, pltpu.VMEM))


def solution(mesh):
    in_specs = (P("chan", "tm"), P("tm"), P(), P())
    out_specs = P("tm", "chan", None, None)
    body = functools.partial(shards, mesh.shape["chan"], mesh.shape["tm"])
    return jax.shard_map(body, mesh=mesh, in_specs=in_specs, out_specs=out_specs, check_vma=False)
```

```python
import functools
import math

import jax
import jax.numpy as jnp
import numpy as np
from jax import lax
from jax.experimental import pallas as pl
from jax.experimental.pallas import tpu as pltpu
from jax.sharding import PartitionSpec as P

MESH = pl.DeviceIdType.MESH

SEG_LEN = 512
F = 256
LOW_BIN = 1
NLAG = 64
SLOTS = 4
LEVEL = 0.5
EPS = 1e-06

BLK = 128
SEGS_DEV = 16
GROUPS = F // 8
DEPTH = SEGS_DEV * 2 * 8
TILE = 32
HALF = TILE // 2
KINDS = 3
OPP, UP, DOWN, OWN = range(4)
MIRROR = NLAG // 2


def transform_table():
    sample = np.arange(SEG_LEN)
    bins = np.arange(F) + LOW_BIN
    phase = (bins[:, None] * sample[None, :] % SEG_LEN) * (2.0 * math.pi / SEG_LEN)
    taper = 0.5 - 0.5 * np.cos(sample * (2.0 * math.pi / SEG_LEN))
    table = np.concatenate([taper[None, :] * np.cos(phase), -taper[None, :] * np.sin(phase)], axis=0)
    return jnp.asarray(table.astype(np.float32)).astype(jnp.bfloat16)


def lag_table(shifts):
    bins = np.arange(F) + LOW_BIN
    phase = (bins[:, None] * shifts[None, :] % SEG_LEN) * (2.0 * math.pi / SEG_LEN)
    table = np.stack([np.cos(phase), -np.sin(phase)], axis=1).reshape(2 * F, len(shifts))
    return jnp.asarray(np.ascontiguousarray(table.T).astype(np.float32)).astype(jnp.bfloat16)


def nt_dot(a, b):
    return lax.dot_general(a, b, (((1,), (1,)), ((), ())), preferred_element_type=jnp.float32)


def stacks_kernel(
    n_chan,
    n_tm,
    scale,
    starts_ref,
    blocks_ref,
    owner_ref,
    record_ref,
    table_hbm,
    lag_ref,
    self_lag_ref,
    out_ref,
    kinds_ref,
    table_ref,
    own_ext,
    next_ext,
    turned,
    sides,
    spectra,
    expanded,
    gram,
    part,
    relay_up,
    relay_down,
    from_down,
    from_up,
    self_part,
    self_relay_up,
    self_relay_down,
    self_from_down,
    self_from_up,
    zero_lag,
    folded,
    unfolded,
    mirror_out,
    mirror_in,
    shared,
    local_sem,
    table_sem,
    near_send,
    near_recv,
    sum_send,
    sum_recv,
    mirror_send,
    mirror_recv,
):
    c = lax.axis_index("chan")
    z = lax.axis_index("tm")
    block_len = record_ref.shape[1]
    up = lax.rem(z + 1, n_tm)
    down = lax.rem(z + n_tm - 1, n_tm)
    opposite = lax.rem(z + 2, n_tm)
    c_next = lax.rem(c + 1, n_chan)
    c_prev = lax.rem(c + n_chan - 1, n_chan)
    c_next2 = lax.rem(c + 2, n_chan)
    c_prev2 = lax.rem(c + n_chan - 2, n_chan)
    odd = lax.rem(c, 2)
    mate = c + 1 - 2 * odd

    tiles = block_len // 128

    def load_copy(tile):
        columns = pl.ds(pl.multiple_of(tile * 128, 128), 128)
        return pltpu.make_async_copy(record_ref.at[:, columns], own_ext.at[tile], local_sem.at[tile])

    def start_load(tile, carry):
        load_copy(tile).start()
        return carry

    def wait_load(tile, carry):
        load_copy(tile).wait()
        return carry

    lax.fori_loop(0, tiles, start_load, 0)
    table_copy = pltpu.make_async_copy(table_hbm, table_ref, table_sem)
    table_copy.start()

    barrier = pltpu.get_barrier_semaphore()
    for who in ((c, up), (c, down), (c, opposite), (c_next2, z), (mate, z), (c_prev, z)):
        pl.semaphore_signal(barrier, inc=1, device_id=who, device_id_type=MESH)
    pl.semaphore_wait(barrier, 6)

    def near(index, src, dst, who):
        return pltpu.make_async_remote_copy(
            src_ref=src,
            dst_ref=dst,
            send_sem=near_send.at[index],
            recv_sem=near_recv.at[index],
            device_id=who,
            device_id_type=MESH,
        )

    main, halo = pl.ds(0, tiles), pl.ds(tiles, SEG_LEN // 128)
    head = own_ext.at[pl.ds(0, SEG_LEN // 128)]
    own_halo = near(0, head, own_ext.at[halo], (c, down))
    next_halo = near(1, own_ext.at[halo], next_ext.at[halo], (c_prev2, z))
    next_main = near(2, own_ext.at[main], next_ext.at[main], (c_prev2, z))
    lax.fori_loop(0, tiles, wait_load, 0)
    own_halo.start()
    next_main.start()

    def to_mate():
        return near(3, spectra.at[2 - 2 * odd], spectra.at[1], (mate, z))

    def forward():
        return near(4, out_ref.at[2], shared, (c_next, z))

    def ring_copies(kind, piece, up_slot, down_slot, below, above):
        routes = (
            (piece(OPP, 0), up_slot, up),
            (piece(OPP, 1), down_slot, down),
            (piece(UP, 1), below(1), up),
            (piece(UP, 0), below(0), up),
            (piece(DOWN, 0), above(0), down),
            (piece(DOWN, 1), above(1), down),
        )
        return [
            pltpu.make_async_remote_copy(
                src_ref=src,
                dst_ref=dst,
                send_sem=sum_send.at[kind, index],
                recv_sem=sum_recv.at[kind, index],
                device_id=(c, who),
                device_id_type=MESH,
            )
            for index, (src, dst, who) in enumerate(routes)
        ]

    def sum_copies(kind):
        def rows(half):
            return pl.ds(half * HALF, HALF)

        k = kind - 1
        return ring_copies(
            kind,
            lambda tile, half: part.at[k, tile, rows(half)],
            relay_up.at[k],
            relay_down.at[k],
            lambda half: from_down.at[k, rows(half)],
            lambda half: from_up.at[k, rows(half)],
        )

    def self_copies():
        return ring_copies(
            0,
            lambda tile, half: self_part.at[tile, half],
            self_relay_up,
            self_relay_down,
            lambda half: self_from_down.at[half],
            lambda half: self_from_up.at[half],
        )

    def mirror_copies():
        return [
            pltpu.make_async_remote_copy(
                src_ref=mirror_out.at[who],
                dst_ref=mirror_in.at[index],
                send_sem=mirror_send.at[index],
                recv_sem=mirror_recv.at[index],
                device_id=(c, who),
                device_id_type=MESH,
            )
            for index, who in enumerate((opposite, up, down))
        ]

    lane = lax.broadcasted_iota(jnp.int32, (BLK, 128), 1)

    def cut(ext, seg):
        start = lax.rem(starts_ref[seg], block_len)
        first = lax.shift_right_logical(start, 7)
        rest = start - first * 128
        turn = jnp.bitwise_and(128 - rest, 127)
        cols = [
            pltpu.roll(ext[first + j].astype(jnp.float32), turn, 1) for j in range(SEG_LEN // 128 + 1)
        ]
        inside = lane < 128 - rest
        return jnp.concatenate(
            [jnp.where(inside, cols[j], cols[j + 1]) for j in range(SEG_LEN // 128)], axis=1
        ).astype(jnp.bfloat16)

    def whiten(ext, kind, turn_too):
        def step(pair, carry):
            pieces = jnp.concatenate([cut(ext, 2 * pair), cut(ext, 2 * pair + 1)], axis=0)
            both = nt_dot(table_ref[...], pieces)
            for h in range(2):
                real = both[:F, BLK * h : BLK * (h + 1)]
                imag = both[F:, BLK * h : BLK * (h + 1)]
                amplitude = jnp.sqrt(real * real + imag * imag)
                level = jnp.mean(amplitude, axis=0, keepdims=True) + EPS
                inverse = 1.0 / (amplitude + LEVEL * level)
                real = (real * inverse).reshape(GROUPS, 8, BLK)
                imag = (imag * inverse).reshape(GROUPS, 8, BLK)
                rows = pl.ds(pl.multiple_of((2 * pair + h) * 16, 16), 16)
                spectra[kind, :, rows, :] = jnp.concatenate([real, imag], axis=1).astype(jnp.bfloat16)
                if turn_too:
                    turned[:, rows, :] = jnp.concatenate([imag, -real], axis=1).astype(jnp.bfloat16)
            return carry

        lax.fori_loop(0, SEGS_DEV // 2, step, 0, unroll=4)

    def dest(tile):
        ahead = jnp.where(tile == OPP, 2, jnp.where(tile == UP, 1, jnp.where(tile == DOWN, n_tm - 1, 0)))
        return lax.rem(z + ahead, n_tm)

    def transpose():
        eye_row = lax.broadcasted_iota(jnp.int32, (BLK, BLK), 0)
        eye_col = lax.broadcasted_iota(jnp.int32, (BLK, BLK), 1)
        eye = jnp.where(eye_row == eye_col, 1.0, 0.0).astype(jnp.bfloat16)

        def step(group, carry):
            sides[group] = nt_dot(eye, jnp.concatenate([spectra[0, group], turned[group]], axis=0))
            return carry

        lax.fori_loop(0, GROUPS, step, 0, unroll=8)

    def cross(kind, group, left):
        row = lax.broadcasted_iota(jnp.int32, (DEPTH, BLK), 0)
        low_bins = jnp.where(row % 8 < 4, 1.0, 0.0).astype(jnp.bfloat16)
        high_bins = jnp.where(row % 8 < 4, 0.0, 1.0).astype(jnp.bfloat16)
        right = spectra[kind, group]
        weights = jnp.concatenate([right * low_bins, right * high_bins], axis=1)
        both = jnp.dot(left, weights, preferred_element_type=jnp.float32)
        both = jnp.concatenate(
            [both[:, :BLK].reshape(TILE, 8, BLK), both[:, BLK:].reshape(TILE, 8, BLK)], axis=1
        )
        rows = pl.ds(pl.multiple_of(group * 16, 16), 16)
        gram[:, rows, :] = both.astype(jnp.bfloat16)

    def left_rows(tile):
        return pl.ds(pl.multiple_of(dest(tile) * TILE * 8, TILE * 8), TILE * 8)

    def pair_lags(table, pair):
        two = jnp.concatenate([gram[2 * pair], gram[2 * pair + 1]], axis=1)
        lags = jnp.dot(table, two, preferred_element_type=jnp.float32) * scale
        return lags[:, :BLK], lags[:, BLK:]

    def start_ready(copies, tile, h):
        for index, (of_tile, of_half) in ((0, (OPP, 0)), (1, (OPP, 1)), (2, (UP, 1)), (4, (DOWN, 0))):

            @pl.when((tile == of_tile) & (h == of_half))
            def _():
                copies[index].start()

    def first_gram(kind, tile):
        direct_row = lax.broadcasted_iota(jnp.int32, (8, DEPTH), 0) % 2 == 0
        row = lax.broadcasted_iota(jnp.int32, (16, DEPTH), 0)
        col = lax.broadcasted_iota(jnp.int32, (16, DEPTH), 1)
        mine = jnp.where(col % 4 == (row // 2) % 4, 1.0, 0.0).astype(jnp.bfloat16)
        first = dest(tile) * TILE

        def expand_step(group, carry):
            parts = []
            for i in range(0, TILE, 2):
                two = []
                for line in (sides[group, pl.ds(first + i, 1), :], sides[group, pl.ds(first + i + 1, 1), :]):
                    two.append(jnp.where(direct_row, line[:, :DEPTH], line[:, DEPTH:]))
                parts.append(jnp.concatenate(two, axis=0).astype(jnp.bfloat16) * mine)
            left = jnp.concatenate(parts, axis=0)
            expanded[group, left_rows(tile)] = left
            cross(kind, group, left)
            return carry

        lax.fori_loop(0, GROUPS, expand_step, 0, unroll=4)

    def later_gram(kind, tile):
        def gram_step(group, carry):
            cross(kind, group, expanded[group, left_rows(tile)])
            return carry

        lax.fori_loop(0, GROUPS, gram_step, 0, unroll=32)

    def self_lags(tile):
        copies = self_copies()

        def half(h, carry):
            def lag_step(i, carry):
                for k, lags in enumerate(pair_lags(self_lag_ref[...], h * (HALF // 2) + i)):
                    self_part[tile, h, 2 * i + k] = lags[:MIRROR].astype(jnp.bfloat16)
                    zero_lag[pl.ds(2 * i + k, 1), :] = lags[MIRROR : MIRROR + 1]
                return carry

            lax.fori_loop(0, HALF // 2, lag_step, 0, unroll=8)
            self_part[tile, h, HALF] = zero_lag[...].astype(jnp.bfloat16)
            start_ready(copies, tile, h)
            return carry

        lax.fori_loop(0, 2, half, 0)

    def kind_lags(kind, tile):
        copies = sum_copies(kind)

        def half(h, carry):
            def lag_step(i, carry):
                pair = h * (HALF // 2) + i
                for k, lags in enumerate(pair_lags(lag_ref[...], pair)):
                    part[kind - 1, tile, 2 * pair + k] = lags.astype(jnp.bfloat16)
                return carry

            lax.fori_loop(0, HALF // 2, lag_step, 0, unroll=8)
            start_ready(copies, tile, h)
            return carry

        lax.fori_loop(0, 2, half, 0)

    def add(count, total, rows, held, held_rows):
        def step(i, carry):
            here = rows(i)
            total[here] = (total[here].astype(jnp.float32) + held[held_rows(i)].astype(jnp.float32)).astype(jnp.bfloat16)
            return carry

        lax.fori_loop(0, count, step, 0, unroll=4 if count % 4 == 0 else 1)

    def relay(kind):
        copies = sum_copies(kind)
        k = kind - 1
        copies[0].wait_recv()
        add(HALF, part, lambda i: (k, UP, i), relay_up, lambda i: (k, i))
        copies[3].start()
        copies[1].wait_recv()
        add(HALF, part, lambda i: (k, DOWN, HALF + i), relay_down, lambda i: (k, i))
        copies[5].start()

    def self_relay():
        copies = self_copies()
        copies[0].wait_recv()
        add(HALF + 1, self_part, lambda i: (UP, 0, i), self_relay_up, lambda i: i)
        copies[3].start()
        copies[1].wait_recv()
        add(HALF + 1, self_part, lambda i: (DOWN, 1, i), self_relay_down, lambda i: i)
        copies[5].start()

    def three(own, below, above):
        return own.astype(jnp.float32) + (below.astype(jnp.float32) + above.astype(jnp.float32))

    def finish(kind):
        copies = sum_copies(kind)
        for index in (2, 3, 4, 5):
            copies[index].wait_recv()
        k = kind - 1

        def step(i, carry):
            out_ref[kind, i] = three(part[k, OWN, i], from_down[k, i], from_up[k, i]).astype(jnp.bfloat16)
            return carry

        lax.fori_loop(0, TILE, step, 0, unroll=4)

        @pl.when(kind == 2)
        def _():
            forward().start()

    def self_finish():
        copies = self_copies()
        for index in (2, 3, 4, 5):
            copies[index].wait_recv()
        column = lax.broadcasted_iota(jnp.int32, (MIRROR, BLK), 1)
        row = lax.broadcasted_iota(jnp.int32, (MIRROR, BLK), 0)

        def half(h, carry):
            zero_lag[...] = three(self_part[OWN, h, HALF], self_from_down[h, HALF], self_from_up[h, HALF])

            def step(i, carry):
                total = three(self_part[OWN, h, i], self_from_down[h, i], self_from_up[h, i])
                mine = h * HALF + i
                total = jnp.where(column == z * TILE + mine, 0.0, total)
                folded[pl.ds(pl.multiple_of(mine * MIRROR, MIRROR), MIRROR), :] = total
                zero = jnp.where(column == z * TILE + mine, 0.0, zero_lag[pl.ds(i, 1), :])
                later = jnp.where(row == 0, zero, pltpu.roll(total, 1, 0))
                out_ref[0, mine, MIRROR:] = later.astype(jnp.bfloat16)
                return carry

            lax.fori_loop(0, HALF, step, 0, unroll=2)
            return carry

        lax.fori_loop(0, 2, half, 0)
        eye_row = lax.broadcasted_iota(jnp.int32, (BLK, BLK), 0)
        eye_col = lax.broadcasted_iota(jnp.int32, (BLK, BLK), 1)
        eye = jnp.where(eye_row == eye_col, 1.0, 0.0).astype(jnp.bfloat16)
        for quad in range(MIRROR // 4):
            lines = [folded[pl.ds(4 * quad + k, TILE, stride=MIRROR), :] for k in range(4)]
            turned_over = nt_dot(eye, jnp.concatenate(lines, axis=0).astype(jnp.bfloat16))
            mirror_out[:, quad] = turned_over.reshape(n_tm, TILE, BLK).astype(jnp.bfloat16)
        for copy in mirror_copies():
            copy.start()
        mirror_in[OWN] = mirror_out[z]

    def self_unfold():
        for copy in mirror_copies():
            copy.wait_recv()
        place = lax.broadcasted_iota(jnp.int32, (TILE, BLK), 1) // TILE
        sources = [opposite, down, up, z]
        for quad in range(MIRROR // 4):
            held = [mirror_in[slot, quad].astype(jnp.float32) for slot in range(n_tm)]
            for k in range(4):
                line = jnp.zeros((TILE, BLK), jnp.float32)
                for slot, source in enumerate(sources):
                    moved = pltpu.roll(held[slot], lax.rem(source + 4 - k, 4) * TILE, 1)
                    line = jnp.where(place == source, moved, line)
                unfolded[pl.ds(MIRROR - 1 - 4 * quad - k, TILE, stride=MIRROR), :] = line

        def step(i, carry):
            lines = unfolded[pl.ds(pl.multiple_of(i * MIRROR, MIRROR), MIRROR), :]
            out_ref[0, i, :MIRROR] = lines.astype(jnp.bfloat16)
            return carry

        lax.fori_loop(0, TILE, step, 0, unroll=4)

    def match(p, slots):
        apart = blocks_ref[1, p] - blocks_ref[0, p]
        kind = jnp.where(blocks_ref[0, p] == c, apart, 3)
        owned = owner_ref[p] - c * SLOTS
        return tuple(held + jnp.where(owned == q, kind + 1, 0) for q, held in enumerate(slots))

    for q, held in enumerate(lax.fori_loop(0, owner_ref.shape[0], match, (0,) * SLOTS)):
        kinds_ref[q] = jnp.minimum(held, KINDS + 1)

    table_copy.wait()
    own_halo.wait()
    next_halo.start()
    whiten(own_ext, 0, True)

    @pl.when(odd == 1)
    def _():
        to_mate().start()

    transpose()

    def kind_of(step):
        return lax.rem(2 * step + 1 - odd, KINDS)

    def finish_any(kind):
        @pl.when(kind == 0)
        def _():
            self_finish()

        @pl.when(kind > 0)
        def _():
            finish(kind)

    zero_lag[...] = jnp.zeros_like(zero_lag)

    def kind_step(step, carry):
        kind = kind_of(step)

        @pl.when(step == 2 - odd)
        def _():
            next_main.wait()
            next_halo.wait()
            whiten(next_ext, 2, False)

            @pl.when(odd == 0)
            def _():
                to_mate().start()

        @pl.when(kind == 1)
        def _():
            to_mate().wait_recv()

        def tile_step(tile, carry):
            @pl.when(step == 0)
            def _():
                first_gram(kind, tile)

            @pl.when(step > 0)
            def _():
                later_gram(kind, tile)

            @pl.when(kind == 0)
            def _():
                self_lags(tile)

            @pl.when(kind > 0)
            def _():
                kind_lags(kind, tile)

            return carry

        lax.fori_loop(0, 4, tile_step, 0)

        @pl.when(kind == 0)
        def _():
            self_relay()

        @pl.when(kind > 0)
        def _():
            relay(kind)

        @pl.when(step > 0)
        def _():
            finish_any(kind_of(step - 1))

        return carry

    lax.fori_loop(0, KINDS, kind_step, 0)
    self_unfold()
    finish(kind_of(2))

    to_mate().wait_send()
    forward().wait_send()
    forward().wait_recv()
    for copy in self_copies() + sum_copies(1) + sum_copies(2) + mirror_copies():
        copy.wait_send()
    out_ref[3] = shared[...]


def place_kernel(kinds_ref, stacks_ref, out_ref, zeros, sem):
    zeros[...] = jnp.zeros_like(zeros)

    def put(q, src):
        return pltpu.make_async_copy(src, out_ref.at[:, q], sem.at[q])

    for q in range(SLOTS):
        held = kinds_ref[q]

        @pl.when(held > 0)
        def _():
            put(q, stacks_ref.at[held - 1]).start()

        @pl.when(held == 0)
        def _():
            put(q, zeros).start()

    for q in range(SLOTS):
        put(q, zeros).wait()


def shards(n_chan, n_tm, record, seg_starts, pair_blocks, pair_owner):
    block_len = record.shape[1]
    scale = 2.0 / math.sqrt(SEGS_DEV * n_tm * F)
    bf16 = jnp.bfloat16
    shifts = np.arange(NLAG) - NLAG // 2
    self_lags = lag_table(np.concatenate([np.arange(1, MIRROR + 1), np.zeros(16, np.int64)]))
    hbm = pl.BlockSpec(memory_space=pl.ANY)
    smem = pl.BlockSpec(memory_space=pltpu.SMEM)
    vmem = pl.BlockSpec(memory_space=pltpu.VMEM)
    stacks, kinds = pl.pallas_call(
        functools.partial(stacks_kernel, n_chan, n_tm, scale),
        out_shape=(
            pltpu.VMEM((4, TILE, NLAG, BLK), bf16),
            pltpu.SMEM((SLOTS,), jnp.int32),
        ),
        in_specs=[smem, smem, smem, hbm, hbm, vmem, vmem],
        out_specs=(vmem, smem),
        scratch_shapes=[
            pltpu.VMEM((2 * F, SEG_LEN), bf16),
            pltpu.VMEM(((block_len + SEG_LEN) // 128, BLK, 128), bf16),
            pltpu.VMEM(((block_len + SEG_LEN) // 128, BLK, 128), bf16),
            pltpu.VMEM((GROUPS, DEPTH, BLK), bf16),
            pltpu.VMEM((GROUPS, BLK, 2 * DEPTH), jnp.float32),
            pltpu.VMEM((KINDS, GROUPS, DEPTH, BLK), bf16),
            pltpu.VMEM((GROUPS, BLK * 8, DEPTH), bf16),
            pltpu.VMEM((TILE, 2 * F, BLK), bf16),
            pltpu.VMEM((KINDS - 1, 4, TILE, NLAG, BLK), bf16),
            pltpu.VMEM((KINDS - 1, HALF, NLAG, BLK), bf16),
            pltpu.VMEM((KINDS - 1, HALF, NLAG, BLK), bf16),
            pltpu.VMEM((KINDS - 1, TILE, NLAG, BLK), bf16),
            pltpu.VMEM((KINDS - 1, TILE, NLAG, BLK), bf16),
            pltpu.VMEM((4, 2, HALF + 1, MIRROR, BLK), bf16),
            pltpu.VMEM((HALF + 1, MIRROR, BLK), bf16),
            pltpu.VMEM((HALF + 1, MIRROR, BLK), bf16),
            pltpu.VMEM((2, HALF + 1, MIRROR, BLK), bf16),
            pltpu.VMEM((2, HALF + 1, MIRROR, BLK), bf16),
            pltpu.VMEM((MIRROR, BLK), jnp.float32),
            pltpu.VMEM((TILE * MIRROR, BLK), jnp.float32),
            pltpu.VMEM((TILE * MIRROR, BLK), jnp.float32),
            pltpu.VMEM((n_tm, MIRROR // 4, TILE, BLK), bf16),
            pltpu.VMEM((n_tm, MIRROR // 4, TILE, BLK), bf16),
            pltpu.VMEM((TILE, NLAG, BLK), bf16),
            pltpu.SemaphoreType.DMA((block_len // 128,)),
            pltpu.SemaphoreType.DMA,
            pltpu.SemaphoreType.DMA((5,)),
            pltpu.SemaphoreType.DMA((5,)),
            pltpu.SemaphoreType.DMA((KINDS, 6)),
            pltpu.SemaphoreType.DMA((KINDS, 6)),
            pltpu.SemaphoreType.DMA((3,)),
            pltpu.SemaphoreType.DMA((3,)),
        ],
        compiler_params=pltpu.CompilerParams(
            collective_id=0, has_side_effects=True, vmem_limit_bytes=60 * 1024 * 1024
        ),
        name="stacks",
    )(seg_starts, pair_blocks.T, pair_owner, record, transform_table(), lag_table(shifts), self_lags)
    return pl.pallas_call(
        place_kernel,
        out_shape=jax.ShapeDtypeStruct((TILE, SLOTS, NLAG, BLK), bf16),
        in_specs=[smem, vmem],
        out_specs=hbm,
        scratch_shapes=[pltpu.VMEM((TILE, NLAG, BLK), bf16), pltpu.SemaphoreType.DMA((SLOTS,))],
        compiler_params=pltpu.CompilerParams(vmem_limit_bytes=4 * 1024 * 1024),
        name="place",
    )(kinds, pltpu.with_memory_space_constraint(stacks, pltpu.VMEM))


def solution(mesh):
    in_specs = (P("chan", "tm"), P("tm"), P(), P())
    out_specs = P("tm", "chan", None, None)
    body = functools.partial(shards, mesh.shape["chan"], mesh.shape["tm"])
    return jax.shard_map(body, mesh=mesh, in_specs=in_specs, out_specs=out_specs, check_vma=False)
```

```python
import functools
import math

import jax
import jax.numpy as jnp
import numpy as np
from jax import lax
from jax.experimental import pallas as pl
from jax.experimental.pallas import tpu as pltpu
from jax.sharding import PartitionSpec as P

MESH = pl.DeviceIdType.MESH

SEG_LEN = 512
F = 256
LOW_BIN = 1
NLAG = 64
SLOTS = 4
LEVEL = 0.5
EPS = 1e-06

BLK = 128
SEGS_DEV = 16
GROUPS = F // 8
DEPTH = SEGS_DEV * 2 * 8
TILE = 32
HALF = TILE // 2
KINDS = 3
OPP, UP, DOWN, OWN = range(4)
MIRROR = NLAG // 2


def transform_table():
    sample = np.arange(SEG_LEN)
    bins = np.arange(F) + LOW_BIN
    phase = (bins[:, None] * sample[None, :] % SEG_LEN) * (2.0 * math.pi / SEG_LEN)
    taper = 0.5 - 0.5 * np.cos(sample * (2.0 * math.pi / SEG_LEN))
    table = np.concatenate([taper[None, :] * np.cos(phase), -taper[None, :] * np.sin(phase)], axis=0)
    return jnp.asarray(table.astype(np.float32)).astype(jnp.bfloat16)


def lag_table(shifts):
    bins = np.arange(F) + LOW_BIN
    phase = (bins[:, None] * shifts[None, :] % SEG_LEN) * (2.0 * math.pi / SEG_LEN)
    table = np.stack([np.cos(phase), -np.sin(phase)], axis=1).reshape(2 * F, len(shifts))
    return jnp.asarray(np.ascontiguousarray(table.T).astype(np.float32)).astype(jnp.bfloat16)


def nt_dot(a, b):
    return lax.dot_general(a, b, (((1,), (1,)), ((), ())), preferred_element_type=jnp.float32)


def stacks_kernel(
    n_chan,
    n_tm,
    scale,
    starts_ref,
    blocks_ref,
    owner_ref,
    record_ref,
    table_hbm,
    lag_ref,
    self_lag_ref,
    out_ref,
    kinds_ref,
    table_ref,
    own_ext,
    next_ext,
    turned,
    sides,
    spectra,
    expanded,
    gram,
    part,
    relay_up,
    relay_down,
    from_down,
    from_up,
    self_part,
    self_relay_up,
    self_relay_down,
    self_from_down,
    self_from_up,
    zero_lag,
    folded,
    unfolded,
    mirror_out,
    mirror_in,
    shared,
    local_sem,
    table_sem,
    near_send,
    near_recv,
    sum_send,
    sum_recv,
    mirror_send,
    mirror_recv,
):
    c = lax.axis_index("chan")
    z = lax.axis_index("tm")
    block_len = record_ref.shape[1]
    up = lax.rem(z + 1, n_tm)
    down = lax.rem(z + n_tm - 1, n_tm)
    opposite = lax.rem(z + 2, n_tm)
    c_next = lax.rem(c + 1, n_chan)
    c_prev = lax.rem(c + n_chan - 1, n_chan)
    c_next2 = lax.rem(c + 2, n_chan)
    c_prev2 = lax.rem(c + n_chan - 2, n_chan)
    odd = lax.rem(c, 2)
    mate = c + 1 - 2 * odd

    tiles = block_len // 128

    def load_copy(tile):
        columns = pl.ds(pl.multiple_of(tile * 128, 128), 128)
        return pltpu.make_async_copy(record_ref.at[:, columns], own_ext.at[tile], local_sem.at[tile])

    def start_load(tile, carry):
        load_copy(tile).start()
        return carry

    def wait_load(tile, carry):
        load_copy(tile).wait()
        return carry

    lax.fori_loop(0, tiles, start_load, 0)
    table_copy = pltpu.make_async_copy(table_hbm, table_ref, table_sem)
    table_copy.start()

    barrier = pltpu.get_barrier_semaphore()
    for who in ((c, up), (c, down), (c, opposite), (c_next2, z), (mate, z), (c_prev, z)):
        pl.semaphore_signal(barrier, inc=1, device_id=who, device_id_type=MESH)
    pl.semaphore_wait(barrier, 6)

    def near(index, src, dst, who):
        return pltpu.make_async_remote_copy(
            src_ref=src,
            dst_ref=dst,
            send_sem=near_send.at[index],
            recv_sem=near_recv.at[index],
            device_id=who,
            device_id_type=MESH,
        )

    main, halo = pl.ds(0, tiles), pl.ds(tiles, SEG_LEN // 128)
    head = own_ext.at[pl.ds(0, SEG_LEN // 128)]
    own_halo = near(0, head, own_ext.at[halo], (c, down))
    next_halo = near(1, own_ext.at[halo], next_ext.at[halo], (c_prev2, z))
    next_main = near(2, own_ext.at[main], next_ext.at[main], (c_prev2, z))
    lax.fori_loop(0, tiles, wait_load, 0)
    own_halo.start()
    next_main.start()

    def to_mate():
        return near(3, spectra.at[2 - 2 * odd], spectra.at[1], (mate, z))

    def forward():
        return near(4, out_ref.at[2], shared, (c_next, z))

    def ring_copies(kind, piece, up_slot, down_slot, below, above):
        routes = (
            (piece(OPP, 0), up_slot, up),
            (piece(OPP, 1), down_slot, down),
            (piece(UP, 1), below(1), up),
            (piece(UP, 0), below(0), up),
            (piece(DOWN, 0), above(0), down),
            (piece(DOWN, 1), above(1), down),
        )
        return [
            pltpu.make_async_remote_copy(
                src_ref=src,
                dst_ref=dst,
                send_sem=sum_send.at[kind, index],
                recv_sem=sum_recv.at[kind, index],
                device_id=(c, who),
                device_id_type=MESH,
            )
            for index, (src, dst, who) in enumerate(routes)
        ]

    def sum_copies(kind):
        def rows(half):
            return pl.ds(half * HALF, HALF)

        k = kind - 1
        return ring_copies(
            kind,
            lambda tile, half: part.at[k, tile, rows(half)],
            relay_up.at[k],
            relay_down.at[k],
            lambda half: from_down.at[k, rows(half)],
            lambda half: from_up.at[k, rows(half)],
        )

    def self_copies():
        return ring_copies(
            0,
            lambda tile, half: self_part.at[tile, half],
            self_relay_up,
            self_relay_down,
            lambda half: self_from_down.at[half],
            lambda half: self_from_up.at[half],
        )

    def mirror_copies():
        return [
            pltpu.make_async_remote_copy(
                src_ref=mirror_out.at[who],
                dst_ref=mirror_in.at[index],
                send_sem=mirror_send.at[index],
                recv_sem=mirror_recv.at[index],
                device_id=(c, who),
                device_id_type=MESH,
            )
            for index, who in enumerate((opposite, up, down))
        ]

    lane = lax.broadcasted_iota(jnp.int32, (BLK, 128), 1)

    def cut(ext, seg):
        start = lax.rem(starts_ref[seg], block_len)
        first = lax.shift_right_logical(start, 7)
        rest = start - first * 128
        turn = jnp.bitwise_and(128 - rest, 127)
        cols = [
            pltpu.roll(ext[first + j].astype(jnp.float32), turn, 1) for j in range(SEG_LEN // 128 + 1)
        ]
        inside = lane < 128 - rest
        return jnp.concatenate(
            [jnp.where(inside, cols[j], cols[j + 1]) for j in range(SEG_LEN // 128)], axis=1
        ).astype(jnp.bfloat16)

    def whiten(ext, kind, turn_too):
        def step(pair, carry):
            pieces = jnp.concatenate([cut(ext, 2 * pair), cut(ext, 2 * pair + 1)], axis=0)
            both = nt_dot(table_ref[...], pieces)
            for h in range(2):
                real = both[:F, BLK * h : BLK * (h + 1)]
                imag = both[F:, BLK * h : BLK * (h + 1)]
                amplitude = jnp.sqrt(real * real + imag * imag)
                level = jnp.mean(amplitude, axis=0, keepdims=True) + EPS
                inverse = 1.0 / (amplitude + LEVEL * level)
                real = (real * inverse).reshape(GROUPS, 8, BLK)
                imag = (imag * inverse).reshape(GROUPS, 8, BLK)
                rows = pl.ds(pl.multiple_of((2 * pair + h) * 16, 16), 16)
                spectra[kind, :, rows, :] = jnp.concatenate([real, imag], axis=1).astype(jnp.bfloat16)
                if turn_too:
                    turned[:, rows, :] = jnp.concatenate([imag, -real], axis=1).astype(jnp.bfloat16)
            return carry

        lax.fori_loop(0, SEGS_DEV // 2, step, 0, unroll=8)

    def dest(tile):
        ahead = jnp.where(tile == OPP, 2, jnp.where(tile == UP, 1, jnp.where(tile == DOWN, n_tm - 1, 0)))
        return lax.rem(z + ahead, n_tm)

    def transpose():
        eye_row = lax.broadcasted_iota(jnp.int32, (BLK, BLK), 0)
        eye_col = lax.broadcasted_iota(jnp.int32, (BLK, BLK), 1)
        eye = jnp.where(eye_row == eye_col, 1.0, 0.0).astype(jnp.bfloat16)

        def step(group, carry):
            sides[group] = nt_dot(eye, jnp.concatenate([spectra[0, group], turned[group]], axis=0))
            return carry

        lax.fori_loop(0, GROUPS, step, 0, unroll=16)

    def cross(kind, group, left):
        row = lax.broadcasted_iota(jnp.int32, (DEPTH, BLK), 0)
        low_bins = jnp.where(row % 8 < 4, 1.0, 0.0).astype(jnp.bfloat16)
        high_bins = jnp.where(row % 8 < 4, 0.0, 1.0).astype(jnp.bfloat16)
        right = spectra[kind, group]
        weights = jnp.concatenate([right * low_bins, right * high_bins], axis=1)
        both = jnp.dot(left, weights, preferred_element_type=jnp.float32)
        both = jnp.concatenate(
            [both[:, :BLK].reshape(TILE, 8, BLK), both[:, BLK:].reshape(TILE, 8, BLK)], axis=1
        )
        rows = pl.ds(pl.multiple_of(group * 16, 16), 16)
        gram[:, rows, :] = both.astype(jnp.bfloat16)

    def left_rows(tile):
        return pl.ds(pl.multiple_of(dest(tile) * TILE * 8, TILE * 8), TILE * 8)

    def pair_lags(table, pair):
        two = jnp.concatenate([gram[2 * pair], gram[2 * pair + 1]], axis=1)
        lags = jnp.dot(table, two, preferred_element_type=jnp.float32) * scale
        return lags[:, :BLK], lags[:, BLK:]

    def start_ready(copies, tile, h):
        for index, (of_tile, of_half) in ((0, (OPP, 0)), (1, (OPP, 1)), (2, (UP, 1)), (4, (DOWN, 0))):

            @pl.when((tile == of_tile) & (h == of_half))
            def _():
                copies[index].start()

    def first_gram(kind, tile):
        direct_row = lax.broadcasted_iota(jnp.int32, (8, DEPTH), 0) % 2 == 0
        row = lax.broadcasted_iota(jnp.int32, (16, DEPTH), 0)
        col = lax.broadcasted_iota(jnp.int32, (16, DEPTH), 1)
        mine = jnp.where(col % 4 == (row // 2) % 4, 1.0, 0.0).astype(jnp.bfloat16)
        first = dest(tile) * TILE

        def expand_step(group, carry):
            parts = []
            for i in range(0, TILE, 2):
                two = []
                for line in (sides[group, pl.ds(first + i, 1), :], sides[group, pl.ds(first + i + 1, 1), :]):
                    two.append(jnp.where(direct_row, line[:, :DEPTH], line[:, DEPTH:]))
                parts.append(jnp.concatenate(two, axis=0).astype(jnp.bfloat16) * mine)
            left = jnp.concatenate(parts, axis=0)
            expanded[group, left_rows(tile)] = left
            cross(kind, group, left)
            return carry

        lax.fori_loop(0, GROUPS, expand_step, 0, unroll=32)

    def later_gram(kind, tile):
        def gram_step(group, carry):
            cross(kind, group, expanded[group, left_rows(tile)])
            return carry

        lax.fori_loop(0, GROUPS, gram_step, 0, unroll=32)

    def self_lags(tile):
        copies = self_copies()

        def half(h, carry):
            def lag_step(i, carry):
                for k, lags in enumerate(pair_lags(self_lag_ref[...], h * (HALF // 2) + i)):
                    self_part[tile, h, 2 * i + k] = lags[:MIRROR].astype(jnp.bfloat16)
                    zero_lag[pl.ds(2 * i + k, 1), :] = lags[MIRROR : MIRROR + 1]
                return carry

            lax.fori_loop(0, HALF // 2, lag_step, 0, unroll=8)
            self_part[tile, h, HALF] = zero_lag[...].astype(jnp.bfloat16)
            start_ready(copies, tile, h)
            return carry

        lax.fori_loop(0, 2, half, 0)

    def kind_lags(kind, tile):
        copies = sum_copies(kind)

        def half(h, carry):
            def lag_step(i, carry):
                pair = h * (HALF // 2) + i
                for k, lags in enumerate(pair_lags(lag_ref[...], pair)):
                    part[kind - 1, tile, 2 * pair + k] = lags.astype(jnp.bfloat16)
                return carry

            lax.fori_loop(0, HALF // 2, lag_step, 0, unroll=8)
            start_ready(copies, tile, h)
            return carry

        lax.fori_loop(0, 2, half, 0)

    def add(count, total, rows, held, held_rows):
        def step(i, carry):
            here = rows(i)
            total[here] = (total[here].astype(jnp.float32) + held[held_rows(i)].astype(jnp.float32)).astype(jnp.bfloat16)
            return carry

        lax.fori_loop(0, count, step, 0, unroll=4 if count % 4 == 0 else 1)

    def relay(kind):
        copies = sum_copies(kind)
        k = kind - 1
        copies[0].wait_recv()
        add(HALF, part, lambda i: (k, UP, i), relay_up, lambda i: (k, i))
        copies[3].start()
        copies[1].wait_recv()
        add(HALF, part, lambda i: (k, DOWN, HALF + i), relay_down, lambda i: (k, i))
        copies[5].start()

    def self_relay():
        copies = self_copies()
        copies[0].wait_recv()
        add(HALF + 1, self_part, lambda i: (UP, 0, i), self_relay_up, lambda i: i)
        copies[3].start()
        copies[1].wait_recv()
        add(HALF + 1, self_part, lambda i: (DOWN, 1, i), self_relay_down, lambda i: i)
        copies[5].start()

    def three(own, below, above):
        return own.astype(jnp.float32) + (below.astype(jnp.float32) + above.astype(jnp.float32))

    def finish(kind):
        copies = sum_copies(kind)
        for index in (2, 3, 4, 5):
            copies[index].wait_recv()
        k = kind - 1

        def step(i, carry):
            out_ref[kind, i] = three(part[k, OWN, i], from_down[k, i], from_up[k, i]).astype(jnp.bfloat16)
            return carry

        lax.fori_loop(0, TILE, step, 0, unroll=4)

        @pl.when(kind == 2)
        def _():
            forward().start()

    def self_finish():
        copies = self_copies()
        for index in (2, 3, 4, 5):
            copies[index].wait_recv()
        column = lax.broadcasted_iota(jnp.int32, (MIRROR, BLK), 1)
        row = lax.broadcasted_iota(jnp.int32, (MIRROR, BLK), 0)

        def half(h, carry):
            zero_lag[...] = three(self_part[OWN, h, HALF], self_from_down[h, HALF], self_from_up[h, HALF])

            def step(i, carry):
                total = three(self_part[OWN, h, i], self_from_down[h, i], self_from_up[h, i])
                mine = h * HALF + i
                total = jnp.where(column == z * TILE + mine, 0.0, total)
                folded[pl.ds(pl.multiple_of(mine * MIRROR, MIRROR), MIRROR), :] = total
                zero = jnp.where(column == z * TILE + mine, 0.0, zero_lag[pl.ds(i, 1), :])
                later = jnp.where(row == 0, zero, pltpu.roll(total, 1, 0))
                out_ref[0, mine, MIRROR:] = later.astype(jnp.bfloat16)
                return carry

            lax.fori_loop(0, HALF, step, 0, unroll=2)
            return carry

        lax.fori_loop(0, 2, half, 0)
        eye_row = lax.broadcasted_iota(jnp.int32, (BLK, BLK), 0)
        eye_col = lax.broadcasted_iota(jnp.int32, (BLK, BLK), 1)
        eye = jnp.where(eye_row == eye_col, 1.0, 0.0).astype(jnp.bfloat16)
        for quad in range(MIRROR // 4):
            lines = [folded[pl.ds(4 * quad + k, TILE, stride=MIRROR), :] for k in range(4)]
            turned_over = nt_dot(eye, jnp.concatenate(lines, axis=0).astype(jnp.bfloat16))
            mirror_out[:, quad] = turned_over.reshape(n_tm, TILE, BLK).astype(jnp.bfloat16)
        for copy in mirror_copies():
            copy.start()
        mirror_in[OWN] = mirror_out[z]

    def self_unfold():
        for copy in mirror_copies():
            copy.wait_recv()
        place = lax.broadcasted_iota(jnp.int32, (TILE, BLK), 1) // TILE
        sources = [opposite, down, up, z]
        for quad in range(MIRROR // 4):
            held = [mirror_in[slot, quad].astype(jnp.float32) for slot in range(n_tm)]
            for k in range(4):
                line = jnp.zeros((TILE, BLK), jnp.float32)
                for slot, source in enumerate(sources):
                    moved = pltpu.roll(held[slot], lax.rem(source + 4 - k, 4) * TILE, 1)
                    line = jnp.where(place == source, moved, line)
                unfolded[pl.ds(MIRROR - 1 - 4 * quad - k, TILE, stride=MIRROR), :] = line

        def step(i, carry):
            lines = unfolded[pl.ds(pl.multiple_of(i * MIRROR, MIRROR), MIRROR), :]
            out_ref[0, i, :MIRROR] = lines.astype(jnp.bfloat16)
            return carry

        lax.fori_loop(0, TILE, step, 0, unroll=4)

    def match(p, slots):
        apart = blocks_ref[1, p] - blocks_ref[0, p]
        kind = jnp.where(blocks_ref[0, p] == c, apart, 3)
        owned = owner_ref[p] - c * SLOTS
        return tuple(held + jnp.where(owned == q, kind + 1, 0) for q, held in enumerate(slots))

    for q, held in enumerate(lax.fori_loop(0, owner_ref.shape[0], match, (0,) * SLOTS)):
        kinds_ref[q] = jnp.minimum(held, KINDS + 1)

    table_copy.wait()
    own_halo.wait()
    next_halo.start()
    whiten(own_ext, 0, True)

    @pl.when(odd == 1)
    def _():
        to_mate().start()

    transpose()

    def kind_of(step):
        return lax.rem(2 * step + 1 - odd, KINDS)

    def finish_any(kind):
        @pl.when(kind == 0)
        def _():
            self_finish()

        @pl.when(kind > 0)
        def _():
            finish(kind)

    zero_lag[...] = jnp.zeros_like(zero_lag)

    def kind_step(step, carry):
        kind = kind_of(step)

        @pl.when(step == 2 - odd)
        def _():
            next_main.wait()
            next_halo.wait()
            whiten(next_ext, 2, False)

            @pl.when(odd == 0)
            def _():
                to_mate().start()

        @pl.when(kind == 1)
        def _():
            to_mate().wait_recv()

        def tile_step(tile, carry):
            @pl.when(step == 0)
            def _():
                first_gram(kind, tile)

            @pl.when(step > 0)
            def _():
                later_gram(kind, tile)

            @pl.when(kind == 0)
            def _():
                self_lags(tile)

            @pl.when(kind > 0)
            def _():
                kind_lags(kind, tile)

            return carry

        lax.fori_loop(0, 4, tile_step, 0)

        @pl.when(kind == 0)
        def _():
            self_relay()

        @pl.when(kind > 0)
        def _():
            relay(kind)

        @pl.when(step > 0)
        def _():
            finish_any(kind_of(step - 1))

        return carry

    lax.fori_loop(0, KINDS, kind_step, 0)
    self_unfold()
    finish(kind_of(2))

    to_mate().wait_send()
    forward().wait_send()
    forward().wait_recv()
    for copy in self_copies() + sum_copies(1) + sum_copies(2) + mirror_copies():
        copy.wait_send()
    out_ref[3] = shared[...]


def place_kernel(kinds_ref, stacks_ref, out_ref, zeros, sem):
    zeros[...] = jnp.zeros_like(zeros)

    def put(q, src):
        return pltpu.make_async_copy(src, out_ref.at[:, q], sem.at[q])

    for q in range(SLOTS):
        held = kinds_ref[q]

        @pl.when(held > 0)
        def _():
            put(q, stacks_ref.at[held - 1]).start()

        @pl.when(held == 0)
        def _():
            put(q, zeros).start()

    for q in range(SLOTS):
        put(q, zeros).wait()


def shards(n_chan, n_tm, record, seg_starts, pair_blocks, pair_owner):
    block_len = record.shape[1]
    scale = 2.0 / math.sqrt(SEGS_DEV * n_tm * F)
    bf16 = jnp.bfloat16
    shifts = np.arange(NLAG) - NLAG // 2
    self_lags = lag_table(np.concatenate([np.arange(1, MIRROR + 1), np.zeros(16, np.int64)]))
    hbm = pl.BlockSpec(memory_space=pl.ANY)
    smem = pl.BlockSpec(memory_space=pltpu.SMEM)
    vmem = pl.BlockSpec(memory_space=pltpu.VMEM)
    stacks, kinds = pl.pallas_call(
        functools.partial(stacks_kernel, n_chan, n_tm, scale),
        out_shape=(
            pltpu.VMEM((4, TILE, NLAG, BLK), bf16),
            pltpu.SMEM((SLOTS,), jnp.int32),
        ),
        in_specs=[smem, smem, smem, hbm, hbm, vmem, vmem],
        out_specs=(vmem, smem),
        scratch_shapes=[
            pltpu.VMEM((2 * F, SEG_LEN), bf16),
            pltpu.VMEM(((block_len + SEG_LEN) // 128, BLK, 128), bf16),
            pltpu.VMEM(((block_len + SEG_LEN) // 128, BLK, 128), bf16),
            pltpu.VMEM((GROUPS, DEPTH, BLK), bf16),
            pltpu.VMEM((GROUPS, BLK, 2 * DEPTH), jnp.float32),
            pltpu.VMEM((KINDS, GROUPS, DEPTH, BLK), bf16),
            pltpu.VMEM((GROUPS, BLK * 8, DEPTH), bf16),
            pltpu.VMEM((TILE, 2 * F, BLK), bf16),
            pltpu.VMEM((KINDS - 1, 4, TILE, NLAG, BLK), bf16),
            pltpu.VMEM((KINDS - 1, HALF, NLAG, BLK), bf16),
            pltpu.VMEM((KINDS - 1, HALF, NLAG, BLK), bf16),
            pltpu.VMEM((KINDS - 1, TILE, NLAG, BLK), bf16),
            pltpu.VMEM((KINDS - 1, TILE, NLAG, BLK), bf16),
            pltpu.VMEM((4, 2, HALF + 1, MIRROR, BLK), bf16),
            pltpu.VMEM((HALF + 1, MIRROR, BLK), bf16),
            pltpu.VMEM((HALF + 1, MIRROR, BLK), bf16),
            pltpu.VMEM((2, HALF + 1, MIRROR, BLK), bf16),
            pltpu.VMEM((2, HALF + 1, MIRROR, BLK), bf16),
            pltpu.VMEM((MIRROR, BLK), jnp.float32),
            pltpu.VMEM((TILE * MIRROR, BLK), jnp.float32),
            pltpu.VMEM((TILE * MIRROR, BLK), jnp.float32),
            pltpu.VMEM((n_tm, MIRROR // 4, TILE, BLK), bf16),
            pltpu.VMEM((n_tm, MIRROR // 4, TILE, BLK), bf16),
            pltpu.VMEM((TILE, NLAG, BLK), bf16),
            pltpu.SemaphoreType.DMA((block_len // 128,)),
            pltpu.SemaphoreType.DMA,
            pltpu.SemaphoreType.DMA((5,)),
            pltpu.SemaphoreType.DMA((5,)),
            pltpu.SemaphoreType.DMA((KINDS, 6)),
            pltpu.SemaphoreType.DMA((KINDS, 6)),
            pltpu.SemaphoreType.DMA((3,)),
            pltpu.SemaphoreType.DMA((3,)),
        ],
        compiler_params=pltpu.CompilerParams(
            collective_id=0, has_side_effects=True, vmem_limit_bytes=60 * 1024 * 1024
        ),
        name="stacks",
    )(seg_starts, pair_blocks.T, pair_owner, record, transform_table(), lag_table(shifts), self_lags)
    return pl.pallas_call(
        place_kernel,
        out_shape=jax.ShapeDtypeStruct((TILE, SLOTS, NLAG, BLK), bf16),
        in_specs=[smem, vmem],
        out_specs=hbm,
        scratch_shapes=[pltpu.VMEM((TILE, NLAG, BLK), bf16), pltpu.SemaphoreType.DMA((SLOTS,))],
        compiler_params=pltpu.CompilerParams(vmem_limit_bytes=4 * 1024 * 1024),
        name="place",
    )(kinds, pltpu.with_memory_space_constraint(stacks, pltpu.VMEM))


def solution(mesh):
    in_specs = (P("chan", "tm"), P("tm"), P(), P())
    out_specs = P("tm", "chan", None, None)
    body = functools.partial(shards, mesh.shape["chan"], mesh.shape["tm"])
    return jax.shard_map(body, mesh=mesh, in_specs=in_specs, out_specs=out_specs, check_vma=False)
```

```python
import functools
import math

import jax
import jax.numpy as jnp
import numpy as np
from jax import lax
from jax.experimental import pallas as pl
from jax.experimental.pallas import tpu as pltpu
from jax.sharding import PartitionSpec as P

MESH = pl.DeviceIdType.MESH

SEG_LEN = 512
F = 256
LOW_BIN = 1
NLAG = 64
SLOTS = 4
LEVEL = 0.5
EPS = 1e-06

BLK = 128
SEGS_DEV = 16
GROUPS = F // 8
DEPTH = SEGS_DEV * 2 * 8
TILE = 32
HALF = TILE // 2
KINDS = 3
OPP, UP, DOWN, OWN = range(4)
MIRROR = NLAG // 2


def transform_table():
    sample = np.arange(SEG_LEN)
    bins = np.arange(F) + LOW_BIN
    phase = (bins[:, None] * sample[None, :] % SEG_LEN) * (2.0 * math.pi / SEG_LEN)
    taper = 0.5 - 0.5 * np.cos(sample * (2.0 * math.pi / SEG_LEN))
    table = np.concatenate([taper[None, :] * np.cos(phase), -taper[None, :] * np.sin(phase)], axis=0)
    return jnp.asarray(table.astype(np.float32)).astype(jnp.bfloat16)


def lag_table(shifts):
    bins = np.arange(F) + LOW_BIN
    phase = (bins[:, None] * shifts[None, :] % SEG_LEN) * (2.0 * math.pi / SEG_LEN)
    table = np.stack([np.cos(phase), -np.sin(phase)], axis=1).reshape(2 * F, len(shifts))
    return jnp.asarray(np.ascontiguousarray(table.T).astype(np.float32)).astype(jnp.bfloat16)


def nt_dot(a, b):
    return lax.dot_general(a, b, (((1,), (1,)), ((), ())), preferred_element_type=jnp.float32)


def stacks_kernel(
    n_chan,
    n_tm,
    scale,
    starts_ref,
    blocks_ref,
    owner_ref,
    record_ref,
    table_hbm,
    lag_ref,
    self_lag_ref,
    out_ref,
    kinds_ref,
    table_ref,
    own_ext,
    next_ext,
    turned,
    sides,
    spectra,
    expanded,
    gram,
    part,
    relay_up,
    relay_down,
    from_down,
    from_up,
    self_part,
    self_relay_up,
    self_relay_down,
    self_from_down,
    self_from_up,
    zero_lag,
    folded,
    unfolded,
    mirror_out,
    mirror_in,
    shared,
    local_sem,
    table_sem,
    near_send,
    near_recv,
    sum_send,
    sum_recv,
    mirror_send,
    mirror_recv,
):
    c = lax.axis_index("chan")
    z = lax.axis_index("tm")
    block_len = record_ref.shape[1]
    up = lax.rem(z + 1, n_tm)
    down = lax.rem(z + n_tm - 1, n_tm)
    opposite = lax.rem(z + 2, n_tm)
    c_next = lax.rem(c + 1, n_chan)
    c_prev = lax.rem(c + n_chan - 1, n_chan)
    c_next2 = lax.rem(c + 2, n_chan)
    c_prev2 = lax.rem(c + n_chan - 2, n_chan)
    odd = lax.rem(c, 2)
    mate = c + 1 - 2 * odd

    tiles = block_len // 128

    def load_copy(tile):
        columns = pl.ds(pl.multiple_of(tile * 128, 128), 128)
        return pltpu.make_async_copy(record_ref.at[:, columns], own_ext.at[tile], local_sem.at[tile])

    def start_load(tile, carry):
        load_copy(tile).start()
        return carry

    def wait_load(tile, carry):
        load_copy(tile).wait()
        return carry

    lax.fori_loop(0, tiles, start_load, 0)
    table_copy = pltpu.make_async_copy(table_hbm, table_ref, table_sem)
    table_copy.start()

    barrier = pltpu.get_barrier_semaphore()
    for who in ((c, up), (c, down), (c, opposite), (c_next2, z), (mate, z), (c_prev, z)):
        pl.semaphore_signal(barrier, inc=1, device_id=who, device_id_type=MESH)
    pl.semaphore_wait(barrier, 6)

    def near(index, src, dst, who):
        return pltpu.make_async_remote_copy(
            src_ref=src,
            dst_ref=dst,
            send_sem=near_send.at[index],
            recv_sem=near_recv.at[index],
            device_id=who,
            device_id_type=MESH,
        )

    main, halo = pl.ds(0, tiles), pl.ds(tiles, SEG_LEN // 128)
    head = own_ext.at[pl.ds(0, SEG_LEN // 128)]
    own_halo = near(0, head, own_ext.at[halo], (c, down))
    next_halo = near(1, own_ext.at[halo], next_ext.at[halo], (c_prev2, z))
    next_main = near(2, own_ext.at[main], next_ext.at[main], (c_prev2, z))
    lax.fori_loop(0, tiles, wait_load, 0)
    own_halo.start()
    next_main.start()

    def to_mate():
        return near(3, spectra.at[2 - 2 * odd], spectra.at[1], (mate, z))

    def forward():
        return near(4, out_ref.at[2], shared, (c_next, z))

    def ring_copies(kind, piece, up_slot, down_slot, below, above):
        routes = (
            (piece(OPP, 0), up_slot, up),
            (piece(OPP, 1), down_slot, down),
            (piece(UP, 1), below(1), up),
            (piece(UP, 0), below(0), up),
            (piece(DOWN, 0), above(0), down),
            (piece(DOWN, 1), above(1), down),
        )
        return [
            pltpu.make_async_remote_copy(
                src_ref=src,
                dst_ref=dst,
                send_sem=sum_send.at[kind, index],
                recv_sem=sum_recv.at[kind, index],
                device_id=(c, who),
                device_id_type=MESH,
            )
            for index, (src, dst, who) in enumerate(routes)
        ]

    def sum_copies(kind):
        def rows(half):
            return pl.ds(half * HALF, HALF)

        k = kind - 1
        return ring_copies(
            kind,
            lambda tile, half: part.at[k, tile, rows(half)],
            relay_up.at[k],
            relay_down.at[k],
            lambda half: from_down.at[k, rows(half)],
            lambda half: from_up.at[k, rows(half)],
        )

    def self_copies():
        return ring_copies(
            0,
            lambda tile, half: self_part.at[tile, half],
            self_relay_up,
            self_relay_down,
            lambda half: self_from_down.at[half],
            lambda half: self_from_up.at[half],
        )

    def mirror_copies():
        return [
            pltpu.make_async_remote_copy(
                src_ref=mirror_out.at[who],
                dst_ref=mirror_in.at[index],
                send_sem=mirror_send.at[index],
                recv_sem=mirror_recv.at[index],
                device_id=(c, who),
                device_id_type=MESH,
            )
            for index, who in enumerate((opposite, up, down))
        ]

    lane = lax.broadcasted_iota(jnp.int32, (BLK, 128), 1)

    def cut(ext, seg):
        start = lax.rem(starts_ref[seg], block_len)
        first = lax.shift_right_logical(start, 7)
        rest = start - first * 128
        turn = jnp.bitwise_and(128 - rest, 127)
        cols = [
            pltpu.roll(ext[first + j].astype(jnp.float32), turn, 1) for j in range(SEG_LEN // 128 + 1)
        ]
        inside = lane < 128 - rest
        return jnp.concatenate(
            [jnp.where(inside, cols[j], cols[j + 1]) for j in range(SEG_LEN // 128)], axis=1
        ).astype(jnp.bfloat16)

    def whiten(ext, kind, turn_too):
        def step(pair, carry):
            pieces = jnp.concatenate([cut(ext, 2 * pair), cut(ext, 2 * pair + 1)], axis=0)
            both = nt_dot(table_ref[...], pieces)
            for h in range(2):
                real = both[:F, BLK * h : BLK * (h + 1)]
                imag = both[F:, BLK * h : BLK * (h + 1)]
                amplitude = jnp.sqrt(real * real + imag * imag)
                level = jnp.mean(amplitude, axis=0, keepdims=True) + EPS
                inverse = 1.0 / (amplitude + LEVEL * level)
                real = (real * inverse).reshape(GROUPS, 8, BLK)
                imag = (imag * inverse).reshape(GROUPS, 8, BLK)
                rows = pl.ds(pl.multiple_of((2 * pair + h) * 16, 16), 16)
                spectra[kind, :, rows, :] = jnp.concatenate([real, imag], axis=1).astype(jnp.bfloat16)
                if turn_too:
                    turned[:, rows, :] = jnp.concatenate([imag, -real], axis=1).astype(jnp.bfloat16)
            return carry

        lax.fori_loop(0, SEGS_DEV // 2, step, 0, unroll=8)

    def dest(tile):
        ahead = jnp.where(tile == OPP, 2, jnp.where(tile == UP, 1, jnp.where(tile == DOWN, n_tm - 1, 0)))
        return lax.rem(z + ahead, n_tm)

    def transpose():
        eye_row = lax.broadcasted_iota(jnp.int32, (BLK, BLK), 0)
        eye_col = lax.broadcasted_iota(jnp.int32, (BLK, BLK), 1)
        eye = jnp.where(eye_row == eye_col, 1.0, 0.0).astype(jnp.bfloat16)

        def step(group, carry):
            sides[group] = nt_dot(eye, jnp.concatenate([spectra[0, group], turned[group]], axis=0))
            return carry

        lax.fori_loop(0, GROUPS, step, 0, unroll=16)

    def cross(kind, group, left):
        row = lax.broadcasted_iota(jnp.int32, (DEPTH, BLK), 0)
        low_bins = jnp.where(row % 8 < 4, 1.0, 0.0).astype(jnp.bfloat16)
        high_bins = jnp.where(row % 8 < 4, 0.0, 1.0).astype(jnp.bfloat16)
        right = spectra[kind, group]
        weights = jnp.concatenate([right * low_bins, right * high_bins], axis=1)
        both = jnp.dot(left, weights, preferred_element_type=jnp.float32)
        both = jnp.concatenate(
            [both[:, :BLK].reshape(TILE, 8, BLK), both[:, BLK:].reshape(TILE, 8, BLK)], axis=1
        )
        rows = pl.ds(pl.multiple_of(group * 16, 16), 16)
        gram[:, rows, :] = both.astype(jnp.bfloat16)

    def left_rows(tile):
        return pl.ds(pl.multiple_of(dest(tile) * TILE * 8, TILE * 8), TILE * 8)

    def pair_lags(table, pair):
        two = jnp.concatenate([gram[2 * pair], gram[2 * pair + 1]], axis=1)
        lags = jnp.dot(table, two, preferred_element_type=jnp.float32) * scale
        return lags[:, :BLK], lags[:, BLK:]

    def start_ready(copies, tile, h):
        for index, (of_tile, of_half) in ((0, (OPP, 0)), (1, (OPP, 1)), (2, (UP, 1)), (4, (DOWN, 0))):

            @pl.when((tile == of_tile) & (h == of_half))
            def _():
                copies[index].start()

    def first_gram(kind, tile):
        direct_row = lax.broadcasted_iota(jnp.int32, (8, DEPTH), 0) % 2 == 0
        row = lax.broadcasted_iota(jnp.int32, (16, DEPTH), 0)
        col = lax.broadcasted_iota(jnp.int32, (16, DEPTH), 1)
        mine = jnp.where(col % 4 == (row // 2) % 4, 1.0, 0.0).astype(jnp.bfloat16)
        first = dest(tile) * TILE

        def expand_step(group, carry):
            parts = []
            for i in range(0, TILE, 2):
                two = []
                for line in (sides[group, pl.ds(first + i, 1), :], sides[group, pl.ds(first + i + 1, 1), :]):
                    two.append(jnp.where(direct_row, line[:, :DEPTH], line[:, DEPTH:]))
                parts.append(jnp.concatenate(two, axis=0).astype(jnp.bfloat16) * mine)
            left = jnp.concatenate(parts, axis=0)
            expanded[group, left_rows(tile)] = left
            cross(kind, group, left)
            return carry

        lax.fori_loop(0, GROUPS, expand_step, 0, unroll=32)

    def later_gram(kind, tile):
        def gram_step(group, carry):
            cross(kind, group, expanded[group, left_rows(tile)])
            return carry

        lax.fori_loop(0, GROUPS, gram_step, 0, unroll=32)

    def self_lags(tile):
        copies = self_copies()

        def half(h, carry):
            def lag_step(i, carry):
                for k, lags in enumerate(pair_lags(self_lag_ref[...], h * (HALF // 2) + i)):
                    self_part[tile, h, 2 * i + k] = lags[:MIRROR].astype(jnp.bfloat16)
                    zero_lag[pl.ds(2 * i + k, 1), :] = lags[MIRROR : MIRROR + 1]
                return carry

            lax.fori_loop(0, HALF // 2, lag_step, 0, unroll=8)
            self_part[tile, h, HALF] = zero_lag[...].astype(jnp.bfloat16)
            start_ready(copies, tile, h)
            return carry

        lax.fori_loop(0, 2, half, 0)

    def kind_lags(kind, tile):
        copies = sum_copies(kind)

        def half(h, carry):
            def lag_step(i, carry):
                pair = h * (HALF // 2) + i
                for k, lags in enumerate(pair_lags(lag_ref[...], pair)):
                    part[kind - 1, tile, 2 * pair + k] = lags.astype(jnp.bfloat16)
                return carry

            lax.fori_loop(0, HALF // 2, lag_step, 0, unroll=8)
            start_ready(copies, tile, h)
            return carry

        lax.fori_loop(0, 2, half, 0)

    def add(count, total, rows, held, held_rows):
        def step(i, carry):
            here = rows(i)
            total[here] = (total[here].astype(jnp.float32) + held[held_rows(i)].astype(jnp.float32)).astype(jnp.bfloat16)
            return carry

        lax.fori_loop(0, count, step, 0, unroll=4 if count % 4 == 0 else 1)

    def relay(kind):
        copies = sum_copies(kind)
        k = kind - 1
        copies[0].wait_recv()
        add(HALF, part, lambda i: (k, UP, i), relay_up, lambda i: (k, i))
        copies[3].start()
        copies[1].wait_recv()
        add(HALF, part, lambda i: (k, DOWN, HALF + i), relay_down, lambda i: (k, i))
        copies[5].start()

    def self_relay():
        copies = self_copies()
        copies[0].wait_recv()
        add(HALF + 1, self_part, lambda i: (UP, 0, i), self_relay_up, lambda i: i)
        copies[3].start()
        copies[1].wait_recv()
        add(HALF + 1, self_part, lambda i: (DOWN, 1, i), self_relay_down, lambda i: i)
        copies[5].start()

    def three(own, below, above):
        return own.astype(jnp.float32) + (below.astype(jnp.float32) + above.astype(jnp.float32))

    def finish(kind):
        copies = sum_copies(kind)
        for index in (2, 3, 4, 5):
            copies[index].wait_recv()
        k = kind - 1

        def step(i, carry):
            out_ref[kind, i] = three(part[k, OWN, i], from_down[k, i], from_up[k, i]).astype(jnp.bfloat16)
            return carry

        lax.fori_loop(0, TILE, step, 0, unroll=4)

        @pl.when((kind == 2) & (c < n_chan - 1))
        def _():
            forward().start()

    def self_finish():
        copies = self_copies()
        for index in (2, 3, 4, 5):
            copies[index].wait_recv()
        column = lax.broadcasted_iota(jnp.int32, (MIRROR, BLK), 1)
        row = lax.broadcasted_iota(jnp.int32, (MIRROR, BLK), 0)

        def half(h, carry):
            zero_lag[...] = three(self_part[OWN, h, HALF], self_from_down[h, HALF], self_from_up[h, HALF])

            def step(i, carry):
                total = three(self_part[OWN, h, i], self_from_down[h, i], self_from_up[h, i])
                mine = h * HALF + i
                total = jnp.where(column == z * TILE + mine, 0.0, total)
                folded[pl.ds(pl.multiple_of(mine * MIRROR, MIRROR), MIRROR), :] = total
                zero = jnp.where(column == z * TILE + mine, 0.0, zero_lag[pl.ds(i, 1), :])
                later = jnp.where(row == 0, zero, pltpu.roll(total, 1, 0))
                out_ref[0, mine, MIRROR:] = later.astype(jnp.bfloat16)
                return carry

            lax.fori_loop(0, HALF, step, 0, unroll=2)
            return carry

        lax.fori_loop(0, 2, half, 0)
        eye_row = lax.broadcasted_iota(jnp.int32, (BLK, BLK), 0)
        eye_col = lax.broadcasted_iota(jnp.int32, (BLK, BLK), 1)
        eye = jnp.where(eye_row == eye_col, 1.0, 0.0).astype(jnp.bfloat16)
        for quad in range(MIRROR // 4):
            lines = [folded[pl.ds(4 * quad + k, TILE, stride=MIRROR), :] for k in range(4)]
            turned_over = nt_dot(eye, jnp.concatenate(lines, axis=0).astype(jnp.bfloat16))
            mirror_out[:, quad] = turned_over.reshape(n_tm, TILE, BLK).astype(jnp.bfloat16)
        for copy in mirror_copies():
            copy.start()
        mirror_in[OWN] = mirror_out[z]

    def self_unfold():
        for copy in mirror_copies():
            copy.wait_recv()
        place = lax.broadcasted_iota(jnp.int32, (TILE, BLK), 1) // TILE
        sources = [opposite, down, up, z]
        for quad in range(MIRROR // 4):
            held = [mirror_in[slot, quad].astype(jnp.float32) for slot in range(n_tm)]
            for k in range(4):
                line = jnp.zeros((TILE, BLK), jnp.float32)
                for slot, source in enumerate(sources):
                    moved = pltpu.roll(held[slot], lax.rem(source + 4 - k, 4) * TILE, 1)
                    line = jnp.where(place == source, moved, line)
                unfolded[pl.ds(MIRROR - 1 - 4 * quad - k, TILE, stride=MIRROR), :] = line

        def step(i, carry):
            lines = unfolded[pl.ds(pl.multiple_of(i * MIRROR, MIRROR), MIRROR), :]
            out_ref[0, i, :MIRROR] = lines.astype(jnp.bfloat16)
            return carry

        lax.fori_loop(0, TILE, step, 0, unroll=4)

    def match(p, slots):
        apart = blocks_ref[1, p] - blocks_ref[0, p]
        kind = jnp.where(blocks_ref[0, p] == c, apart, 3)
        owned = owner_ref[p] - c * SLOTS
        return tuple(held + jnp.where(owned == q, kind + 1, 0) for q, held in enumerate(slots))

    for q, held in enumerate(lax.fori_loop(0, owner_ref.shape[0], match, (0,) * SLOTS)):
        kinds_ref[q] = jnp.minimum(held, KINDS + 1)

    table_copy.wait()
    own_halo.wait()
    next_halo.start()
    whiten(own_ext, 0, True)

    @pl.when(odd == 1)
    def _():
        to_mate().start()

    transpose()

    def kind_of(step):
        return lax.rem(2 * step + 1 - odd, KINDS)

    def finish_any(kind):
        @pl.when(kind == 0)
        def _():
            self_finish()

        @pl.when(kind > 0)
        def _():
            finish(kind)

    zero_lag[...] = jnp.zeros_like(zero_lag)

    def kind_step(step, carry):
        kind = kind_of(step)

        @pl.when(step == 2 - odd)
        def _():
            next_main.wait()
            next_halo.wait()
            whiten(next_ext, 2, False)

            @pl.when(odd == 0)
            def _():
                to_mate().start()

        @pl.when(kind == 1)
        def _():
            to_mate().wait_recv()

        def tile_step(tile, carry):
            @pl.when(step == 0)
            def _():
                first_gram(kind, tile)

            @pl.when(step > 0)
            def _():
                later_gram(kind, tile)

            @pl.when(kind == 0)
            def _():
                self_lags(tile)

            @pl.when(kind > 0)
            def _():
                kind_lags(kind, tile)

            return carry

        lax.fori_loop(0, 4, tile_step, 0)

        @pl.when(kind == 0)
        def _():
            self_relay()

        @pl.when(kind > 0)
        def _():
            relay(kind)

        @pl.when(step > 0)
        def _():
            finish_any(kind_of(step - 1))

        return carry

    lax.fori_loop(0, KINDS, kind_step, 0)
    self_unfold()
    finish(kind_of(2))

    to_mate().wait_send()

    @pl.when(c < n_chan - 1)
    def _():
        forward().wait_send()

    for copy in self_copies() + sum_copies(1) + sum_copies(2) + mirror_copies():
        copy.wait_send()

    @pl.when(c == 0)
    def _():
        out_ref[3] = jnp.zeros((TILE, NLAG, BLK), jnp.bfloat16)

    @pl.when(c > 0)
    def _():
        forward().wait_recv()
        out_ref[3] = shared[...]


def place_kernel(kinds_ref, stacks_ref, out_ref, zeros, sem):
    zeros[...] = jnp.zeros_like(zeros)

    def put(q, src):
        return pltpu.make_async_copy(src, out_ref.at[:, q], sem.at[q])

    for q in range(SLOTS):
        held = kinds_ref[q]

        @pl.when(held > 0)
        def _():
            put(q, stacks_ref.at[held - 1]).start()

        @pl.when(held == 0)
        def _():
            put(q, zeros).start()

    for q in range(SLOTS):
        put(q, zeros).wait()


def shards(n_chan, n_tm, record, seg_starts, pair_blocks, pair_owner):
    block_len = record.shape[1]
    scale = 2.0 / math.sqrt(SEGS_DEV * n_tm * F)
    bf16 = jnp.bfloat16
    shifts = np.arange(NLAG) - NLAG // 2
    self_lags = lag_table(np.concatenate([np.arange(1, MIRROR + 1), np.zeros(16, np.int64)]))
    hbm = pl.BlockSpec(memory_space=pl.ANY)
    smem = pl.BlockSpec(memory_space=pltpu.SMEM)
    vmem = pl.BlockSpec(memory_space=pltpu.VMEM)
    stacks, kinds = pl.pallas_call(
        functools.partial(stacks_kernel, n_chan, n_tm, scale),
        out_shape=(
            pltpu.VMEM((4, TILE, NLAG, BLK), bf16),
            pltpu.SMEM((SLOTS,), jnp.int32),
        ),
        in_specs=[smem, smem, smem, hbm, hbm, vmem, vmem],
        out_specs=(vmem, smem),
        scratch_shapes=[
            pltpu.VMEM((2 * F, SEG_LEN), bf16),
            pltpu.VMEM(((block_len + SEG_LEN) // 128, BLK, 128), bf16),
            pltpu.VMEM(((block_len + SEG_LEN) // 128, BLK, 128), bf16),
            pltpu.VMEM((GROUPS, DEPTH, BLK), bf16),
            pltpu.VMEM((GROUPS, BLK, 2 * DEPTH), jnp.float32),
            pltpu.VMEM((KINDS, GROUPS, DEPTH, BLK), bf16),
            pltpu.VMEM((GROUPS, BLK * 8, DEPTH), bf16),
            pltpu.VMEM((TILE, 2 * F, BLK), bf16),
            pltpu.VMEM((KINDS - 1, 4, TILE, NLAG, BLK), bf16),
            pltpu.VMEM((KINDS - 1, HALF, NLAG, BLK), bf16),
            pltpu.VMEM((KINDS - 1, HALF, NLAG, BLK), bf16),
            pltpu.VMEM((KINDS - 1, TILE, NLAG, BLK), bf16),
            pltpu.VMEM((KINDS - 1, TILE, NLAG, BLK), bf16),
            pltpu.VMEM((4, 2, HALF + 1, MIRROR, BLK), bf16),
            pltpu.VMEM((HALF + 1, MIRROR, BLK), bf16),
            pltpu.VMEM((HALF + 1, MIRROR, BLK), bf16),
            pltpu.VMEM((2, HALF + 1, MIRROR, BLK), bf16),
            pltpu.VMEM((2, HALF + 1, MIRROR, BLK), bf16),
            pltpu.VMEM((MIRROR, BLK), jnp.float32),
            pltpu.VMEM((TILE * MIRROR, BLK), jnp.float32),
            pltpu.VMEM((TILE * MIRROR, BLK), jnp.float32),
            pltpu.VMEM((n_tm, MIRROR // 4, TILE, BLK), bf16),
            pltpu.VMEM((n_tm, MIRROR // 4, TILE, BLK), bf16),
            pltpu.VMEM((TILE, NLAG, BLK), bf16),
            pltpu.SemaphoreType.DMA((block_len // 128,)),
            pltpu.SemaphoreType.DMA,
            pltpu.SemaphoreType.DMA((5,)),
            pltpu.SemaphoreType.DMA((5,)),
            pltpu.SemaphoreType.DMA((KINDS, 6)),
            pltpu.SemaphoreType.DMA((KINDS, 6)),
            pltpu.SemaphoreType.DMA((3,)),
            pltpu.SemaphoreType.DMA((3,)),
        ],
        compiler_params=pltpu.CompilerParams(
            collective_id=0, has_side_effects=True, vmem_limit_bytes=60 * 1024 * 1024
        ),
        name="stacks",
    )(seg_starts, pair_blocks.T, pair_owner, record, transform_table(), lag_table(shifts), self_lags)
    return pl.pallas_call(
        place_kernel,
        out_shape=jax.ShapeDtypeStruct((TILE, SLOTS, NLAG, BLK), bf16),
        in_specs=[smem, vmem],
        out_specs=hbm,
        scratch_shapes=[pltpu.VMEM((TILE, NLAG, BLK), bf16), pltpu.SemaphoreType.DMA((SLOTS,))],
        compiler_params=pltpu.CompilerParams(vmem_limit_bytes=4 * 1024 * 1024),
        name="place",
    )(kinds, pltpu.with_memory_space_constraint(stacks, pltpu.VMEM))


def solution(mesh):
    in_specs = (P("chan", "tm"), P("tm"), P(), P())
    out_specs = P("tm", "chan", None, None)
    body = functools.partial(shards, mesh.shape["chan"], mesh.shape["tm"])
    return jax.shard_map(body, mesh=mesh, in_specs=in_specs, out_specs=out_specs, check_vma=False)
```
